256 devices in a mesh: dp: 16 (over x, y_hi, core), tensor: 16 (over z, y_lo).
Axes of the slice: x: 4, y: 4 (y_hi: 2, y_lo: 2; y = y_hi * 2 + y_lo), z: 8, core: 2. Of those that a mesh axis runs over, the one named last changes fastest.
Arguments:
- tokens: bfloat16 [12288, 4096], P(('dp', 'tensor')), may hold values from -0.875 to 0.875
- queries: bfloat16 [12288, 8192], P('dp', 'tensor'), may hold values from -6 to 6
- saved_keys: bfloat16 [12288, 512], P('dp', 'tensor'), may hold values from -6 to 6
- saved_values: bfloat16 [12288, 512], P('dp', 'tensor'), may hold values from -6 to 6
- outputs: bfloat16 [12288, 8192], P('dp', 'tensor'), may hold values from -6 to 6
- out_grads: bfloat16 [12288, 8192], P('dp', 'tensor'), may hold values from -6 to 6
- log_norms: float32 [64, 12288], P('tensor', 'dp'), may hold values from 4 to 6
- w_query: bfloat16 [4096, 8192], P(None, 'tensor'), may hold values from -0.09375 to 0.09375
- w_key: bfloat16 [4096, 512], P(None, 'tensor'), may hold values from -0.09375 to 0.09375
- w_value: bfloat16 [4096, 512], P(None, 'tensor'), may hold values from -0.09375 to 0.09375
Outputs:
- token_grads: bfloat16 [12288, 4096], P(('dp', 'tensor'))
- query_wgrad: float32 [4096, 8192], P('dp', 'tensor')
- key_wgrad: float32 [4096, 512], P('dp', 'tensor')
- value_wgrad: float32 [4096, 512], P('dp', 'tensor')
The draws below stay inside these ranges and needn't reach their ends.
All inputs are finite; a program needn't handle non-finite values.
Results may differ from the reference program's by a relative error of at most 0.0059.
Values may be sent and summed in bfloat16 or wider, within the bound.
No kernel may reach another device: no remote copies, remote signals or barrier semaphores. Data moves between devices by JAX's collectives and lax.ppermute only.
A program may use at most 128 MiB of HBM per device.

```python
import jax
import jax.numpy as jnp
from jax import lax

D = 4096
HQ = 64
KVH = 4
DH = 128
SEQ = 768
TOKENS = 12288
N_DP = 16


def strengthened(drawn, key, source, target, blocks, factor):
    owner, partner = [(jnp.arange(drawn.shape[position]) // (drawn.shape[position] // blocks)).reshape([-1 if axis == position else 1 for axis in range(drawn.ndim)]) for position in (source, target)]
    chosen = jax.random.permutation(key, blocks)[partner]
    strong = (owner == chosen) | (owner == (partner + blocks // 2) % blocks)
    return jnp.where(strong, factor * drawn, drawn)


def level_of(stream_key, extent, pieces, low, high):
    gain, own = 1.0, jax.random.fold_in(stream_key, 6)
    for dim, shards_of in pieces:
        heights = jnp.exp(jax.random.uniform(jax.random.fold_in(own, dim), (shards_of,), jnp.float32, low / len(pieces), high / len(pieces)))
        gain = gain * jnp.repeat(heights, extent[dim] // shards_of).reshape([-1 if axis == dim else 1 for axis in range(len(extent))])
    return gain


def bell_draw(own_key, dims, width, bound, split=(), kind=jnp.bfloat16):
    values = jax.random.normal(own_key, dims, jnp.float32) * width
    if len(split) > 0:
        values = level_of(own_key, dims, split, -0.22, 0.18) * values
    return jnp.clip(values, min=-bound, max=bound).astype(kind)


def noise_with(own_key, dims, spread, bound, shards, heavy, dtype=jnp.bfloat16):
    drawn = spread * jax.random.normal(own_key, dims, jnp.float32)
    if shards:
        drawn = drawn * level_of(own_key, dims, shards, -0.22, 0.18)
    return jnp.clip(strengthened(drawn, jax.random.fold_in(own_key, 3), *heavy), -bound, bound).astype(dtype)


def setup_inputs(seed: int = 0) -> dict:
    seeds = jax.random.split(jax.random.key(seed), 11)
    tokens = noise_with(seeds[0], (TOKENS, D), (4 * TOKENS ** -0.5), 0.875, ((0, 256),), (0, 1, 256, 6.0))
    queries = bell_draw(seeds[1], (TOKENS, HQ * DH), 1.0, 6.0, ((0, 16), (1, 16)))
    saved_keys = bell_draw(seeds[2], (TOKENS, KVH * DH), 1.0, 6.0, ((0, 16), (1, 16)))
    saved_values = bell_draw(seeds[3], (TOKENS, KVH * DH), 1.0, 6.0, ((0, 16), (1, 16)))
    outputs = bell_draw(seeds[4], (TOKENS, HQ * DH), 1.0, 6.0, ((0, 16), (1, 16)))
    out_grads = bell_draw(seeds[5], (TOKENS, HQ * DH), 1.0, 6.0, ((0, 16), (1, 16)))
    log_norms = jnp.clip(4.0 + 2.0 * jax.random.uniform(seeds[6], (HQ, TOKENS), jnp.float32) ** level_of(seeds[6], (HQ, TOKENS), ((0, 16), (1, 16)), -0.2, 0.2), 4.0, 6.0)
    w_query = bell_draw(seeds[7], (D, HQ * DH), D ** -0.5, 0.09375, ((1, 16),))
    w_key = bell_draw(seeds[8], (D, KVH * DH), D ** -0.5, 0.09375, ((1, 16),))
    w_value = bell_draw(seeds[9], (D, KVH * DH), D ** -0.5, 0.09375, ((1, 16),))
    return {"tokens": tokens, "queries": queries, "saved_keys": saved_keys, "saved_values": saved_values, "outputs": outputs, "out_grads": out_grads, "log_norms": log_norms, "w_query": w_query, "w_key": w_key, "w_value": w_value}


def attend_group(query_block, key_block, value_block, output_block, grad_block, norm_block):
    scaling = DH ** -0.5
    length = query_block.shape[0]
    row_ids = jnp.arange(length)[:, None]
    col_ids = jnp.arange(length)[None, :]
    causal = col_ids <= row_ids
    query_f = query_block.astype(jnp.float32)
    key_f = key_block.astype(jnp.float32)
    value_f = value_block.astype(jnp.float32)
    grad_f = grad_block.astype(jnp.float32)
    scores = jnp.einsum("shd,td->hst", query_f, key_f) * scaling
    probs = jnp.where(causal[None], jnp.exp(scores - norm_block[:, :, None]), jnp.float32(0.0))
    probs_low = probs.astype(jnp.bfloat16)
    delta = jnp.sum(grad_f * output_block.astype(jnp.float32), axis=-1).T
    dprobs = jnp.einsum("shd,td->hst", grad_f, value_f)
    dscores = (probs * (dprobs - delta[:, :, None])).astype(jnp.bfloat16)
    dscores_f = dscores.astype(jnp.float32)
    grad_q = (jnp.einsum("hst,td->shd", dscores_f, key_f) * scaling).astype(jnp.bfloat16)
    grad_k = (jnp.einsum("hst,shd->td", dscores_f, query_f) * scaling).astype(jnp.bfloat16)
    grad_v = jnp.einsum("hst,shd->td", probs_low.astype(jnp.float32), grad_f).astype(jnp.bfloat16)
    return grad_q, grad_k, grad_v


def reference(tokens, queries, saved_keys, saved_values, outputs, out_grads, log_norms, w_query, w_key, w_value):
    group_size = HQ // KVH
    query_blocks = queries.reshape(N_DP, SEQ, KVH, group_size, DH).transpose(0, 2, 1, 3, 4)
    output_blocks = outputs.reshape(N_DP, SEQ, KVH, group_size, DH).transpose(0, 2, 1, 3, 4)
    grad_blocks = out_grads.reshape(N_DP, SEQ, KVH, group_size, DH).transpose(0, 2, 1, 3, 4)
    key_blocks = saved_keys.reshape(N_DP, SEQ, KVH, DH).transpose(0, 2, 1, 3)
    value_blocks = saved_values.reshape(N_DP, SEQ, KVH, DH).transpose(0, 2, 1, 3)
    norm_blocks = log_norms.reshape(KVH, group_size, N_DP, SEQ).transpose(2, 0, 1, 3)

    def per_group(bundle):
        return attend_group(*bundle)

    def per_replica(bundle):
        return lax.map(per_group, bundle)

    grad_q, grad_k, grad_v = lax.map(per_replica, (query_blocks, key_blocks, value_blocks, output_blocks, grad_blocks, norm_blocks))
    grad_q = grad_q.transpose(0, 2, 1, 3, 4).reshape(TOKENS, HQ * DH)
    grad_k = grad_k.transpose(0, 2, 1, 3).reshape(TOKENS, KVH * DH)
    grad_v = grad_v.transpose(0, 2, 1, 3).reshape(TOKENS, KVH * DH)
    grad_cols = jnp.concatenate([grad_q, grad_k, grad_v], axis=1)
    weight_cols = jnp.concatenate([w_query, w_key, w_value], axis=1)
    token_grads = lax.dot_general(grad_cols, weight_cols, (((1,), (1,)), ((), ())), preferred_element_type=jnp.float32).astype(jnp.bfloat16)
    weight_grads = lax.dot_general(tokens, grad_cols, (((0,), (0,)), ((), ())), preferred_element_type=jnp.float32)
    query_wgrad = weight_grads[:, : HQ * DH]
    key_wgrad = weight_grads[:, HQ * DH : HQ * DH + KVH * DH]
    value_wgrad = weight_grads[:, HQ * DH + KVH * DH :]
    return token_grads, query_wgrad, key_wgrad, value_wgrad
```

```python
import jax
import jax.numpy as jnp
from jax import lax
from jax.sharding import PartitionSpec as P

KVH = 4
DH = 128
NZ = 8
NX = 4


def shift(value, axis, step):
    size = lax.axis_size(axis)
    pairs = [(source, (source + step) % size) for source in range(size)]
    return lax.ppermute(value, axis, pairs)


def swap(value, axis, mask):
    pairs = [(source, source ^ mask) for source in range(lax.axis_size(axis))]
    return lax.ppermute(value, axis, pairs)


def after(value, *earlier):
    return lax.optimization_barrier((value, *earlier))[0]


def pick(value, index, axis=0):
    return lax.dynamic_index_in_dim(value, index, axis, keepdims=False)


def ordered(flag, first, second, axis):
    return jnp.where(
        flag,
        jnp.concatenate([second, first], axis=axis),
        jnp.concatenate([first, second], axis=axis),
    )


def gather_tokens(block, z):
    rows = block.shape[2]
    half = NX // 2

    def put(whole, piece, owner, start=0):
        return lax.dynamic_update_slice(whole, piece, (start, 0, (owner % NZ) * rows, 0))

    whole = jnp.zeros((NX, block.shape[1], rows * NZ, block.shape[3]), block.dtype)
    whole = put(whole, block, z)
    up = down = block
    for step in range(1, NZ // 2):
        up = shift(up, "tensor", 2)
        down = shift(down, "tensor", -2)
        whole = put(whole, up, z - step)
        whole = put(whole, down, z + step)
    up = shift(up[:half], "tensor", 2)
    down = shift(down[half:], "tensor", -2)
    whole = put(whole, up, z + NZ // 2)
    return put(whole, down, z + NZ // 2, half)


def body(
    tokens,
    queries,
    saved_keys,
    saved_values,
    outputs,
    out_grads,
    log_norms,
    w_query,
    w_key,
    w_value,
):
    t = lax.axis_index("tensor")
    d = lax.axis_index("dp")
    z, h = t // 2, t % 2
    zb = z % 2
    c = d % 2
    group = d // 2
    x, yh = group // 2, group % 2
    seq = queries.shape[0]
    heads = log_norms.shape[0]
    kv_w = saved_keys.shape[1]
    q_w = queries.shape[1]
    width = tokens.shape[1]
    scaling = DH ** (-0.5)
    bf = jnp.bfloat16
    f32 = jnp.float32

    kv = jnp.stack([saved_keys.T, saved_values.T])
    kv_y = swap(kv, "tensor", 1)
    kv2 = ordered(h == 1, kv, kv_y, 1)
    kv_z = swap(kv2, "tensor", 2)
    kv4 = ordered(zb == 1, kv2, kv_z, 1)
    key_t, value_t = kv4[0], kv4[1]

    n_own = tokens.shape[0]
    tk = tokens.reshape(n_own, NX, 2, 2, 2, DH).transpose(3, 4, 1, 0, 2, 5)
    tk = tk.reshape(2, 2, NX, n_own, 2 * DH)
    tk_mine = pick(tk, h, 1)
    tk_send = after(pick(tk, 1 - h, 1), kv_y)
    tk_y = swap(tk_send, "tensor", 1)
    tk2 = ordered(h == 1, tk_mine, tk_y, 2)
    tk_c = swap(pick(tk2, 1 - c), "dp", 1)
    block = jnp.stack([pick(tk2, c), tk_c], axis=1)

    quarter = width // 4
    piece = quarter // NZ

    def weight_rows(start, size):
        return [
            lax.dynamic_slice_in_dim(w, start, size, 0) for w in (w_query, w_key, w_value)
        ]

    far = jnp.concatenate(weight_rows(((1 - h) * 2 + c) * quarter + group * piece, piece), axis=1)
    far = swap(after(far, kv_y), "tensor", 1)
    far_y = swap(far, "dp", 2)
    far2 = ordered(yh == 1, far, far_y, 0)
    far_up = shift(far2, "dp", 4)
    far_down = shift(far2, "dp", -4)
    far_up2 = shift(far_up[:piece], "dp", 4)
    far_down2 = shift(far_down[piece:], "dp", -4)
    far4 = jnp.concatenate([far2, far_down, far_up2, far_down2, far_up], axis=0)
    far4 = jnp.concatenate([far4, far4], axis=0)
    far4 = lax.dynamic_slice_in_dim(far4, ((NX - x) % NX) * 2 * piece, quarter, 0)
    near_q, near_k, near_v = weight_rows((h * 2 + c) * quarter, quarter)
    weights = jnp.concatenate(
        [
            near_q,
            far4[:, :q_w],
            near_k,
            far4[:, q_w : q_w + kv_w],
            near_v,
            far4[:, q_w + kv_w :],
        ],
        axis=1,
    )

    row_ids = jnp.arange(seq)[:, None]
    col_ids = jnp.arange(seq)[None, :]
    causal = col_ids <= row_ids
    own_q, far_q = [], []
    key_grad = value_grad = 0.0
    for head in range(heads):
        cols = slice(head * DH, (head + 1) * DH)
        query, grad, output = queries[:, cols], out_grads[:, cols], outputs[:, cols]
        scores = jnp.dot(query, key_t, preferred_element_type=f32) * scaling
        probs = jnp.where(causal, jnp.exp(scores - log_norms[head][:, None]), f32(0.0))
        delta = jnp.sum(grad.astype(f32) * output.astype(f32), axis=-1)
        dprobs = jnp.dot(grad, value_t, preferred_element_type=f32)
        dscores = (probs * (dprobs - delta[:, None])).astype(bf)
        grad_q = jnp.einsum("st,dt->sd", dscores, key_t, preferred_element_type=f32)
        grad_q = (grad_q * scaling).astype(bf)
        own_q.append(grad_q)
        far_q.append(swap(grad_q, "tensor", 1))
        key_grad += jnp.einsum("st,sd->dt", dscores, query, preferred_element_type=f32)
        value_grad += jnp.einsum("st,sd->dt", probs.astype(bf), grad, preferred_element_type=f32)

    kv_grad = jnp.stack([key_grad * scaling, value_grad]).reshape(2, 2, 2 * kv_w, seq)
    kv_send = pick(kv_grad, 1 - zb, 1).astype(bf)
    kv_grad = pick(kv_grad, zb, 1) + swap(kv_send, "tensor", 2).astype(f32)
    kv_grad = (kv_grad + swap(kv_grad.astype(bf), "tensor", 1).astype(f32)).astype(bf)
    kv_grad = ordered(h == 1, kv_grad[:, :kv_w], kv_grad[:, kv_w:], 1)
    kv_grad = kv_grad.reshape(4 * kv_w, seq).T

    here = jnp.concatenate([*own_q, *far_q, kv_grad], axis=1)
    there = jnp.concatenate(
        [
            swap(jnp.concatenate(own_q, axis=1), "dp", 1),
            swap(jnp.concatenate(far_q, axis=1), "dp", 1),
            swap(kv_grad, "dp", 1),
        ],
        axis=1,
    )
    grads = jnp.stack([here, there])

    rows = seq // NZ

    def token_part(owner):
        left = lax.dynamic_slice_in_dim(grads, (owner % NZ) * rows, rows, 1)
        return lax.dot_general(
            left, weights, (((2,), (1,)), ((), ())), preferred_element_type=f32
        )

    far_part = token_part(z + NZ // 2).astype(bf)
    up, down = shift(far_part[:1], "tensor", 2), shift(far_part[1:], "tensor", -2)
    up = jnp.concatenate([up, jnp.zeros_like(up)])
    down = jnp.concatenate([jnp.zeros_like(down), down])
    for step in reversed(range(1, NZ // 2)):
        up = shift((token_part(z + step) + up.astype(f32)).astype(bf), "tensor", 2)
        down = shift((token_part(z - step) + down.astype(f32)).astype(bf), "tensor", -2)
    token_sum = token_part(z) + up.astype(f32) + down.astype(f32)
    token_sum = token_sum.astype(bf)
    other = swap(token_sum[1], "dp", 1)
    both = ordered(c == 1, token_sum[0], other, 1)
    both = both.reshape(2, n_own, 2 * quarter)
    other = swap(pick(both, 1 - h), "tensor", 1)
    token_grads = ordered(h == 1, pick(both, h), other, 1)

    all_tokens = gather_tokens(block, z)

    def weight_part(owner):
        left = pick(all_tokens, owner % NX)
        return lax.dot_general(
            left, grads, (((0, 1), (0, 1)), ((), ())), preferred_element_type=f32
        )

    far_part = weight_part(x + 2).astype(bf)
    up, down = shift(far_part[:DH], "dp", 4), shift(far_part[DH:], "dp", -4)
    up = jnp.concatenate([up, jnp.zeros_like(up)])
    down = jnp.concatenate([jnp.zeros_like(down), down])
    up = shift((weight_part(x + 1) + up.astype(f32)).astype(bf), "dp", 4)
    down = shift((weight_part(x - 1) + down.astype(f32)).astype(bf), "dp", -4)
    weight_sum = weight_part(x) + up.astype(f32) + down.astype(f32)
    weight_sum = weight_sum.reshape(2, DH, weight_sum.shape[1])
    weight_sum = pick(weight_sum, yh) + swap(
        pick(weight_sum, 1 - yh).astype(bf), "dp", 2
    ).astype(f32)
    k0 = 2 * q_w
    own = jnp.concatenate(
        [
            weight_sum[:, :q_w],
            weight_sum[:, k0 : k0 + kv_w],
            weight_sum[:, k0 + 2 * kv_w : k0 + 3 * kv_w],
        ],
        axis=1,
    )
    far = jnp.concatenate(
        [
            weight_sum[:, q_w:k0],
            weight_sum[:, k0 + kv_w : k0 + 2 * kv_w],
            weight_sum[:, k0 + 3 * kv_w :],
        ],
        axis=1,
    )
    far = swap(far.astype(bf), "tensor", 1).astype(f32)
    wgrad = ordered(h == 1, own, far, 0)
    return (
        token_grads,
        wgrad[:, :q_w],
        wgrad[:, q_w : q_w + kv_w],
        wgrad[:, q_w + kv_w :],
    )


def solution(mesh):
    in_specs = (
        P(("dp", "tensor"), None),
        P("dp", "tensor"),
        P("dp", "tensor"),
        P("dp", "tensor"),
        P("dp", "tensor"),
        P("dp", "tensor"),
        P("tensor", "dp"),
        P(None, "tensor"),
        P(None, "tensor"),
        P(None, "tensor"),
    )
    out_specs = (P(("dp", "tensor"), None), P("dp", "tensor"), P("dp", "tensor"), P("dp", "tensor"))
    return jax.shard_map(body, mesh=mesh, in_specs=in_specs, out_specs=out_specs, check_vma=False)
```

```python
import functools

import jax
import jax.numpy as jnp
from jax import lax
from jax.experimental import pallas as pl
from jax.experimental.pallas import tpu as pltpu
from jax.sharding import PartitionSpec as P

DH = 128
NZ = 8
NX = 4
TILE = 256
MIB = 2**20
BF = jnp.bfloat16
F32 = jnp.float32
ANY = pl.BlockSpec(memory_space=pl.ANY)
SMEM = pl.BlockSpec(memory_space=pltpu.SMEM)


def shift(value, axis, step):
    size = lax.axis_size(axis)
    pairs = [(source, (source + step) % size) for source in range(size)]
    return lax.ppermute(value, axis, pairs)


def swap(value, axis, mask):
    pairs = [(source, source ^ mask) for source in range(lax.axis_size(axis))]
    return lax.ppermute(value, axis, pairs)


def after(value, *earlier):
    return lax.optimization_barrier((value, *earlier))[0]


def pick(value, index, axis=0):
    return lax.dynamic_index_in_dim(value, index, axis, keepdims=False)


def ordered(flag, first, second, axis):
    return jnp.where(
        flag,
        jnp.concatenate([second, first], axis=axis),
        jnp.concatenate([first, second], axis=axis),
    )


def dot(left, right, left_dim, right_dim):
    return lax.dot_general(
        left, right, (((left_dim,), (right_dim,)), ((), ())), preferred_element_type=F32
    )


def attend_kernel(last, spot, kv0, kv1, kv2, kv3, query, grad, output, norms, sums, *rest):
    if last:
        out_q, send, keep, keys, values, total = rest
    else:
        out_q, keep, keys, values, total = rest
    head = pl.program_id(0)
    scaling = DH ** (-0.5)
    seq = query.shape[0]
    part = kv0.shape[0] // 2
    me = spot[0]

    @pl.when(head == 0)
    def _():
        for index, ref in enumerate((kv0, kv1, kv2, kv3)):
            place = pl.ds(pl.multiple_of(lax.bitwise_xor(me, index) * part, part), part)
            keys[place, :] = ref[:part, :]
            values[place, :] = ref[part:, :]
        if last:
            total[...] = sums[...]
        else:
            total[...] = jnp.zeros_like(total)

    which = lax.broadcasted_iota(jnp.int32, norms.shape, 1) == head + sums.shape[0] * int(last)
    norm = jnp.sum(jnp.where(which, norms[...], 0.0), axis=1, keepdims=True)
    for tile in range(seq // TILE):
        rows = slice(tile * TILE, (tile + 1) * TILE)
        width = (tile + 1) * TILE
        query_t, grad_t = query[rows, :], grad[rows, :]
        scores = dot(query_t, keys[:, :width], 1, 0)
        probs = jnp.exp(scores * scaling - norm[rows])
        row_ids = lax.broadcasted_iota(jnp.int32, probs.shape, 0) + tile * TILE
        col_ids = lax.broadcasted_iota(jnp.int32, probs.shape, 1)
        probs = jnp.where(col_ids <= row_ids, probs, 0.0)
        delta = jnp.sum(grad_t.astype(F32) * output[rows, :].astype(F32), axis=1, keepdims=True)
        dprobs = dot(grad_t, values[:, :width], 1, 0)
        dscores = (probs * (dprobs - delta)).astype(BF)
        out_q[rows, :] = (dot(dscores, keys[:, :width], 1, 1) * scaling).astype(BF)
        total[0, :, :width] += dot(query_t, dscores, 0, 0)
        total[1, :, :width] += dot(grad_t, probs.astype(BF), 0, 0)

    @pl.when(head == pl.num_programs(0) - 1)
    def _():
        if last:
            half = DH // 2
            mine = lax.shift_right_logical(me, 1)
            near = pl.ds(pl.multiple_of(mine * half, half), half)
            far = pl.ds(pl.multiple_of((1 - mine) * half, half), half)
            for index, factor in enumerate((scaling, 1.0)):
                keep[index] = total[index, near, :] * factor
                send[index] = (total[index, far, :] * factor).astype(BF)
        else:
            keep[...] = total[...]


def attend(spot, kvs, queries, out_grads, outputs, norms, sums):
    last = sums is not None
    seq = queries.shape[0]
    heads = norms.shape[1] // 2
    part = heads if last else 0
    if not last:
        sums = jnp.zeros((heads, 8, DH), F32)
    cols = pl.BlockSpec((seq, DH), lambda head: (0, head + part))
    full = lambda a: pl.BlockSpec(a.shape, lambda head: (0,) * a.ndim)
    big = jax.ShapeDtypeStruct((2, DH, seq), F32)
    outs = [jax.ShapeDtypeStruct((seq, heads * DH), BF)]
    if last:
        outs += [
            jax.ShapeDtypeStruct((2, DH // 2, seq), BF),
            jax.ShapeDtypeStruct((2, DH // 2, seq), F32),
        ]
    else:
        outs += [big]
    return pl.pallas_call(
        functools.partial(attend_kernel, last),
        grid=(heads,),
        in_specs=[SMEM, *[full(kv) for kv in kvs], cols, cols, cols, full(norms), full(sums)],
        out_specs=[
            pl.BlockSpec((seq, DH), lambda head: (0, head)),
            *[full(out) for out in outs[1:]],
        ],
        out_shape=outs,
        scratch_shapes=[
            pltpu.VMEM((DH, seq), BF),
            pltpu.VMEM((DH, seq), BF),
            pltpu.VMEM(big.shape, F32),
        ],
        compiler_params=pltpu.CompilerParams(vmem_limit_bytes=24 * MIB),
        cost_estimate=pl.CostEstimate(
            flops=heads * 10 * seq * seq * DH, bytes_accessed=4 * MIB, transcendentals=heads * seq * seq
        ),
        name="attend",
    )(spot, *kvs, queries, out_grads, outputs, norms, sums)


def offsets(pieces):
    starts, at = [], 0
    for piece in pieces:
        starts.append(at)
        at += piece.shape[1]
    return starts, at


def run_copies(copies):
    for copy in copies:
        copy.start()
    for copy in copies:
        copy.wait()


def token_kernel(first, n_pieces, spot, weights, *rest):
    pieces, (out, held, sems) = rest[: 2 * n_pieces], rest[2 * n_pieces :]
    starts, _ = offsets(pieces[:n_pieces])
    z = spot[0]
    rows = out.shape[-2]
    seq = pieces[0].shape[0]

    def start_row(owner):
        return pl.multiple_of(lax.rem(owner + NZ, NZ) * rows, rows)

    @pl.when(pl.program_id(0) == 0)
    def _():
        source = pl.ds(start_row(z + NZ // 2), rows) if first else pl.ds(0, seq)
        run_copies(
            [
                pltpu.make_async_copy(
                    piece.at[source, :],
                    held.at[
                        index // n_pieces,
                        :,
                        pl.ds(starts[index % n_pieces], piece.shape[1]),
                    ],
                    sems.at[index],
                )
                for index, piece in enumerate(pieces)
            ]
        )

    if first:
        block = held[...]
    else:
        step = pl.program_id(0)
        away = 3 - step // 2
        owner = z + jnp.where(step % 2 == 0, away, -away)
        block = held[:, pl.ds(start_row(owner), rows), :]
    block = block.reshape(2 * rows, block.shape[2])
    out[...] = dot(block, weights[...], 1, 1).astype(out.dtype).reshape(out.shape)


def token_parts(first, spot, weights, here, there):
    seq = here[0].shape[0]
    rows = seq // NZ
    _, depth = offsets(here)
    steps = 1 if first else NZ - 1
    dtype = BF if first else F32
    width = weights.shape[0]
    return pl.pallas_call(
        functools.partial(token_kernel, first, len(here)),
        grid=(steps,),
        in_specs=[
            SMEM,
            pl.BlockSpec(weights.shape, lambda step: (0, 0)),
            *[ANY] * (2 * len(here)),
        ],
        out_specs=pl.BlockSpec((1, 2, rows, width), lambda step: (step, 0, 0, 0)),
        out_shape=jax.ShapeDtypeStruct((steps, 2, rows, width), dtype),
        scratch_shapes=[
            pltpu.VMEM((2, rows if first else seq, depth), BF),
            pltpu.SemaphoreType.DMA((2 * len(here),)),
        ],
        compiler_params=pltpu.CompilerParams(vmem_limit_bytes=24 * MIB),
        cost_estimate=pl.CostEstimate(
            flops=4 * steps * rows * depth * width, bytes_accessed=8 * MIB, transcendentals=0
        ),
        name="token_parts",
    )(spot, weights, *here, *there)


def weight_kernel(first, n_pieces, spot, *rest):
    blocks, rest = rest[:NZ], rest[NZ:]
    pieces, (out, held, lefts, sems, left_sems) = rest[: 2 * n_pieces], rest[2 * n_pieces :]
    starts, _ = offsets(pieces[:n_pieces])
    z, x = spot[0], spot[1]
    rows = blocks[0].shape[2]
    places = (0, -1, 1, -2, 2, -3, 3, 4)
    aways = (2,) if first else (1, 3, 0)

    @pl.when(pl.program_id(0) == 0)
    def _():
        copies = [
            pltpu.make_async_copy(
                piece,
                held.at[
                    index // n_pieces, :, pl.ds(starts[index % n_pieces], piece.shape[1])
                ],
                sems.at[index],
            )
            for index, piece in enumerate(pieces)
        ]
        for slot, away in enumerate(aways):
            part = lax.rem(x + away, NX)
            for index, (block, place) in enumerate(zip(blocks, places)):
                start = pl.multiple_of(lax.rem(z + place + NZ, NZ) * rows, rows)
                copies.append(
                    pltpu.make_async_copy(
                        block.at[part],
                        lefts.at[slot, :, pl.ds(start, rows), :],
                        left_sems.at[slot, index],
                    )
                )
        run_copies(copies)

    left = lefts[pl.program_id(0)]
    left = left.reshape(left.shape[0] * left.shape[1], left.shape[2])
    right = held[...].reshape(left.shape[0], held.shape[2])
    out[0] = dot(left, right, 0, 0).astype(out.dtype)


def weight_parts(first, spot, blocks, here, there):
    seq = here[0].shape[0]
    _, depth = offsets(here)
    steps = 1 if first else NX - 1
    dtype = BF if first else F32
    wide = blocks[0].shape[3]
    return pl.pallas_call(
        functools.partial(weight_kernel, first, len(here)),
        grid=(steps,),
        in_specs=[SMEM, *[ANY] * (NZ + 2 * len(here))],
        out_specs=pl.BlockSpec((1, wide, depth), lambda step: (step, 0, 0)),
        out_shape=jax.ShapeDtypeStruct((steps, wide, depth), dtype),
        scratch_shapes=[
            pltpu.VMEM((2, seq, depth), BF),
            pltpu.VMEM((steps, 2, seq, wide), BF),
            pltpu.SemaphoreType.DMA((2 * len(here),)),
            pltpu.SemaphoreType.DMA((steps, NZ)),
        ],
        compiler_params=pltpu.CompilerParams(vmem_limit_bytes=24 * MIB),
        cost_estimate=pl.CostEstimate(
            flops=4 * steps * wide * depth * seq, bytes_accessed=8 * MIB, transcendentals=0
        ),
        name="weight_parts",
    )(spot, *blocks, *here, *there)


def gather_tokens(block):
    half = NX // 2
    blocks = [block]
    up = down = block
    for step in range(1, NZ // 2):
        up = shift(up, "tensor", 2)
        down = shift(down, "tensor", -2)
        blocks += [up, down]
    up = shift(up[:half], "tensor", 2)
    down = shift(down[half:], "tensor", -2)
    return blocks + [jnp.concatenate([up, down])]


def body(
    tokens,
    queries,
    saved_keys,
    saved_values,
    outputs,
    out_grads,
    log_norms,
    w_query,
    w_key,
    w_value,
):
    t = lax.axis_index("tensor")
    d = lax.axis_index("dp")
    z, h = t // 2, t % 2
    zb = z % 2
    c = d % 2
    group = d // 2
    x, yh = group // 2, group % 2
    seq = queries.shape[0]
    kv_w = saved_keys.shape[1]
    q_w = queries.shape[1]
    width = tokens.shape[1]

    kv = jnp.concatenate([saved_keys.T, saved_values.T])
    kvs = [kv] + [swap(kv, "tensor", mask) for mask in (1, 2, 3)]

    n_own = tokens.shape[0]
    tk = tokens.reshape(n_own, NX, 2, 2, 2, DH).transpose(3, 4, 1, 0, 2, 5)
    tk = tk.reshape(2, 2, NX, n_own, 2 * DH)
    tk_mine = pick(tk, h, 1)
    tk_y = swap(pick(tk, 1 - h, 1), "tensor", 1)
    tk2 = ordered(h == 1, tk_mine, tk_y, 2)
    tk_c = swap(pick(tk2, 1 - c), "dp", 1)
    block = jnp.stack([pick(tk2, c), tk_c], axis=1)
    blocks = gather_tokens(block)

    quarter = width // 4
    piece = quarter // NZ

    def weight_rows(start, size):
        return [
            lax.dynamic_slice_in_dim(w, start, size, 0) for w in (w_query, w_key, w_value)
        ]

    far = jnp.concatenate(weight_rows(((1 - h) * 2 + c) * quarter + group * piece, piece), axis=1)
    far = swap(far, "tensor", 1)
    far_y = swap(far, "dp", 2)
    far2 = ordered(yh == 1, far, far_y, 0)
    far_up = shift(far2, "dp", 4)
    far_down = shift(far2, "dp", -4)
    far_up2 = shift(far_up[:piece], "dp", 4)
    far_down2 = shift(far_down[piece:], "dp", -4)
    far4 = jnp.concatenate([far2, far_down, far_up2, far_down2, far_up], axis=0)
    far4 = jnp.concatenate([far4, far4], axis=0)
    far4 = lax.dynamic_slice_in_dim(far4, ((NX - x) % NX) * 2 * piece, quarter, 0)
    near_q, near_k, near_v = weight_rows((h * 2 + c) * quarter, quarter)
    weights = jnp.concatenate(
        [
            near_q,
            far4[:, :q_w],
            near_k,
            far4[:, q_w : q_w + kv_w],
            near_v,
            far4[:, q_w + kv_w :],
        ],
        axis=1,
    )

    spot = jnp.stack([2 * zb + h]).astype(jnp.int32)
    norms = log_norms.T
    own0, sums = attend(spot, kvs, queries, out_grads, outputs, norms, None)
    own1, kv_send, kv_keep = attend(spot, kvs, queries, out_grads, outputs, norms, sums)
    far0 = swap(own0, "tensor", 1)
    far1 = swap(own1, "tensor", 1)

    kv_keep = kv_keep + swap(kv_send, "tensor", 2).astype(F32)
    kv_grad = (kv_keep + swap(kv_keep.astype(BF), "tensor", 1).astype(F32)).astype(BF)
    kv_grad = ordered(h == 1, kv_grad[:, :kv_w], kv_grad[:, kv_w:], 1)
    kv_grad = kv_grad.reshape(4 * kv_w, seq).T

    here = [own0, own1, far0, far1, kv_grad]
    there = [swap(value, "dp", 1) for value in here]
    spot = jnp.stack([z, x]).astype(jnp.int32)

    part = token_parts(True, spot, weights, here, there)[0]
    up, down = shift(part[:1], "tensor", 2), shift(part[1:], "tensor", -2)
    weight_part = weight_parts(True, spot, blocks, here, there)[0]
    parts = token_parts(False, after(spot, weight_part), weights, here, there)
    up = jnp.concatenate([up, jnp.zeros_like(up)])
    down = jnp.concatenate([jnp.zeros_like(down), down])
    for step in range(0, NZ - 2, 2):
        up = shift((parts[step] + up.astype(F32)).astype(BF), "tensor", 2)
        down = shift((parts[step + 1] + down.astype(F32)).astype(BF), "tensor", -2)
    token_sum = (parts[NZ - 2] + up.astype(F32) + down.astype(F32)).astype(BF)
    other = swap(token_sum[1], "dp", 1)
    both = ordered(c == 1, token_sum[0], other, 1)
    both = both.reshape(2, n_own, 2 * quarter)
    other = swap(pick(both, 1 - h), "tensor", 1)
    token_grads = ordered(h == 1, pick(both, h), other, 1)

    up, down = shift(weight_part[:DH], "dp", 4), shift(weight_part[DH:], "dp", -4)
    up = jnp.concatenate([up, jnp.zeros_like(up)])
    down = jnp.concatenate([jnp.zeros_like(down), down])
    wparts = weight_parts(False, after(spot, parts), blocks, here, there)
    up = shift((wparts[0] + up.astype(F32)).astype(BF), "dp", 4)
    down = shift((wparts[1] + down.astype(F32)).astype(BF), "dp", -4)
    weight_sum = wparts[2] + up.astype(F32) + down.astype(F32)
    weight_sum = weight_sum.reshape(2, DH, weight_sum.shape[1])
    weight_sum = pick(weight_sum, yh) + swap(
        pick(weight_sum, 1 - yh).astype(BF), "dp", 2
    ).astype(F32)
    k0 = 2 * q_w
    own = jnp.concatenate(
        [
            weight_sum[:, :q_w],
            weight_sum[:, k0 : k0 + kv_w],
            weight_sum[:, k0 + 2 * kv_w : k0 + 3 * kv_w],
        ],
        axis=1,
    )
    far = jnp.concatenate(
        [
            weight_sum[:, q_w:k0],
            weight_sum[:, k0 + kv_w : k0 + 2 * kv_w],
            weight_sum[:, k0 + 3 * kv_w :],
        ],
        axis=1,
    )
    far = swap(far.astype(BF), "tensor", 1).astype(F32)
    wgrad = ordered(h == 1, own, far, 0)
    return (
        token_grads,
        wgrad[:, :q_w],
        wgrad[:, q_w : q_w + kv_w],
        wgrad[:, q_w + kv_w :],
    )


def solution(mesh):
    in_specs = (
        P(("dp", "tensor"), None),
        P("dp", "tensor"),
        P("dp", "tensor"),
        P("dp", "tensor"),
        P("dp", "tensor"),
        P("dp", "tensor"),
        P("tensor", "dp"),
        P(None, "tensor"),
        P(None, "tensor"),
        P(None, "tensor"),
    )
    out_specs = (P(("dp", "tensor"), None), P("dp", "tensor"), P("dp", "tensor"), P("dp", "tensor"))
    return jax.shard_map(body, mesh=mesh, in_specs=in_specs, out_specs=out_specs, check_vma=False)
```

```python
import functools

import jax
import jax.numpy as jnp
from jax import lax
from jax.experimental import pallas as pl
from jax.experimental.pallas import tpu as pltpu
from jax.sharding import PartitionSpec as P

DH = 128
NZ = 8
NX = 4
TILE = 256
MIB = 2**20
BF = jnp.bfloat16
F32 = jnp.float32
ANY = pl.BlockSpec(memory_space=pl.ANY)
SMEM = pl.BlockSpec(memory_space=pltpu.SMEM)
VMEM = pl.BlockSpec(memory_space=pltpu.VMEM)
Z, H, C, X, ZB = range(5)


def shift(value, axis, step):
    size = lax.axis_size(axis)
    pairs = [(source, (source + step) % size) for source in range(size)]
    return lax.ppermute(value, axis, pairs)


def swap(value, axis, mask):
    pairs = [(source, source ^ mask) for source in range(lax.axis_size(axis))]
    return lax.ppermute(value, axis, pairs)


def swap_quad(value, core, side):
    tensor = lax.axis_size("tensor")
    size = lax.axis_size("dp") * tensor
    mask = core * tensor + side
    pairs = [(source, source ^ mask) for source in range(size)]
    return lax.ppermute(value, ("dp", "tensor"), pairs)


def dot(left, right, left_dim, right_dim):
    return lax.dot_general(
        left, right, (((left_dim,), (right_dim,)), ((), ())), preferred_element_type=F32
    )


def run_copies(copies):
    for copy in copies:
        copy.start()
    for copy in copies:
        copy.wait()


def call(
    kernel, name, spot, ins, specs, outs, out_specs, scratch=(), grid=(), work=0, later=(), through=(), vmem=20
):
    n_ins, n_later, n_through = 1 + len(ins), len(later), len(through)
    n_outs = len(outs)

    def whole(*refs):
        ins_end = n_ins + n_later + n_through
        kernel(*refs[:n_ins], *refs[ins_end : ins_end + n_outs], *refs[ins_end + n_outs + n_through :])

    return pl.pallas_call(
        whole,
        grid=grid,
        in_specs=[SMEM, *specs, *[ANY] * (n_later + n_through)],
        out_specs=[*out_specs, *[ANY] * n_through],
        out_shape=[*outs, *[shape(value.shape, value.dtype) for value in through]],
        input_output_aliases={
            n_ins + n_later + index: n_outs + index for index in range(n_through)
        },
        scratch_shapes=scratch,
        compiler_params=pltpu.CompilerParams(vmem_limit_bytes=vmem * MIB),
        cost_estimate=pl.CostEstimate(flops=work, bytes_accessed=0, transcendentals=0),
        name=name,
    )(spot, *ins, *later, *through)


def tie_kernel(*refs):
    pass


def tie(spot, values, later):
    return call(tie_kernel, "tie", spot, (), [], [], [], later=later, through=values)


def shape(dims, dtype=BF):
    return jax.ShapeDtypeStruct(tuple(dims), dtype)


def pack_kernel(spot, tokens, keys, values, own, side, core, both, kv):
    h, c = spot[H], spot[C]
    width = tokens.shape[1]
    kv_w = keys.shape[0]
    for index in range(kv.shape[0]):
        kv[index, :kv_w, :] = keys[...]
        kv[index, kv_w:, :] = values[...]
    for to, to_c, to_h in ((own, c, h), (side, c, 1 - h), (core, 1 - c, h), (both, 1 - c, 1 - h)):
        for part in range(NX):
            for half in range(2):
                start = part * (width // NX) + half * 4 * DH + to_c * 2 * DH + to_h * DH
                start = pl.multiple_of(start, DH)
                to[part, :, half * DH : (half + 1) * DH] = tokens[:, pl.ds(start, DH)]


def pack(spot, tokens, keys, values):
    part = shape((NX, tokens.shape[0], 2 * DH))
    kv = shape((4, 2 * keys.shape[0], keys.shape[1]))
    return call(
        pack_kernel,
        "pack",
        spot,
        (tokens, keys, values),
        [VMEM] * 3,
        [part] * 4 + [kv],
        [VMEM] * 5,
    )


def prepare_kernel(
    spot, query_in, grad_in, output, norms, w_query, w_key, w_value, query, grad, stats, w_send, sem
):
    h, c, x = spot[H], spot[C], spot[X]
    kv_w = w_key.shape[0]
    piece = w_send.shape[0] - kv_w
    row = pl.multiple_of(((1 - h) * 2 + c) * (w_query.shape[0] // 4) + x * piece, piece)
    copy = pltpu.make_async_copy(
        w_query.at[pl.ds(row, piece), :], w_send.at[pl.ds(0, piece), :], sem
    )
    copy.start()
    w_send[piece:, :piece] = w_key[:, pl.ds(row, piece)]
    w_send[piece:, piece:] = w_value[:, pl.ds(row, piece)]
    query[...] = query_in[...]
    grad[...] = grad_in[...]
    heads, seq = norms.shape
    stats[...] = jnp.concatenate([norms[...], jnp.zeros((DH - heads, seq), F32)]).T
    lane = lax.broadcasted_iota(jnp.int32, stats.shape, 1)
    for head in range(heads):
        cols = slice(head * DH, (head + 1) * DH)
        delta = grad_in[:, cols].astype(F32) * output[:, cols].astype(F32)
        delta = jnp.sum(delta, axis=1, keepdims=True)
        stats[...] = jnp.where(lane == heads + head, delta, stats[...])
    copy.wait()


def prepare(spot, queries, out_grads, outputs, norms, w_query, w_key, w_value, later):
    w_send = shape((w_query.shape[0] // 16 + w_key.shape[0], w_query.shape[1]))
    return call(
        prepare_kernel,
        "prepare",
        spot,
        (queries, out_grads, outputs, norms, w_query, w_key, w_value),
        [VMEM] * 4 + [ANY] + [VMEM] * 2,
        [shape(queries.shape)] * 2 + [shape((queries.shape[0], DH), F32), w_send],
        [VMEM] * 4,
        [pltpu.SemaphoreType.DMA],
        later=later,
    )


def block_kernel(spot, own, side, core, both, out):
    h = spot[H]
    rows = own.shape[1]
    near = pl.ds(pl.multiple_of(h * rows, rows), rows)
    far = pl.ds(pl.multiple_of((1 - h) * rows, rows), rows)
    out[:, 0, near, :] = own[...]
    out[:, 0, far, :] = side[...]
    out[:, 1, near, :] = core[...]
    out[:, 1, far, :] = both[...]


def token_block(spot, parts, later):
    part, rows, wide = parts[0].shape
    return call(
        block_kernel,
        "token_block",
        spot,
        parts,
        [VMEM] * 4,
        [shape((part, 2, 2 * rows, wide))],
        [VMEM],
        later=later,
    )[0]


def repeat_kernel(spot, value, out):
    for index in range(out.shape[0]):
        out[index] = value[...]


def repeat(spot, value, times, later):
    return call(
        repeat_kernel,
        "repeat",
        spot,
        (value,),
        [VMEM],
        [shape((times, *value.shape))],
        [VMEM],
        later=later,
    )[0]


def weights_kernel(spot, w_query, w_key, w_value, far_own, far_core, out, out_kv, sems):
    h, c = spot[H], spot[C]
    half, q2 = out.shape
    q_w, kv_w = q2 // 2, w_key.shape[0]
    piece = far_own.shape[1] - kv_w
    start = pl.multiple_of(h * half, half)
    near = [pl.ds(pl.multiple_of(kind * 2 * kv_w + h * kv_w, kv_w), kv_w) for kind in (0, 1)]
    far = [pl.ds(pl.multiple_of(kind * 2 * kv_w + (1 - h) * kv_w, kv_w), kv_w) for kind in (0, 1)]
    pairs = [
        (w_query.at[pl.ds(start, half), :], out.at[:, pl.ds(0, q_w)]),
        (w_key.at[:, pl.ds(start, half)], out_kv.at[near[0], :]),
        (w_value.at[:, pl.ds(start, half)], out_kv.at[near[1], :]),
    ]
    for ref, place in ((far_own, c), (far_core, 1 - c)):
        for index in range(NX):
            row = pl.multiple_of(place * (half // 2) + index * piece, piece)
            pairs.append(
                (ref.at[index, pl.ds(0, piece), :], out.at[pl.ds(row, piece), pl.ds(q_w, q_w)])
            )
            for kind in (0, 1):
                pairs.append(
                    (
                        ref.at[index, pl.ds(piece, kv_w), pl.ds(kind * piece, piece)],
                        out_kv.at[far[kind], pl.ds(row, piece)],
                    )
                )
    run_copies(
        [
            pltpu.make_async_copy(source, target, sems.at[index])
            for index, (source, target) in enumerate(pairs)
        ]
    )


def gather_weights(spot, w_query, w_key, w_value, far_own, far_core, later):
    width, q_w = w_query.shape
    return call(
        weights_kernel,
        "gather_weights",
        spot,
        (w_query, w_key, w_value, far_own, far_core),
        [ANY] * 5,
        [shape((width // 2, 2 * q_w)), shape((4 * w_key.shape[0], width // 2))],
        [ANY] * 2,
        [pltpu.SemaphoreType.DMA((3 + 6 * NX,))],
        later=later,
    )


def attend_kernel(spot, kv, query, grad, stats, out_a, out_b, send, keep, keys, values, total):
    head = pl.program_id(0)
    heads = pl.num_programs(0)
    scaling = DH ** (-0.5)
    seq = query.shape[0]
    part = kv.shape[1] // 2

    @pl.when(head == 0)
    def _():
        for index in range(kv.shape[0]):
            keys[index * part : (index + 1) * part, :] = kv[index, :part, :]
            values[index * part : (index + 1) * part, :] = kv[index, part:, :]
        total[...] = jnp.zeros_like(total)

    lane = lax.broadcasted_iota(jnp.int32, stats.shape, 1)
    norm = jnp.sum(jnp.where(lane == head, stats[...], 0.0), axis=1, keepdims=True)
    delta = jnp.sum(jnp.where(lane == heads + head, stats[...], 0.0), axis=1, keepdims=True)
    for tile in range(seq // TILE):
        rows = slice(tile * TILE, (tile + 1) * TILE)
        width = (tile + 1) * TILE
        query_t, grad_t = query[rows, :], grad[rows, :]
        scores = dot(query_t, keys[:, :width], 1, 0)
        probs = jnp.exp(scores * scaling - norm[rows])
        row_ids = lax.broadcasted_iota(jnp.int32, probs.shape, 0) + tile * TILE
        col_ids = lax.broadcasted_iota(jnp.int32, probs.shape, 1)
        probs = jnp.where(col_ids <= row_ids, probs, 0.0)
        dprobs = dot(grad_t, values[:, :width], 1, 0)
        dscores = (probs * (dprobs - delta[rows])).astype(BF)
        grad_q = (dot(dscores, keys[:, :width], 1, 1) * scaling).astype(BF)

        @pl.when(head < heads - 1)
        def _():
            out_a[rows, :] = grad_q

        @pl.when(head == heads - 1)
        def _():
            out_b[rows, :] = grad_q

        total[0, :, :width] += dot(query_t, dscores, 0, 0)
        total[1, :, :width] += dot(grad_t, probs.astype(BF), 0, 0)

    @pl.when(head == heads - 1)
    def _():
        half = DH // 2
        mine = spot[ZB]
        near = pl.ds(pl.multiple_of(mine * half, half), half)
        far = pl.ds(pl.multiple_of((1 - mine) * half, half), half)
        for index, factor in enumerate((scaling, 1.0)):
            keep[index] = total[index, near, :] * factor
            send[index] = (total[index, far, :] * factor).astype(BF)


def attend(spot, kv, queries, out_grads, stats, later):
    seq = queries.shape[0]
    heads = queries.shape[1] // DH
    cols = pl.BlockSpec((seq, DH), lambda head: (0, head))
    full = lambda a: pl.BlockSpec(a.shape, lambda head: (0,) * len(a.shape))
    outs = [
        shape((seq, (heads - 1) * DH)),
        shape((seq, DH)),
        shape((2, DH // 2, seq)),
        shape((2, DH // 2, seq), F32),
    ]
    return call(
        attend_kernel,
        "attend",
        spot,
        (kv, queries, out_grads, stats),
        [full(kv), cols, cols, full(stats)],
        outs,
        [
            pl.BlockSpec((seq, DH), lambda head: (0, jnp.minimum(head, heads - 2))),
            *[full(out) for out in outs[1:]],
        ],
        [
            pltpu.VMEM((DH, seq), BF),
            pltpu.VMEM((DH, seq), BF),
            pltpu.VMEM((2, DH, seq), F32),
        ],
        grid=(heads,),
        work=10**9,
        later=later,
    )


def middle_kernel(spot, keep, arrived, out, send):
    total = keep[...] + arrived[...].astype(F32)
    out[...] = total
    send[...] = total.astype(BF)


def middle(spot, keep, arrived, later, through):
    return call(
        middle_kernel,
        "kv_middle",
        spot,
        (keep, arrived),
        [VMEM] * 2,
        [shape(keep.shape, F32), shape(keep.shape)],
        [VMEM] * 2,
        later=later,
        through=through,
    )


def final_kv_kernel(spot, keep, arrived, out):
    total = keep[...] + arrived[...].astype(F32)
    out[...] = total.reshape(out.shape[1], out.shape[0]).T.astype(BF)


def final_kv(spot, keep, arrived, later, through):
    return call(
        final_kv_kernel,
        "kv_final",
        spot,
        (keep, arrived),
        [VMEM] * 2,
        [shape((keep.shape[2], keep.shape[0] * keep.shape[1]))],
        [VMEM],
        later=later,
        through=through,
    )


def offsets(pieces):
    starts, at = [], 0
    for piece in pieces:
        starts.append(at)
        at += piece.shape[1]
    return starts, at


def load_rows(aways, z, pieces, held, sems):
    starts, _ = offsets(pieces)
    rows = pieces[0].shape[0] // NZ
    copies = []
    for slot, away in enumerate(aways):
        row = pl.multiple_of(lax.rem(z + away + NZ, NZ) * rows, rows)
        for index, piece in enumerate(pieces):
            copies.append(
                pltpu.make_async_copy(
                    piece.at[pl.ds(row, rows), :],
                    held.at[pl.ds(slot * rows, rows), pl.ds(starts[index], piece.shape[1])],
                    sems.at[slot, index],
                )
            )
    return copies


def first_kernel(spot, weights, weights_kv, *rest):
    pieces, (last_up, last_down, up, down, held, sems, last_sems) = rest[:5], rest[5:]
    copies = load_rows((NZ // 2,), spot[Z], pieces, held, sems)
    wide = up.shape[1] // 2
    half, pair, _, cols = last_up.shape
    for index, (last, out, first) in enumerate(((last_up, up, 0), (last_down, down, half // 2))):
        for part in range(half // 2):
            for rep in range(pair):
                slot = part * pair + rep
                copies.append(
                    pltpu.make_async_copy(
                        last.at[first + part, rep],
                        out.at[:, pl.ds(wide + slot * cols, cols)],
                        last_sems.at[index, slot],
                    )
                )
    for copy in copies:
        copy.start()
    for copy in copies[: len(pieces)]:
        copy.wait()
    deep = weights.shape[1]
    left, left_kv = held[:, :deep], held[:, deep:]
    for index, out in enumerate((up, down)):
        part = slice(index * wide, (index + 1) * wide)
        out[:, :wide] = (
            dot(left, weights[part, :], 1, 1) + dot(left_kv, weights_kv[:, part], 1, 0)
        ).astype(BF)
    for copy in copies[len(pieces) :]:
        copy.wait()


def first_parts(spot, weights, weights_kv, pieces, last_up, last_down):
    rows = pieces[0].shape[0] // NZ
    width, deep = weights.shape
    depth = deep + weights_kv.shape[0]
    return call(
        first_kernel,
        "first_parts",
        spot,
        (weights, weights_kv, *pieces, last_up, last_down),
        [VMEM] * 2 + [ANY] * 7,
        [shape((rows, width))] * 2,
        [VMEM] * 2,
        [
            pltpu.VMEM((rows, depth), BF),
            pltpu.SemaphoreType.DMA((1, 5)),
            pltpu.SemaphoreType.DMA((2, 4)),
        ],
    )


def token_kernel(aways, spot, weights, weights_kv, *rest):
    pieces, (out, held, sems) = rest[:5], rest[5:]

    @pl.when(pl.program_id(0) == 0)
    def _():
        run_copies(load_rows(aways, spot[Z], pieces, held, sems))

    deep = weights.shape[1]
    total = dot(held[:, :deep], weights[...], 1, 1) + dot(held[:, deep:], weights_kv[...], 1, 0)
    out[...] = total.reshape(out.shape)


def token_parts(aways, spot, weights, weights_kv, pieces, later):
    rows = pieces[0].shape[0] // NZ
    width, deep = weights.shape
    depth = deep + weights_kv.shape[0]
    wide = 512
    return call(
        functools.partial(token_kernel, aways),
        "token_parts",
        spot,
        (weights, weights_kv, *pieces),
        [
            pl.BlockSpec((wide, deep), lambda step: (step, 0)),
            pl.BlockSpec((depth - deep, wide), lambda step: (0, step)),
            *[ANY] * 5,
        ],
        [shape((len(aways), rows, width), F32)],
        [pl.BlockSpec((len(aways), rows, wide), lambda step: (0, 0, step))],
        [
            pltpu.VMEM((len(aways) * rows, depth), BF),
            pltpu.SemaphoreType.DMA((len(aways), 5)),
        ],
        grid=(width // wide,),
        work=10**9,
        later=later,
    )[0]


def ring_kernel(kind, spot, up, down, ups, downs, *outs):
    wide = up.shape[1] // 2
    if kind == "first":
        for arrived, part, out, start in ((up, ups, outs[0], 0), (down, downs, outs[1], wide)):
            out[...] = part[0].astype(BF)
            cols = slice(start, start + wide)
            out[:, cols] = (part[0, :, cols] + arrived[:, :wide].astype(F32)).astype(BF)
    elif kind == "next":
        for arrived, part, out in ((up, ups, outs[0]), (down, downs, outs[1])):
            out[...] = (part[0] + arrived[...].astype(F32)).astype(BF)
    else:
        own, send = outs
        h = spot[H]
        rows = own.shape[0]
        for out, side in ((own, h), (send, 1 - h)):
            here = pl.ds(pl.multiple_of(side * rows, rows), rows)
            total = ups[0, here, :] + up[here, :].astype(F32) + down[here, :].astype(F32)
            out[...] = total.astype(BF)


def ring_step(kind, spot, up, down, parts, slots, later):
    _, rows, width = parts.shape
    whole = lambda a: pl.BlockSpec(a.shape, lambda step: (0,) * len(a.shape))
    term = [pl.BlockSpec((1, rows, width), lambda step, slot=slot: (slot, 0, 0)) for slot in slots]
    out = shape((rows // 2 if kind == "last" else rows, width))
    return call(
        functools.partial(ring_kernel, kind),
        "ring_step",
        spot,
        (up, down, parts, parts),
        [whole(up), whole(down), *term],
        [out] * 2,
        [whole(out)] * 2,
        grid=(1,),
        later=later,
    )


def wgrad_kernel(spot, *rest):
    blocks, (up, down), rest = rest[: NZ - 1], rest[NZ - 1 : NZ + 1], rest[NZ + 1 :]
    pieces, (out, held, lefts, sems, left_sems, last_sems) = rest[:10], rest[10:]
    starts, _ = offsets(pieces[:5])
    z = spot[Z]
    rows = blocks[0].shape[2]
    cols = blocks[0].shape[3]
    places = (0, -1, 1, -2, 2, -3, 3)

    @pl.when(pl.program_id(0) == 0)
    def _():
        def place(away):
            return pl.ds(pl.multiple_of(lax.rem(z + away + NZ, NZ) * rows, rows), rows)

        copies = [
            pltpu.make_async_copy(
                piece,
                held.at[index // 5, :, pl.ds(starts[index % 5], piece.shape[1])],
                sems.at[index],
            )
            for index, piece in enumerate(pieces)
        ]
        for index, (block, away) in enumerate(zip(blocks, places)):
            copies.append(
                pltpu.make_async_copy(
                    block, lefts.at[:, :, place(away), :], left_sems.at[index]
                )
            )
        for index, last in enumerate((up, down)):
            for slot in range(NX):
                copies.append(
                    pltpu.make_async_copy(
                        last.at[:, pl.ds(last.shape[1] // 2 + slot * cols, cols)],
                        lefts.at[index * (NX // 2) + slot // 2, slot % 2, place(NZ // 2), :],
                        last_sems.at[index, slot],
                    )
                )
        run_copies(copies)

    left = lefts[pl.program_id(0)]
    left = left.reshape(left.shape[0] * left.shape[1], left.shape[2])
    right = held[...].reshape(left.shape[0], held.shape[2])
    out[0] = dot(left, right, 0, 0).astype(out.dtype)


def wgrad_parts(spot, blocks, up, down, here, there, later):
    seq = here[0].shape[0]
    _, depth = offsets(here)
    wide = blocks[0].shape[3]
    return call(
        wgrad_kernel,
        "wgrad_parts",
        spot,
        (*blocks, up, down, *here, *there),
        [ANY] * (NZ + 11),
        [shape((NX, wide, depth))],
        [pl.BlockSpec((1, wide, depth), lambda step: (step, 0, 0))],
        [
            pltpu.VMEM((2, seq, depth), BF),
            pltpu.VMEM((NX, 2, seq, wide), BF),
            pltpu.SemaphoreType.DMA((10,)),
            pltpu.SemaphoreType.DMA((NZ - 1,)),
            pltpu.SemaphoreType.DMA((2, NX)),
        ],
        grid=(NX,),
        work=10**10,
        later=later,
    )[0]


def wgrad_sum_kernel(spot, terms, own, own_kv, send):
    total = terms[0].astype(F32)
    for index in range(1, terms.shape[0]):
        total += terms[index].astype(F32)
    q_w = own.shape[1]
    own[...] = total[:, :q_w]
    own_kv[...] = total[:, 2 * q_w :]
    send[...] = total[:, q_w:].astype(BF)


def wgrad_sum(spot, terms, q_w):
    _, rows, depth = terms.shape
    return call(
        wgrad_sum_kernel,
        "wgrad_sum",
        spot,
        (terms,),
        [VMEM],
        [shape((rows, q_w), F32), shape((rows, depth - 2 * q_w), F32), shape((rows, depth - q_w))],
        [VMEM] * 3,
    )


def wgrad_final_kernel(spot, own, own_kv, arrived, out, out_k, out_v, turned):
    h = spot[H]
    rows, q_w = own.shape
    kv_w = out_k.shape[0]
    near = pl.ds(pl.multiple_of(h * rows, rows), rows)
    far = pl.ds(pl.multiple_of((1 - h) * rows, rows), rows)
    out[near, :] = own[...]
    out[far, :] = arrived[:, :q_w].astype(F32)
    for cols, value in ((near, own_kv[...]), (far, arrived[:, q_w:].astype(F32))):
        turned[...] = value.T
        for index, to in enumerate((out_k, out_v)):
            start = pl.multiple_of((2 * index + h) * kv_w, kv_w)
            to[:, cols] = turned[pl.ds(start, kv_w), :]


def wgrad_final(spot, own, own_kv, arrived, kv_w):
    rows, q_w = own.shape
    return call(
        wgrad_final_kernel,
        "wgrad_final",
        spot,
        (own, own_kv, arrived),
        [VMEM] * 3,
        [shape((2 * rows, q_w), F32)] + [shape((kv_w, 2 * rows), F32)] * 2,
        [VMEM] * 3,
        [pltpu.VMEM((own_kv.shape[1], rows), F32)],
    )


def body(
    tokens,
    queries,
    saved_keys,
    saved_values,
    outputs,
    out_grads,
    log_norms,
    w_query,
    w_key,
    w_value,
):
    t = lax.axis_index("tensor")
    d = lax.axis_index("dp")
    h = t % 2
    spot = jnp.stack([t // 2, h, d % 2, d // 4, t // 2 % 2]).astype(jnp.int32)
    kv_w = saved_keys.shape[1]
    q_w = queries.shape[1]
    n_own = tokens.shape[0]
    heads4 = [[4 * k + j for j in range(4)] for k in range(4)]
    ring_x = [[r + 4 * k for k in range(NX)] for r in range(4)]
    plane = [[r + 2 * k for k in range(8)] for r in range(2)]

    w_key, w_value = w_key.T, w_value.T
    own, side, core, both, kv = pack(spot, tokens, saved_keys.T, saved_values.T)
    side = swap_quad(side, 0, 1)
    core = swap_quad(core, 1, 0)
    both = swap_quad(both, 1, 1)
    kv = lax.all_to_all(kv, "tensor", 0, 0, axis_index_groups=heads4, tiled=True)
    queries, out_grads, stats, w_send = prepare(
        spot, queries, out_grads, outputs, log_norms, w_query, w_key, w_value, [own]
    )
    w_side = swap(w_send, "tensor", 1)

    block = token_block(spot, (own, side, core, both), [stats])
    up1, down1 = shift(block, "tensor", 2), shift(block, "tensor", -2)
    own_a, own_b, kv_send, kv_keep = attend(spot, kv, queries, out_grads, stats, [block])
    far_a = swap(own_a, "tensor", 1)
    kv_z = swap(kv_send, "tensor", 2)
    up1, down1, own_b = tie(spot, [up1, down1, own_b], [])
    up2, down2 = shift(up1, "tensor", 2), shift(down1, "tensor", -2)
    w_side = repeat(spot, w_side, NX, [up1])
    w_far = lax.all_to_all(w_side, "dp", 0, 0, axis_index_groups=ring_x, tiled=True)
    kv_keep, kv_send = middle(spot, kv_keep, kv_z, [w_side], [])
    up2, down2, far_a, w_far, kv_send = tie(spot, [up2, down2, far_a, w_far, kv_send], [])
    up3, down3 = shift(up2, "tensor", 2), shift(down2, "tensor", -2)
    kv_y = swap(kv_send, "tensor", 1)
    far_b = swap(own_b, "tensor", 1)
    w_core = swap(w_far, "dp", 1)
    weights, weights_kv = gather_weights(spot, w_query, w_key, w_value, w_far, w_core, [])
    (kv_grad,) = final_kv(spot, kv_keep, kv_y, [weights_kv, far_b], [])
    here = [own_a, own_b, far_a, far_b, kv_grad]
    there = [swap(value, "dp", 1) for value in here]

    up, down = first_parts(spot, weights, weights_kv, here, up3, down3)
    up_next, down_next = shift(up, "tensor", 2), shift(down, "tensor", -2)
    last_up, last_down = up_next, down_next
    parts = token_parts((3, -3, 2, -2, 1, -1, 0), spot, weights, weights_kv, here, [up])
    up, down = ring_step("first", spot, up_next, down_next, parts, (0, 1), [])
    up_next, down_next = shift(up, "tensor", 2), shift(down, "tensor", -2)
    blocks = [block, up1, down1, up2, down2, up3, down3]
    terms = wgrad_parts(spot, blocks, last_up, last_down, here, there, [parts])
    for slots in ((2, 3), (4, 5)):
        up, down = ring_step("next", spot, up_next, down_next, parts, slots, [])
        up_next, down_next = shift(up, "tensor", 2), shift(down, "tensor", -2)
    mine, other = ring_step("last", spot, up_next, down_next, parts, (6, 6), [])
    other = swap(other, "tensor", 1)
    token_grads = jnp.where(
        h == 1,
        jnp.concatenate([other, mine], axis=1),
        jnp.concatenate([mine, other], axis=1),
    )

    terms = terms.reshape(8, DH, terms.shape[2])
    terms = lax.all_to_all(terms, "dp", 0, 0, axis_index_groups=plane, tiled=True)
    own, own_kv, send = wgrad_sum(spot, terms, q_w)
    query_wgrad, key_wgrad, value_wgrad = wgrad_final(
        spot, own, own_kv, swap(send, "tensor", 1), kv_w
    )
    return token_grads, query_wgrad, key_wgrad.T, value_wgrad.T


def solution(mesh):
    in_specs = (
        P(("dp", "tensor"), None),
        P("dp", "tensor"),
        P("dp", "tensor"),
        P("dp", "tensor"),
        P("dp", "tensor"),
        P("dp", "tensor"),
        P("tensor", "dp"),
        P(None, "tensor"),
        P(None, "tensor"),
        P(None, "tensor"),
    )
    out_specs = (P(("dp", "tensor"), None), P("dp", "tensor"), P("dp", "tensor"), P("dp", "tensor"))
    return jax.shard_map(body, mesh=mesh, in_specs=in_specs, out_specs=out_specs, check_vma=False)
```

```python
import functools

import jax
import jax.numpy as jnp
from jax import lax
from jax.experimental import pallas as pl
from jax.experimental.pallas import tpu as pltpu
from jax.sharding import PartitionSpec as P

DH = 128
NZ = 8
NX = 4
TILE = 256
MIB = 2**20
BF = jnp.bfloat16
F32 = jnp.float32
ANY = pl.BlockSpec(memory_space=pl.ANY)
SMEM = pl.BlockSpec(memory_space=pltpu.SMEM)
VMEM = pl.BlockSpec(memory_space=pltpu.VMEM)
Z, H, C, X, ZB = range(5)


def shift(value, axis, step):
    size = lax.axis_size(axis)
    pairs = [(source, (source + step) % size) for source in range(size)]
    return lax.ppermute(value, axis, pairs)


def swap(value, axis, mask):
    pairs = [(source, source ^ mask) for source in range(lax.axis_size(axis))]
    return lax.ppermute(value, axis, pairs)


def swap_quad(value, core, side):
    tensor = lax.axis_size("tensor")
    size = lax.axis_size("dp") * tensor
    mask = core * tensor + side
    pairs = [(source, source ^ mask) for source in range(size)]
    return lax.ppermute(value, ("dp", "tensor"), pairs)


def dot(left, right, left_dim, right_dim):
    return lax.dot_general(
        left, right, (((left_dim,), (right_dim,)), ((), ())), preferred_element_type=F32
    )


def run_copies(copies):
    for copy in copies:
        copy.start()
    for copy in copies:
        copy.wait()


def call(
    kernel, name, spot, ins, specs, outs, out_specs, scratch=(), grid=(), work=0, later=(), through=(), vmem=20
):
    n_ins, n_later, n_through = 1 + len(ins), len(later), len(through)
    n_outs = len(outs)

    def whole(*refs):
        ins_end = n_ins + n_later + n_through
        kernel(*refs[:n_ins], *refs[ins_end : ins_end + n_outs], *refs[ins_end + n_outs + n_through :])

    return pl.pallas_call(
        whole,
        grid=grid,
        in_specs=[SMEM, *specs, *[ANY] * (n_later + n_through)],
        out_specs=[*out_specs, *[ANY] * n_through],
        out_shape=[*outs, *[shape(value.shape, value.dtype) for value in through]],
        input_output_aliases={
            n_ins + n_later + index: n_outs + index for index in range(n_through)
        },
        scratch_shapes=scratch,
        compiler_params=pltpu.CompilerParams(vmem_limit_bytes=vmem * MIB),
        cost_estimate=pl.CostEstimate(flops=work, bytes_accessed=0, transcendentals=0),
        name=name,
    )(spot, *ins, *later, *through)


def shape(dims, dtype=BF):
    return jax.ShapeDtypeStruct(tuple(dims), dtype)


def pack_kernel(spot, tokens, keys, values, own, side, core, both, kv):
    h, c = spot[H], spot[C]
    width = tokens.shape[1]
    kv_w = keys.shape[0]
    for index in range(kv.shape[0]):
        kv[index, :kv_w, :] = keys[...]
        kv[index, kv_w:, :] = values[...]
    for to, to_c, to_h in ((own, c, h), (side, c, 1 - h), (core, 1 - c, h), (both, 1 - c, 1 - h)):
        for part in range(NX):
            for half in range(2):
                start = part * (width // NX) + half * 4 * DH + to_c * 2 * DH + to_h * DH
                start = pl.multiple_of(start, DH)
                to[part, :, half * DH : (half + 1) * DH] = tokens[:, pl.ds(start, DH)]


def pack(spot, tokens, keys, values):
    part = shape((NX, tokens.shape[0], 2 * DH))
    kv = shape((4, 2 * keys.shape[0], keys.shape[1]))
    return call(
        pack_kernel,
        "pack",
        spot,
        (tokens, keys, values),
        [VMEM] * 3,
        [part] * 4 + [kv],
        [VMEM] * 5,
        vmem=64,
    )


def block_kernel(quarter, spot, own, side, core, both, out, start):
    start[0] = ((1 - spot[H]) * 2 + spot[C]) * quarter + spot[X] * (quarter // NX)
    h = spot[H]
    rows = own.shape[1]
    near = pl.ds(pl.multiple_of(h * rows, rows), rows)
    far = pl.ds(pl.multiple_of((1 - h) * rows, rows), rows)
    out[:, 0, near, :] = own[...]
    out[:, 0, far, :] = side[...]
    out[:, 1, near, :] = core[...]
    out[:, 1, far, :] = both[...]


def token_block(spot, parts, quarter, later):
    part, rows, wide = parts[0].shape
    return call(
        functools.partial(block_kernel, quarter),
        "token_block",
        spot,
        parts,
        [VMEM] * 4,
        [shape((part, 2, 2 * rows, wide)), shape((1,), jnp.int32)],
        [VMEM, SMEM],
        later=later,
    )


def halves_kernel(spot, up, down, out_up, out_down):
    out_up[...] = up[...]
    out_down[...] = down[...]


def halves(spot, up, down, later):
    part = (up.shape[0] // 2, *up.shape[1:])
    zeros = (0,) * (len(part) - 1)
    first = pl.BlockSpec(part, lambda step: (0, *zeros))
    return call(
        halves_kernel,
        "halves",
        spot,
        (up, down),
        [first, pl.BlockSpec(part, lambda step: (1, *zeros))],
        [shape(part)] * 2,
        [first] * 2,
        grid=(1,),
        later=later,
    )


def repeat_kernel(spot, value, out):
    if len(value.shape) == len(out.shape):
        out[...] = value[...]
    else:
        for index in range(out.shape[0]):
            out[index] = value[...]


def repeat(spot, value, times, later):
    return call(
        repeat_kernel,
        "repeat",
        spot,
        (value,),
        [VMEM],
        [shape((times, *value.shape) if times else value.shape)],
        [VMEM],
        later=later,
    )[0]


def weights_kernel(spot, w_query, w_key, w_value, far_own, far_core, out, out_kv, sems):
    h, c = spot[H], spot[C]
    half, q2 = out.shape
    q_w, kv_w = q2 // 2, w_key.shape[0]
    piece = far_own.shape[1] - kv_w
    start = pl.multiple_of(h * half, half)
    near = [pl.ds(pl.multiple_of(kind * 2 * kv_w + h * kv_w, kv_w), kv_w) for kind in (0, 1)]
    far = [pl.ds(pl.multiple_of(kind * 2 * kv_w + (1 - h) * kv_w, kv_w), kv_w) for kind in (0, 1)]
    pairs = [
        (w_query.at[pl.ds(start, half), :], out.at[:, pl.ds(0, q_w)]),
        (w_key.at[:, pl.ds(start, half)], out_kv.at[near[0], :]),
        (w_value.at[:, pl.ds(start, half)], out_kv.at[near[1], :]),
    ]
    for ref, place in ((far_own, c), (far_core, 1 - c)):
        for index in range(NX):
            row = pl.multiple_of(place * (half // 2) + index * piece, piece)
            pairs.append(
                (ref.at[index, pl.ds(0, piece), :], out.at[pl.ds(row, piece), pl.ds(q_w, q_w)])
            )
            for kind in (0, 1):
                pairs.append(
                    (
                        ref.at[index, pl.ds(piece, kv_w), pl.ds(kind * piece, piece)],
                        out_kv.at[far[kind], pl.ds(row, piece)],
                    )
                )
    run_copies(
        [
            pltpu.make_async_copy(source, target, sems.at[index])
            for index, (source, target) in enumerate(pairs)
        ]
    )


def gather_weights(spot, w_query, w_key, w_value, far_own, far_core, later):
    width, q_w = w_query.shape
    return call(
        weights_kernel,
        "gather_weights",
        spot,
        (w_query, w_key, w_value, far_own, far_core),
        [ANY] * 5,
        [shape((width // 2, 2 * q_w)), shape((4 * w_key.shape[0], width // 2))],
        [ANY] * 2,
        [pltpu.SemaphoreType.DMA((3 + 6 * NX,))],
        later=later,
    )


def attend_kernel(
    spot, kv, query, grad, output, norms, out_a, out_b, send, keep, keys, values, total, turned, grads
):
    head = pl.program_id(0)
    heads = pl.num_programs(0)
    scaling = DH ** (-0.5)
    seq = query.shape[0]
    part = kv.shape[1] // 2

    @pl.when(head == 0)
    def _():
        for index in range(kv.shape[0]):
            keys[index * part : (index + 1) * part, :] = kv[index, :part, :]
            values[index * part : (index + 1) * part, :] = kv[index, part:, :]
        total[...] = jnp.zeros_like(total)
        filler = jnp.zeros((DH - norms.shape[0], seq), F32)
        turned[...] = jnp.concatenate([norms[...], filler]).T

    which = lax.broadcasted_iota(jnp.int32, turned.shape, 1) == head
    norm = jnp.sum(jnp.where(which, turned[...], 0.0), axis=1, keepdims=True)
    for tile in range(seq // TILE):
        rows = slice(tile * TILE, (tile + 1) * TILE)
        width = (tile + 1) * TILE
        query_t, grad_t = query[rows, :], grad[rows, :]
        scores = dot(query_t, keys[:, :width], 1, 0)
        probs = jnp.exp(scores * scaling - norm[rows])
        row_ids = lax.broadcasted_iota(jnp.int32, probs.shape, 0) + tile * TILE
        col_ids = lax.broadcasted_iota(jnp.int32, probs.shape, 1)
        probs = jnp.where(col_ids <= row_ids, probs, 0.0)
        delta = jnp.sum(grad_t.astype(F32) * output[rows, :].astype(F32), axis=1, keepdims=True)
        dprobs = dot(grad_t, values[:, :width], 1, 0)
        dscores = (probs * (dprobs - delta)).astype(BF)
        grads[rows, :] = (dot(dscores, keys[:, :width], 1, 1) * scaling).astype(BF)
        total[0, :, :width] += dot(query_t, dscores, 0, 0)
        total[1, :, :width] += dot(grad_t, probs.astype(BF), 0, 0)

    @pl.when(head < heads - 1)
    def _():
        out_a[...] = grads[...]

    @pl.when(head == heads - 1)
    def _():
        out_b[...] = grads[...]
        half = DH // 2
        mine = spot[ZB]
        near = pl.ds(pl.multiple_of(mine * half, half), half)
        far = pl.ds(pl.multiple_of((1 - mine) * half, half), half)
        for index, factor in enumerate((scaling, 1.0)):
            keep[index] = total[index, near, :] * factor
            send[index] = (total[index, far, :] * factor).astype(BF)


def attend(spot, kv, queries, out_grads, outputs, norms, later):
    seq = queries.shape[0]
    heads = queries.shape[1] // DH
    cols = pl.BlockSpec((seq, DH), lambda head: (0, head))
    full = lambda a: pl.BlockSpec(a.shape, lambda head: (0,) * len(a.shape))
    outs = [
        shape((seq, (heads - 1) * DH)),
        shape((seq, DH)),
        shape((2, DH // 2, seq)),
        shape((2, DH // 2, seq), F32),
    ]
    return call(
        attend_kernel,
        "attend",
        spot,
        (kv, queries, out_grads, outputs, norms),
        [full(kv), cols, cols, cols, full(norms)],
        outs,
        [
            pl.BlockSpec((seq, DH), lambda head: (0, jnp.minimum(head, heads - 2))),
            *[full(out) for out in outs[1:]],
        ],
        [
            pltpu.VMEM((DH, seq), BF),
            pltpu.VMEM((DH, seq), BF),
            pltpu.VMEM((2, DH, seq), F32),
            pltpu.VMEM((seq, DH), F32),
            pltpu.VMEM((seq, DH), BF),
        ],
        grid=(heads,),
        work=10**9,
        later=later,
    )


def middle_kernel(spot, keep, arrived, out, send):
    total = keep[...] + arrived[...].astype(F32)
    out[...] = total
    send[...] = total.astype(BF)


def middle(spot, keep, arrived, later, through):
    return call(
        middle_kernel,
        "kv_middle",
        spot,
        (keep, arrived),
        [VMEM] * 2,
        [shape(keep.shape, F32), shape(keep.shape)],
        [VMEM] * 2,
        later=later,
        through=through,
    )


def final_kv_kernel(spot, keep, arrived, out):
    total = keep[...] + arrived[...].astype(F32)
    out[...] = total.reshape(out.shape[1], out.shape[0]).T.astype(BF)


def final_kv(spot, keep, arrived, later, through):
    return call(
        final_kv_kernel,
        "kv_final",
        spot,
        (keep, arrived),
        [VMEM] * 2,
        [shape((keep.shape[2], keep.shape[0] * keep.shape[1]))],
        [VMEM],
        later=later,
        through=through,
    )


def offsets(pieces):
    starts, at = [], 0
    for piece in pieces:
        starts.append(at)
        at += piece.shape[1]
    return starts, at


AWAYS = (4, 3, -3, 2, -2, 1, -1, 0)


def load_rows(aways, z, pieces, held, sems):
    starts, _ = offsets(pieces)
    rows = pieces[0].shape[0] // NZ
    copies = []
    for slot, away in enumerate(aways):
        row = pl.multiple_of(lax.rem(z + away + NZ, NZ) * rows, rows)
        for index, piece in enumerate(pieces):
            copies.append(
                pltpu.make_async_copy(
                    piece.at[pl.ds(row, rows), :],
                    held.at[pl.ds(slot * rows, rows), pl.ds(starts[index], piece.shape[1])],
                    sems.at[slot, index],
                )
            )
    return copies


def early_kernel(spot, weights, *rest):
    pieces, (out, held, sems) = rest[:3], rest[3:]

    @pl.when(pl.program_id(0) == 0)
    def _():
        run_copies(load_rows(AWAYS, spot[Z], pieces, held, sems))

    total = dot(held[...], weights[:, : held.shape[1]], 1, 1)
    out[...] = total.reshape(out.shape)


def early_parts(spot, weights, pieces, later):
    seq = pieces[0].shape[0]
    width, deep = weights.shape
    _, depth = offsets(pieces)
    wide = 512
    return call(
        early_kernel,
        "early_parts",
        spot,
        (weights, *pieces),
        [pl.BlockSpec((wide, deep), lambda step: (step, 0)), *[ANY] * 3],
        [shape((NZ, seq // NZ, width), F32)],
        [pl.BlockSpec((NZ, seq // NZ, wide), lambda step: (0, 0, step))],
        [pltpu.VMEM((seq, depth), BF), pltpu.SemaphoreType.DMA((NZ, 3))],
        grid=(width // wide,),
        work=10**9,
        later=later,
    )[0]


def first_kernel(spot, weights, weights_kv, base, far, kv, up, down, held, sems):
    run_copies(load_rows(AWAYS[:1], spot[Z], (far, kv), held, sems))
    wide = up.shape[1]
    deep = far.shape[1]
    for index, out in enumerate((up, down)):
        part = slice(index * wide, (index + 1) * wide)
        total = dot(held[:, :deep], weights[part, :], 1, 1)
        total += dot(held[:, deep:], weights_kv[:, part], 1, 0)
        out[...] = (base[0, :, part] + total).astype(BF)


def first_parts(spot, weights, weights_kv, base, far, kv):
    _, rows, width = base.shape
    depth, deep = far.shape[1] + kv.shape[1], far.shape[1]
    last = weights.shape[1] // deep - 1
    out = pl.BlockSpec((rows, width // 2), lambda step: (0, 0))
    return call(
        first_kernel,
        "first_parts",
        spot,
        (weights, weights_kv, base, far, kv),
        [
            pl.BlockSpec((width, deep), lambda step: (0, last)),
            pl.BlockSpec(weights_kv.shape, lambda step: (0, 0)),
            pl.BlockSpec((1, rows, width), lambda step: (0, 0, 0)),
            ANY,
            ANY,
        ],
        [shape((rows, width // 2))] * 2,
        [out] * 2,
        [pltpu.VMEM((rows, depth), BF), pltpu.SemaphoreType.DMA((1, 2))],
        grid=(1,),
    )


def rest_kernel(spot, weights, weights_kv, base, far, kv, out, held, sems):
    @pl.when(pl.program_id(0) == 0)
    def _():
        run_copies(load_rows(AWAYS[1:], spot[Z], (far, kv), held, sems))

    deep = far.shape[1]
    total = dot(held[:, :deep], weights[...], 1, 1) + dot(held[:, deep:], weights_kv[...], 1, 0)
    out[...] = (base[1:] + total.reshape(out.shape)).astype(BF)


def rest_parts(spot, weights, weights_kv, base, far, kv, later):
    count, rows, width = base.shape
    depth, deep = far.shape[1] + kv.shape[1], far.shape[1]
    last = weights.shape[1] // deep - 1
    wide = 512
    return call(
        rest_kernel,
        "rest_parts",
        spot,
        (weights, weights_kv, base, far, kv),
        [
            pl.BlockSpec((wide, deep), lambda step: (step, last)),
            pl.BlockSpec((kv.shape[1], wide), lambda step: (0, step)),
            pl.BlockSpec((count, rows, wide), lambda step: (0, 0, step)),
            ANY,
            ANY,
        ],
        [shape((count - 1, rows, width))],
        [pl.BlockSpec((count - 1, rows, wide), lambda step: (0, 0, step))],
        [pltpu.VMEM(((count - 1) * rows, depth), BF), pltpu.SemaphoreType.DMA((count - 1, 2))],
        grid=(width // wide,),
        work=10**9,
        later=later,
    )[0]


def ring_kernel(kind, spot, up, down, ups, downs, *outs):
    wide = up.shape[1]
    if kind == "first":
        for arrived, part, out, start in ((up, ups, outs[0], 0), (down, downs, outs[1], wide)):
            out[...] = part[0]
            cols = slice(start, start + wide)
            out[:, cols] = (part[0, :, cols].astype(F32) + arrived[...].astype(F32)).astype(BF)
    elif kind == "next":
        for arrived, part, out in ((up, ups, outs[0]), (down, downs, outs[1])):
            out[...] = (part[0].astype(F32) + arrived[...].astype(F32)).astype(BF)
    else:
        own, send = outs
        h = spot[H]
        rows = own.shape[0]
        for out, side in ((own, h), (send, 1 - h)):
            here = pl.ds(pl.multiple_of(side * rows, rows), rows)
            total = ups[0, here, :].astype(F32) + up[here, :].astype(F32) + down[here, :].astype(F32)
            out[...] = total.astype(BF)


def ring_step(kind, spot, up, down, parts, slots, later):
    _, rows, width = parts.shape
    whole = lambda a: pl.BlockSpec(a.shape, lambda step: (0,) * len(a.shape))
    term = [pl.BlockSpec((1, rows, width), lambda step, slot=slot: (slot, 0, 0)) for slot in slots]
    out = shape((rows // 2 if kind == "last" else rows, width))
    return call(
        functools.partial(ring_kernel, kind),
        "ring_step",
        spot,
        (up, down, parts, parts),
        [whole(up), whole(down), *term],
        [out] * 2,
        [whole(out)] * 2,
        grid=(1,),
        later=later,
    )


def wgrad_kernel(spot, *rest):
    blocks, (up, down), rest = rest[: NZ - 1], rest[NZ - 1 : NZ + 1], rest[NZ + 1 :]
    pieces, (out, held, lefts, sems, left_sems, last_sems) = rest[:10], rest[10:]
    starts, _ = offsets(pieces[:5])
    z = spot[Z]
    rows = blocks[0].shape[2]
    places = (0, -1, 1, -2, 2, -3, 3)

    @pl.when(pl.program_id(0) == 0)
    def _():
        def place(away):
            return pl.ds(pl.multiple_of(lax.rem(z + away + NZ, NZ) * rows, rows), rows)

        copies = [
            pltpu.make_async_copy(
                piece,
                held.at[index // 5, :, pl.ds(starts[index % 5], piece.shape[1])],
                sems.at[index],
            )
            for index, piece in enumerate(pieces)
        ]
        for index, (block, away) in enumerate(zip(blocks, places)):
            copies.append(
                pltpu.make_async_copy(
                    block, lefts.at[:, :, place(away), :], left_sems.at[index]
                )
            )
        for index, last in enumerate((up, down)):
            half = NX // 2
            copies.append(
                pltpu.make_async_copy(
                    last,
                    lefts.at[pl.ds(index * half, half), :, place(NZ // 2), :],
                    last_sems.at[index],
                )
            )
        run_copies(copies)

    left = lefts[pl.program_id(0)]
    left = left.reshape(left.shape[0] * left.shape[1], left.shape[2])
    right = held[...].reshape(left.shape[0], held.shape[2])
    out[0] = dot(left, right, 0, 0).astype(out.dtype)


def wgrad_parts(spot, blocks, up, down, here, there, later):
    seq = here[0].shape[0]
    _, depth = offsets(here)
    wide = blocks[0].shape[3]
    return call(
        wgrad_kernel,
        "wgrad_parts",
        spot,
        (*blocks, up, down, *here, *there),
        [ANY] * (NZ + 11),
        [shape((NX, wide, depth))],
        [pl.BlockSpec((1, wide, depth), lambda step: (step, 0, 0))],
        [
            pltpu.VMEM((2, seq, depth), BF),
            pltpu.VMEM((NX, 2, seq, wide), BF),
            pltpu.SemaphoreType.DMA((10,)),
            pltpu.SemaphoreType.DMA((NZ - 1,)),
            pltpu.SemaphoreType.DMA((2,)),
        ],
        grid=(NX,),
        work=10**10,
        later=later,
    )[0]


def wgrad_sum_kernel(spot, terms, own, own_kv, send):
    total = terms[0].astype(F32)
    for index in range(1, terms.shape[0]):
        total += terms[index].astype(F32)
    q_w = own.shape[1]
    own[...] = total[:, :q_w]
    own_kv[...] = total[:, 2 * q_w :]
    send[...] = total[:, q_w:].astype(BF)


def wgrad_sum(spot, terms, q_w, later):
    _, rows, depth = terms.shape
    return call(
        wgrad_sum_kernel,
        "wgrad_sum",
        spot,
        (terms,),
        [VMEM],
        [shape((rows, q_w), F32), shape((rows, depth - 2 * q_w), F32), shape((rows, depth - q_w))],
        [VMEM] * 3,
        later=later,
    )


def wgrad_final_kernel(spot, own, own_kv, arrived, out, out_k, out_v, turned):
    h = spot[H]
    rows, q_w = own.shape
    kv_w = out_k.shape[0]
    near = pl.ds(pl.multiple_of(h * rows, rows), rows)
    far = pl.ds(pl.multiple_of((1 - h) * rows, rows), rows)
    out[near, :] = own[...]
    out[far, :] = arrived[:, :q_w].astype(F32)
    for cols, value in ((near, own_kv[...]), (far, arrived[:, q_w:].astype(F32))):
        turned[...] = value.T
        for index, to in enumerate((out_k, out_v)):
            start = pl.multiple_of((2 * index + h) * kv_w, kv_w)
            to[:, cols] = turned[pl.ds(start, kv_w), :]


def wgrad_final(spot, own, own_kv, arrived, kv_w):
    rows, q_w = own.shape
    return call(
        wgrad_final_kernel,
        "wgrad_final",
        spot,
        (own, own_kv, arrived),
        [VMEM] * 3,
        [shape((2 * rows, q_w), F32)] + [shape((kv_w, 2 * rows), F32)] * 2,
        [VMEM] * 3,
        [pltpu.VMEM((own_kv.shape[1], rows), F32)],
    )


def body(
    tokens,
    queries,
    saved_keys,
    saved_values,
    outputs,
    out_grads,
    log_norms,
    w_query,
    w_key,
    w_value,
):
    t = lax.axis_index("tensor")
    d = lax.axis_index("dp")
    h = t % 2
    spot = jnp.stack([t // 2, h, d % 2, d // 4, t // 2 % 2]).astype(jnp.int32)
    kv_w = saved_keys.shape[1]
    q_w = queries.shape[1]
    n_own = tokens.shape[0]
    heads4 = [[4 * k + j for j in range(4)] for k in range(4)]
    ring_x = [[r + 4 * k for k in range(NX)] for r in range(4)]
    plane = [[r + 2 * k for k in range(8)] for r in range(2)]

    w_key, w_value = w_key.T, w_value.T
    own, side, core, both, kv = pack(spot, tokens, saved_keys.T, saved_values.T)
    side = swap_quad(side, 0, 1)
    core = swap_quad(core, 1, 0)
    both = swap_quad(both, 1, 1)
    kv = lax.all_to_all(kv, "tensor", 0, 0, axis_index_groups=heads4, tiled=True)
    quarter = tokens.shape[1] // 4
    block, start = token_block(spot, (own, side, core, both), quarter, [])
    up1, down1 = shift(block, "tensor", 2), shift(block, "tensor", -2)
    piece = quarter // NX
    row = start[0]
    w_send = jnp.concatenate(
        [
            lax.dynamic_slice_in_dim(w_query, row, piece, 0),
            jnp.concatenate(
                [lax.dynamic_slice_in_dim(w, row, piece, 1) for w in (w_key, w_value)], axis=1
            ),
        ]
    )
    w_side = swap(w_send, "tensor", 1)

    own_a, own_b, kv_send, kv_keep = attend(
        spot, kv, queries, out_grads, outputs, log_norms, [block]
    )
    w_side = repeat(spot, w_side, NX, [own_a, up1, down1])
    w_far = lax.all_to_all(w_side, "dp", 0, 0, axis_index_groups=ring_x, tiled=True)
    far_a = swap(own_a, "tensor", 1)
    kv_z = swap(kv_send, "tensor", 2)
    up2, down2 = shift(up1, "tensor", 2), shift(down1, "tensor", -2)
    kv_keep, kv_send = middle(spot, kv_keep, kv_z, [up2, down2, far_a], [])
    kv_y = swap(kv_send, "tensor", 1)
    far_b = swap(own_b, "tensor", 1)
    up3, down3 = shift(up2, "tensor", 2), shift(down2, "tensor", -2)
    w_far = repeat(spot, w_far, 0, [kv_send])
    w_core = swap(w_far, "dp", 1)
    weights, weights_kv = gather_weights(
        spot, w_query, w_key, w_value, w_far, w_core, [kv_send]
    )
    base = early_parts(spot, weights, [own_a, own_b, far_a], [])
    up4, down4 = halves(spot, up3, down3, [base])
    up4, down4 = shift(up4, "tensor", 2), shift(down4, "tensor", -2)
    (kv_grad,) = final_kv(spot, kv_keep, kv_y, [base, far_b], [])
    here = [own_a, own_b, far_a, far_b, kv_grad]
    there = [swap(value, "dp", 1) for value in here]

    up, down = first_parts(spot, weights, weights_kv, base, far_b, kv_grad)
    up_next, down_next = shift(up, "tensor", 2), shift(down, "tensor", -2)
    parts = rest_parts(spot, weights, weights_kv, base, far_b, kv_grad, [up])
    blocks = [block, up1, down1, up2, down2, up3, down3]
    terms = wgrad_parts(
        spot, blocks, up4, down4, here, there, [parts, up_next, down_next]
    )
    for kind, slots in (("first", (0, 1)), ("next", (2, 3)), ("next", (4, 5))):
        up, down = ring_step(kind, spot, up_next, down_next, parts, slots, [terms])
        up_next, down_next = shift(up, "tensor", 2), shift(down, "tensor", -2)

    terms = terms.reshape(8, DH, terms.shape[2])
    terms = lax.all_to_all(terms, "dp", 0, 0, axis_index_groups=plane, tiled=True)
    w_own, w_own_kv, w_send = wgrad_sum(spot, terms, q_w, [up])
    w_other = swap(w_send, "tensor", 1)

    mine, other = ring_step("last", spot, up_next, down_next, parts, (6, 6), [w_send])
    other = swap(other, "tensor", 1)
    token_grads = jnp.where(
        h == 1,
        jnp.concatenate([other, mine], axis=1),
        jnp.concatenate([mine, other], axis=1),
    )
    query_wgrad, key_wgrad, value_wgrad = wgrad_final(spot, w_own, w_own_kv, w_other, kv_w)
    return token_grads, query_wgrad, key_wgrad.T, value_wgrad.T


def solution(mesh):
    in_specs = (
        P(("dp", "tensor"), None),
        P("dp", "tensor"),
        P("dp", "tensor"),
        P("dp", "tensor"),
        P("dp", "tensor"),
        P("dp", "tensor"),
        P("tensor", "dp"),
        P(None, "tensor"),
        P(None, "tensor"),
        P(None, "tensor"),
    )
    out_specs = (P(("dp", "tensor"), None), P("dp", "tensor"), P("dp", "tensor"), P("dp", "tensor"))
    return jax.shard_map(body, mesh=mesh, in_specs=in_specs, out_specs=out_specs, check_vma=False)
```

```python
import functools

import jax
import jax.numpy as jnp
from jax import lax
from jax.experimental import pallas as pl
from jax.experimental.pallas import tpu as pltpu
from jax.sharding import PartitionSpec as P

DH = 128
NZ = 8
NX = 4
TILE = 256
MIB = 2**20
BF = jnp.bfloat16
F32 = jnp.float32
ANY = pl.BlockSpec(memory_space=pl.ANY)
SMEM = pl.BlockSpec(memory_space=pltpu.SMEM)
VMEM = pl.BlockSpec(memory_space=pltpu.VMEM)
Z, H, C, X, ZB = range(5)


def shift(value, axis, step):
    size = lax.axis_size(axis)
    pairs = [(source, (source + step) % size) for source in range(size)]
    return lax.ppermute(value, axis, pairs)


def swap(value, axis, mask):
    pairs = [(source, source ^ mask) for source in range(lax.axis_size(axis))]
    return lax.ppermute(value, axis, pairs)


def swap_quad(value, core, side):
    tensor = lax.axis_size("tensor")
    size = lax.axis_size("dp") * tensor
    mask = core * tensor + side
    pairs = [(source, source ^ mask) for source in range(size)]
    return lax.ppermute(value, ("dp", "tensor"), pairs)


def dot(left, right, left_dim, right_dim):
    return lax.dot_general(
        left, right, (((left_dim,), (right_dim,)), ((), ())), preferred_element_type=F32
    )


def run_copies(copies):
    for copy in copies:
        copy.start()
    for copy in copies:
        copy.wait()


def call(
    kernel, name, spot, ins, specs, outs, out_specs, scratch=(), grid=(), work=0, later=(), through=(), vmem=20
):
    n_ins, n_later, n_through = 1 + len(ins), len(later), len(through)
    n_outs = len(outs)

    def whole(*refs):
        ins_end = n_ins + n_later + n_through
        kernel(*refs[:n_ins], *refs[ins_end : ins_end + n_outs], *refs[ins_end + n_outs + n_through :])

    return pl.pallas_call(
        whole,
        grid=grid,
        in_specs=[SMEM, *specs, *[ANY] * (n_later + n_through)],
        out_specs=[*out_specs, *[ANY] * n_through],
        out_shape=[*outs, *[shape(value.shape, value.dtype) for value in through]],
        input_output_aliases={
            n_ins + n_later + index: n_outs + index for index in range(n_through)
        },
        scratch_shapes=scratch,
        compiler_params=pltpu.CompilerParams(vmem_limit_bytes=vmem * MIB),
        cost_estimate=pl.CostEstimate(flops=work, bytes_accessed=0, transcendentals=0),
        name=name,
    )(spot, *ins, *later, *through)


def shape(dims, dtype=BF):
    return jax.ShapeDtypeStruct(tuple(dims), dtype)


def pack_kernel(spot, tokens, keys, values, own, side, core, both, kv):
    h, c = spot[H], spot[C]
    width = tokens.shape[1]
    kv_w = keys.shape[0]
    for index in range(kv.shape[0]):
        kv[index, :kv_w, :] = keys[...]
        kv[index, kv_w:, :] = values[...]
    for to, to_c, to_h in ((own, c, h), (side, c, 1 - h), (core, 1 - c, h), (both, 1 - c, 1 - h)):
        for part in range(NX):
            for half in range(2):
                start = part * (width // NX) + half * 4 * DH + to_c * 2 * DH + to_h * DH
                start = pl.multiple_of(start, DH)
                to[part, :, half * DH : (half + 1) * DH] = tokens[:, pl.ds(start, DH)]


def pack(spot, tokens, keys, values):
    part = shape((NX, tokens.shape[0], 2 * DH))
    kv = shape((4, 2 * keys.shape[0], keys.shape[1]))
    return call(
        pack_kernel,
        "pack",
        spot,
        (tokens, keys, values),
        [VMEM] * 3,
        [part] * 4 + [kv],
        [VMEM] * 5,
        vmem=64,
    )


def block_kernel(quarter, spot, own, side, core, both, out, start):
    start[0] = ((1 - spot[H]) * 2 + spot[C]) * quarter + spot[X] * (quarter // NX)
    h = spot[H]
    rows = own.shape[1]
    near = pl.ds(pl.multiple_of(h * rows, rows), rows)
    far = pl.ds(pl.multiple_of((1 - h) * rows, rows), rows)
    out[:, 0, near, :] = own[...]
    out[:, 0, far, :] = side[...]
    out[:, 1, near, :] = core[...]
    out[:, 1, far, :] = both[...]


def token_block(spot, parts, quarter, later):
    part, rows, wide = parts[0].shape
    return call(
        functools.partial(block_kernel, quarter),
        "token_block",
        spot,
        parts,
        [VMEM] * 4,
        [shape((part, 2, 2 * rows, wide)), shape((1,), jnp.int32)],
        [VMEM, SMEM],
        later=later,
    )


def halves_kernel(spot, up, down, out_up, out_down):
    out_up[...] = up[...]
    out_down[...] = down[...]


def halves(spot, up, down, later):
    part = (up.shape[0] // 2, *up.shape[1:])
    zeros = (0,) * (len(part) - 1)
    first = pl.BlockSpec(part, lambda step: (0, *zeros))
    return call(
        halves_kernel,
        "halves",
        spot,
        (up, down),
        [first, pl.BlockSpec(part, lambda step: (1, *zeros))],
        [shape(part)] * 2,
        [first] * 2,
        grid=(1,),
        later=later,
    )


def repeat_kernel(spot, value, out):
    if len(value.shape) == len(out.shape):
        out[...] = value[...]
    else:
        for index in range(out.shape[0]):
            out[index] = value[...]


def repeat(spot, value, times, later):
    return call(
        repeat_kernel,
        "repeat",
        spot,
        (value,),
        [VMEM],
        [shape((times, *value.shape) if times else value.shape)],
        [VMEM],
        later=later,
    )[0]


def weights_kernel(spot, w_query, w_key, w_value, far_own, far_core, out, out_kv, sems):
    h, c = spot[H], spot[C]
    half, q2 = out.shape
    q_w, kv_w = q2 // 2, w_key.shape[0]
    piece = far_own.shape[1] - kv_w
    start = pl.multiple_of(h * half, half)
    near = [pl.ds(pl.multiple_of(kind * 2 * kv_w + h * kv_w, kv_w), kv_w) for kind in (0, 1)]
    far = [pl.ds(pl.multiple_of(kind * 2 * kv_w + (1 - h) * kv_w, kv_w), kv_w) for kind in (0, 1)]
    pairs = [
        (w_query.at[pl.ds(start, half), :], out.at[:, pl.ds(0, q_w)]),
        (w_key.at[:, pl.ds(start, half)], out_kv.at[near[0], :]),
        (w_value.at[:, pl.ds(start, half)], out_kv.at[near[1], :]),
    ]
    for ref, place in ((far_own, c), (far_core, 1 - c)):
        for index in range(NX):
            row = pl.multiple_of(place * (half // 2) + index * piece, piece)
            pairs.append(
                (ref.at[index, pl.ds(0, piece), :], out.at[pl.ds(row, piece), pl.ds(q_w, q_w)])
            )
            for kind in (0, 1):
                pairs.append(
                    (
                        ref.at[index, pl.ds(piece, kv_w), pl.ds(kind * piece, piece)],
                        out_kv.at[far[kind], pl.ds(row, piece)],
                    )
                )
    run_copies(
        [
            pltpu.make_async_copy(source, target, sems.at[index])
            for index, (source, target) in enumerate(pairs)
        ]
    )


def gather_weights(spot, w_query, w_key, w_value, far_own, far_core, later):
    width, q_w = w_query.shape
    return call(
        weights_kernel,
        "gather_weights",
        spot,
        (w_query, w_key, w_value, far_own, far_core),
        [ANY] * 5,
        [shape((width // 2, 2 * q_w)), shape((4 * w_key.shape[0], width // 2))],
        [ANY] * 2,
        [pltpu.SemaphoreType.DMA((3 + 6 * NX,))],
        later=later,
    )


def attend_kernel(
    spot, kv, query, grad, output, norms, out_a, out_b, send, keep, keys, values, total, turned, grads
):
    head = pl.program_id(0)
    heads = pl.num_programs(0)
    scaling = DH ** (-0.5)
    seq = query.shape[0]
    part = kv.shape[1] // 2

    @pl.when(head == 0)
    def _():
        for index in range(kv.shape[0]):
            keys[index * part : (index + 1) * part, :] = kv[index, :part, :]
            values[index * part : (index + 1) * part, :] = kv[index, part:, :]
        total[...] = jnp.zeros_like(total)
        filler = jnp.zeros((DH - norms.shape[0], seq), F32)
        turned[...] = jnp.concatenate([norms[...], filler]).T

    which = lax.broadcasted_iota(jnp.int32, turned.shape, 1) == head
    norm = jnp.sum(jnp.where(which, turned[...], 0.0), axis=1, keepdims=True)
    for tile in range(seq // TILE):
        rows = slice(tile * TILE, (tile + 1) * TILE)
        width = (tile + 1) * TILE
        query_t, grad_t = query[rows, :], grad[rows, :]
        scores = dot(query_t, keys[:, :width], 1, 0)
        probs = jnp.exp(scores * scaling - norm[rows])
        row_ids = lax.broadcasted_iota(jnp.int32, probs.shape, 0) + tile * TILE
        col_ids = lax.broadcasted_iota(jnp.int32, probs.shape, 1)
        probs = jnp.where(col_ids <= row_ids, probs, 0.0)
        delta = jnp.sum(grad_t.astype(F32) * output[rows, :].astype(F32), axis=1, keepdims=True)
        dprobs = dot(grad_t, values[:, :width], 1, 0)
        dscores = (probs * (dprobs - delta)).astype(BF)
        grads[rows, :] = (dot(dscores, keys[:, :width], 1, 1) * scaling).astype(BF)
        total[0, :, :width] += dot(query_t, dscores, 0, 0)
        total[1, :, :width] += dot(grad_t, probs.astype(BF), 0, 0)

    @pl.when(head < heads - 1)
    def _():
        out_a[...] = grads[...]

    @pl.when(head == heads - 1)
    def _():
        out_b[...] = grads[...]
        half = DH // 2
        mine = spot[ZB]
        near = pl.ds(pl.multiple_of(mine * half, half), half)
        far = pl.ds(pl.multiple_of((1 - mine) * half, half), half)
        for index, factor in enumerate((scaling, 1.0)):
            keep[index] = total[index, near, :] * factor
            send[index] = (total[index, far, :] * factor).astype(BF)


def attend(spot, kv, queries, out_grads, outputs, norms, later):
    seq = queries.shape[0]
    heads = queries.shape[1] // DH
    cols = pl.BlockSpec((seq, DH), lambda head: (0, head))
    full = lambda a: pl.BlockSpec(a.shape, lambda head: (0,) * len(a.shape))
    outs = [
        shape((seq, (heads - 1) * DH)),
        shape((seq, DH)),
        shape((2, DH // 2, seq)),
        shape((2, DH // 2, seq), F32),
    ]
    return call(
        attend_kernel,
        "attend",
        spot,
        (kv, queries, out_grads, outputs, norms),
        [full(kv), cols, cols, cols, full(norms)],
        outs,
        [
            pl.BlockSpec((seq, DH), lambda head: (0, jnp.minimum(head, heads - 2))),
            *[full(out) for out in outs[1:]],
        ],
        [
            pltpu.VMEM((DH, seq), BF),
            pltpu.VMEM((DH, seq), BF),
            pltpu.VMEM((2, DH, seq), F32),
            pltpu.VMEM((seq, DH), F32),
            pltpu.VMEM((seq, DH), BF),
        ],
        grid=(heads,),
        work=10**9,
        later=later,
    )


def middle_kernel(spot, keep, arrived, out, send):
    total = keep[...] + arrived[...].astype(F32)
    out[...] = total
    send[...] = total.astype(BF)


def middle(spot, keep, arrived, later, through):
    return call(
        middle_kernel,
        "kv_middle",
        spot,
        (keep, arrived),
        [VMEM] * 2,
        [shape(keep.shape, F32), shape(keep.shape)],
        [VMEM] * 2,
        later=later,
        through=through,
    )


def final_kv_kernel(spot, keep, arrived, early, far, out):
    total = keep[...] + arrived[...].astype(F32)
    start = early.shape[1]
    deep = start + far.shape[1]
    out[:, :start] = early[...]
    out[:, start:deep] = far[...]
    out[:, deep:] = total.reshape(out.shape[1] - deep, out.shape[0]).T.astype(BF)


def final_kv(spot, keep, arrived, early, far, later):
    return call(
        final_kv_kernel,
        "kv_final",
        spot,
        (keep, arrived, early, far),
        [VMEM] * 4,
        [shape((keep.shape[2], early.shape[1] + far.shape[1] + keep.shape[0] * keep.shape[1]))],
        [VMEM],
        later=later,
    )[0]


def offsets(pieces):
    starts, at = [], 0
    for piece in pieces:
        starts.append(at)
        at += piece.shape[1]
    return starts, at


AWAYS = (4, 3, -3, 2, -2, 1, -1, 0)


def load_rows(aways, z, pieces, held, sems):
    starts, total = offsets(pieces)
    skip = total - held.shape[1]
    rows = pieces[0].shape[0] // NZ
    copies = []
    for slot, away in enumerate(aways):
        row = pl.multiple_of(lax.rem(z + away + NZ, NZ) * rows, rows)
        for index, piece in enumerate(pieces):
            copies.append(
                pltpu.make_async_copy(
                    piece.at[pl.ds(row, rows), pl.ds(skip, piece.shape[1] - skip)],
                    held.at[
                        pl.ds(slot * rows, rows), pl.ds(starts[index], piece.shape[1] - skip)
                    ],
                    sems.at[slot, index],
                )
            )
    return copies


def early_kernel(spot, weights, *rest):
    pieces, (out, packed, held, sems) = rest[:3], rest[3:]
    rows = out.shape[1]

    @pl.when(pl.program_id(0) == 0)
    def _():
        run_copies(load_rows(AWAYS, spot[Z], pieces, held, sems))
        for slot, away in enumerate(AWAYS):
            row = pl.multiple_of(lax.rem(spot[Z] + away + NZ, NZ) * rows, rows)
            packed[pl.ds(row, rows), :] = held[slot * rows : (slot + 1) * rows, :]

    total = dot(held[...], weights[:, : held.shape[1]], 1, 1)
    out[...] = total.reshape(out.shape)


def early_parts(spot, weights, pieces, later):
    seq = pieces[0].shape[0]
    width, deep = weights.shape
    _, depth = offsets(pieces)
    wide = 512
    return call(
        early_kernel,
        "early_parts",
        spot,
        (weights, *pieces),
        [pl.BlockSpec((wide, deep), lambda step: (step, 0)), *[ANY] * 3],
        [shape((NZ, seq // NZ, width), F32), shape((seq, depth))],
        [
            pl.BlockSpec((NZ, seq // NZ, wide), lambda step: (0, 0, step)),
            pl.BlockSpec((seq, depth), lambda step: (0, 0)),
        ],
        [pltpu.VMEM((seq, depth), BF), pltpu.SemaphoreType.DMA((NZ, 3))],
        grid=(width // wide,),
        work=10**9,
        later=later,
    )


def first_kernel(spot, weights, weights_kv, base, late, up, down, held, sems):
    run_copies(load_rows(AWAYS[:1], spot[Z], (late,), held, sems))
    wide = up.shape[1]
    deep = weights.shape[1]
    for index, out in enumerate((up, down)):
        part = slice(index * wide, (index + 1) * wide)
        total = dot(held[:, :deep], weights[part, :], 1, 1)
        total += dot(held[:, deep:], weights_kv[:, part], 1, 0)
        out[...] = (base[0, :, part] + total).astype(BF)


def first_parts(spot, weights, weights_kv, base, late, deep):
    _, rows, width = base.shape
    depth = deep + weights_kv.shape[0]
    last = weights.shape[1] // deep - 1
    out = pl.BlockSpec((rows, width // 2), lambda step: (0, 0))
    return call(
        first_kernel,
        "first_parts",
        spot,
        (weights, weights_kv, base, late),
        [
            pl.BlockSpec((width, deep), lambda step: (0, last)),
            pl.BlockSpec(weights_kv.shape, lambda step: (0, 0)),
            pl.BlockSpec((1, rows, width), lambda step: (0, 0, 0)),
            ANY,
        ],
        [shape((rows, width // 2))] * 2,
        [out] * 2,
        [pltpu.VMEM((rows, depth), BF), pltpu.SemaphoreType.DMA((1, 1))],
        grid=(1,),
    )


def rest_kernel(spot, weights, weights_kv, base, late, out, held, sems):
    @pl.when(pl.program_id(0) == 0)
    def _():
        run_copies(load_rows(AWAYS[1:], spot[Z], (late,), held, sems))

    deep = weights.shape[1]
    total = dot(held[:, :deep], weights[...], 1, 1) + dot(held[:, deep:], weights_kv[...], 1, 0)
    out[...] = (base[1:] + total.reshape(out.shape)).astype(BF)


def rest_parts(spot, weights, weights_kv, base, late, deep, later):
    count, rows, width = base.shape
    depth = deep + weights_kv.shape[0]
    last = weights.shape[1] // deep - 1
    wide = 512
    return call(
        rest_kernel,
        "rest_parts",
        spot,
        (weights, weights_kv, base, late),
        [
            pl.BlockSpec((wide, deep), lambda step: (step, last)),
            pl.BlockSpec((depth - deep, wide), lambda step: (0, step)),
            pl.BlockSpec((count, rows, wide), lambda step: (0, 0, step)),
            ANY,
        ],
        [shape((count - 1, rows, width))],
        [pl.BlockSpec((count - 1, rows, wide), lambda step: (0, 0, step))],
        [pltpu.VMEM(((count - 1) * rows, depth), BF), pltpu.SemaphoreType.DMA((count - 1, 1))],
        grid=(width // wide,),
        work=10**9,
        later=later,
    )[0]


def ring_kernel(kind, spot, up, down, ups, downs, *outs):
    wide = up.shape[1]
    if kind == "first":
        for arrived, part, out, start in ((up, ups, outs[0], 0), (down, downs, outs[1], wide)):
            out[...] = part[0]
            cols = slice(start, start + wide)
            out[:, cols] = (part[0, :, cols].astype(F32) + arrived[...].astype(F32)).astype(BF)
    elif kind == "next":
        for arrived, part, out in ((up, ups, outs[0]), (down, downs, outs[1])):
            out[...] = (part[0].astype(F32) + arrived[...].astype(F32)).astype(BF)
    else:
        own, send = outs
        h = spot[H]
        rows = own.shape[0]
        for out, side in ((own, h), (send, 1 - h)):
            here = pl.ds(pl.multiple_of(side * rows, rows), rows)
            total = ups[0, here, :].astype(F32) + up[here, :].astype(F32) + down[here, :].astype(F32)
            out[...] = total.astype(BF)


def ring_step(kind, spot, up, down, parts, slots, later):
    _, rows, width = parts.shape
    whole = lambda a: pl.BlockSpec(a.shape, lambda step: (0,) * len(a.shape))
    term = [pl.BlockSpec((1, rows, width), lambda step, slot=slot: (slot, 0, 0)) for slot in slots]
    out = shape((rows // 2 if kind == "last" else rows, width))
    return call(
        functools.partial(ring_kernel, kind),
        "ring_step",
        spot,
        (up, down, parts, parts),
        [whole(up), whole(down), *term],
        [out] * 2,
        [whole(out)] * 2,
        grid=(1,),
        later=later,
    )


def wgrad_kernel(spot, *rest):
    blocks, (up, down), rest = rest[: NZ - 1], rest[NZ - 1 : NZ + 1], rest[NZ + 1 :]
    pieces, (out, held, lefts, sems, left_sems, last_sems) = rest[:2], rest[2:]
    z = spot[Z]
    rows = blocks[0].shape[2]
    places = (0, -1, 1, -2, 2, -3, 3)

    @pl.when(pl.program_id(0) == 0)
    def _():
        def place(away):
            return pl.ds(pl.multiple_of(lax.rem(z + away + NZ, NZ) * rows, rows), rows)

        copies = [
            pltpu.make_async_copy(piece, held.at[index], sems.at[index])
            for index, piece in enumerate(pieces)
        ]
        for index, (block, away) in enumerate(zip(blocks, places)):
            copies.append(
                pltpu.make_async_copy(
                    block, lefts.at[:, :, place(away), :], left_sems.at[index]
                )
            )
        for index, last in enumerate((up, down)):
            half = NX // 2
            copies.append(
                pltpu.make_async_copy(
                    last,
                    lefts.at[pl.ds(index * half, half), :, place(NZ // 2), :],
                    last_sems.at[index],
                )
            )
        run_copies(copies)

    left = lefts[pl.program_id(0)]
    left = left.reshape(left.shape[0] * left.shape[1], left.shape[2])
    right = held[...].reshape(left.shape[0], held.shape[2])
    out[0] = dot(left, right, 0, 0).astype(out.dtype)


def wgrad_parts(spot, blocks, up, down, here, there, later):
    seq, depth = here.shape
    wide = blocks[0].shape[3]
    return call(
        wgrad_kernel,
        "wgrad_parts",
        spot,
        (*blocks, up, down, here, there),
        [ANY] * (NZ + 3),
        [shape((NX, wide, depth))],
        [pl.BlockSpec((1, wide, depth), lambda step: (step, 0, 0))],
        [
            pltpu.VMEM((2, seq, depth), BF),
            pltpu.VMEM((NX, 2, seq, wide), BF),
            pltpu.SemaphoreType.DMA((2,)),
            pltpu.SemaphoreType.DMA((NZ - 1,)),
            pltpu.SemaphoreType.DMA((2,)),
        ],
        grid=(NX,),
        work=10**10,
        later=later,
    )[0]


def wgrad_sum_kernel(spot, terms, own, own_kv, send):
    total = terms[0].astype(F32)
    for index in range(1, terms.shape[0]):
        total += terms[index].astype(F32)
    q_w = own.shape[1]
    own[...] = total[:, :q_w]
    own_kv[...] = total[:, 2 * q_w :]
    send[...] = total[:, q_w:].astype(BF)


def wgrad_sum(spot, terms, q_w, later):
    _, rows, depth = terms.shape
    return call(
        wgrad_sum_kernel,
        "wgrad_sum",
        spot,
        (terms,),
        [VMEM],
        [shape((rows, q_w), F32), shape((rows, depth - 2 * q_w), F32), shape((rows, depth - q_w))],
        [VMEM] * 3,
        later=later,
    )


def final_kernel(
    spot, mine, other, own, own_kv, arrived, out_tokens, out, out_k, out_v, turned
):
    h = spot[H]
    wide = mine.shape[1]
    out_tokens[:, pl.ds(pl.multiple_of(h * wide, wide), wide)] = mine[...]
    out_tokens[:, pl.ds(pl.multiple_of((1 - h) * wide, wide), wide)] = other[...]
    rows, q_w = own.shape
    kv_w = out_k.shape[0]
    near = pl.ds(pl.multiple_of(h * rows, rows), rows)
    far = pl.ds(pl.multiple_of((1 - h) * rows, rows), rows)
    out[near, :] = own[...]
    out[far, :] = arrived[:, :q_w].astype(F32)
    for cols, value in ((near, own_kv[...]), (far, arrived[:, q_w:].astype(F32))):
        turned[...] = value.T
        for index, to in enumerate((out_k, out_v)):
            start = pl.multiple_of((2 * index + h) * kv_w, kv_w)
            to[:, cols] = turned[pl.ds(start, kv_w), :]


def final(spot, mine, other, own, own_kv, arrived, kv_w):
    n_own, wide = mine.shape
    rows, q_w = own.shape
    return call(
        final_kernel,
        "final",
        spot,
        (mine, other, own, own_kv, arrived),
        [VMEM] * 5,
        [
            shape((n_own, 2 * wide)),
            shape((2 * rows, q_w), F32),
            *[shape((kv_w, 2 * rows), F32)] * 2,
        ],
        [VMEM] * 4,
        [pltpu.VMEM((own_kv.shape[1], rows), F32)],
    )


def body(
    tokens,
    queries,
    saved_keys,
    saved_values,
    outputs,
    out_grads,
    log_norms,
    w_query,
    w_key,
    w_value,
):
    t = lax.axis_index("tensor")
    d = lax.axis_index("dp")
    h = t % 2
    spot = jnp.stack([t // 2, h, d % 2, d // 4, t // 2 % 2]).astype(jnp.int32)
    kv_w = saved_keys.shape[1]
    q_w = queries.shape[1]
    n_own = tokens.shape[0]
    heads4 = [[4 * k + j for j in range(4)] for k in range(4)]
    ring_x = [[r + 4 * k for k in range(NX)] for r in range(4)]
    plane = [[r + 2 * k for k in range(8)] for r in range(2)]

    w_key, w_value = w_key.T, w_value.T
    own, side, core, both, kv = pack(spot, tokens, saved_keys.T, saved_values.T)
    side = swap_quad(side, 0, 1)
    core = swap_quad(core, 1, 0)
    both = swap_quad(both, 1, 1)
    kv = lax.all_to_all(kv, "tensor", 0, 0, axis_index_groups=heads4, tiled=True)
    quarter = tokens.shape[1] // 4
    block, start = token_block(spot, (own, side, core, both), quarter, [])
    up1, down1 = shift(block, "tensor", 2), shift(block, "tensor", -2)
    piece = quarter // NX
    row = start[0]
    w_send = jnp.concatenate(
        [
            lax.dynamic_slice_in_dim(w_query, row, piece, 0),
            jnp.concatenate(
                [lax.dynamic_slice_in_dim(w, row, piece, 1) for w in (w_key, w_value)], axis=1
            ),
        ]
    )
    w_side = swap(w_send, "tensor", 1)

    own_a, own_b, kv_send, kv_keep = attend(
        spot, kv, queries, out_grads, outputs, log_norms, [block]
    )
    w_side = repeat(spot, w_side, NX, [own_a, up1, down1])
    w_far = lax.all_to_all(w_side, "dp", 0, 0, axis_index_groups=ring_x, tiled=True)
    far_a = swap(own_a, "tensor", 1)
    kv_z = swap(kv_send, "tensor", 2)
    up2, down2 = shift(up1, "tensor", 2), shift(down1, "tensor", -2)
    kv_keep, kv_send = middle(spot, kv_keep, kv_z, [up2, down2, far_a], [])
    kv_y = swap(kv_send, "tensor", 1)
    far_b = swap(own_b, "tensor", 1)
    up3, down3 = shift(up2, "tensor", 2), shift(down2, "tensor", -2)
    w_far = repeat(spot, w_far, 0, [kv_send])
    w_core = swap(w_far, "dp", 1)
    weights, weights_kv = gather_weights(
        spot, w_query, w_key, w_value, w_far, w_core, [kv_send]
    )
    base, early = early_parts(spot, weights, [own_a, own_b, far_a], [])
    up4, down4 = halves(spot, up3, down3, [base])
    up4, down4 = shift(up4, "tensor", 2), shift(down4, "tensor", -2)
    here = final_kv(spot, kv_keep, kv_y, early, far_b, [base, up3, down3])
    there = swap(here, "dp", 1)

    up, down = first_parts(spot, weights, weights_kv, base, here, DH)
    up_next, down_next = shift(up, "tensor", 2), shift(down, "tensor", -2)
    parts = rest_parts(spot, weights, weights_kv, base, here, DH, [up])
    blocks = [block, up1, down1, up2, down2, up3, down3]
    terms = wgrad_parts(
        spot, blocks, up4, down4, here, there, [parts, up_next, down_next]
    )
    for kind, slots in (("first", (0, 1)), ("next", (2, 3)), ("next", (4, 5))):
        up, down = ring_step(kind, spot, up_next, down_next, parts, slots, [terms])
        up_next, down_next = shift(up, "tensor", 2), shift(down, "tensor", -2)

    terms = terms.reshape(8, DH, terms.shape[2])
    terms = lax.all_to_all(terms, "dp", 0, 0, axis_index_groups=plane, tiled=True)
    w_own, w_own_kv, w_send = wgrad_sum(spot, terms, q_w, [up])
    w_other = swap(w_send, "tensor", 1)

    mine, other = ring_step("last", spot, up_next, down_next, parts, (6, 6), [w_send])
    other = swap(other, "tensor", 1)
    token_grads, query_wgrad, key_wgrad, value_wgrad = final(
        spot, mine, other, w_own, w_own_kv, w_other, kv_w
    )
    return token_grads, query_wgrad, key_wgrad.T, value_wgrad.T


def solution(mesh):
    in_specs = (
        P(("dp", "tensor"), None),
        P("dp", "tensor"),
        P("dp", "tensor"),
        P("dp", "tensor"),
        P("dp", "tensor"),
        P("dp", "tensor"),
        P("tensor", "dp"),
        P(None, "tensor"),
        P(None, "tensor"),
        P(None, "tensor"),
    )
    out_specs = (P(("dp", "tensor"), None), P("dp", "tensor"), P("dp", "tensor"), P("dp", "tensor"))
    return jax.shard_map(body, mesh=mesh, in_specs=in_specs, out_specs=out_specs, check_vma=False)
```

```python
import functools

import jax
import jax.numpy as jnp
from jax import lax
from jax.experimental import pallas as pl
from jax.experimental.pallas import tpu as pltpu
from jax.sharding import PartitionSpec as P

DH = 128
NZ = 8
NX = 4
TILE = 256
MIB = 2**20
BF = jnp.bfloat16
F32 = jnp.float32
ANY = pl.BlockSpec(memory_space=pl.ANY)
SMEM = pl.BlockSpec(memory_space=pltpu.SMEM)
VMEM = pl.BlockSpec(memory_space=pltpu.VMEM)
Z, H, C, X, ZB = range(5)


def shift(value, axis, step):
    size = lax.axis_size(axis)
    pairs = [(source, (source + step) % size) for source in range(size)]
    return lax.ppermute(value, axis, pairs)


def swap(value, axis, mask):
    pairs = [(source, source ^ mask) for source in range(lax.axis_size(axis))]
    return lax.ppermute(value, axis, pairs)


def swap_quad(value, core, side):
    tensor = lax.axis_size("tensor")
    size = lax.axis_size("dp") * tensor
    mask = core * tensor + side
    pairs = [(source, source ^ mask) for source in range(size)]
    return lax.ppermute(value, ("dp", "tensor"), pairs)


def dot(left, right, left_dim, right_dim):
    return lax.dot_general(
        left, right, (((left_dim,), (right_dim,)), ((), ())), preferred_element_type=F32
    )


def run_copies(copies):
    for copy in copies:
        copy.start()
    for copy in copies:
        copy.wait()


def call(
    kernel, name, spot, ins, specs, outs, out_specs, scratch=(), grid=(), work=0, later=(), through=(), vmem=20
):
    n_ins, n_later, n_through = 1 + len(ins), len(later), len(through)
    n_outs = len(outs)

    def whole(*refs):
        ins_end = n_ins + n_later + n_through
        kernel(*refs[:n_ins], *refs[ins_end : ins_end + n_outs], *refs[ins_end + n_outs + n_through :])

    return pl.pallas_call(
        whole,
        grid=grid,
        in_specs=[SMEM, *specs, *[ANY] * (n_later + n_through)],
        out_specs=[*out_specs, *[ANY] * n_through],
        out_shape=[*outs, *[shape(value.shape, value.dtype) for value in through]],
        input_output_aliases={
            n_ins + n_later + index: n_outs + index for index in range(n_through)
        },
        scratch_shapes=scratch,
        compiler_params=pltpu.CompilerParams(vmem_limit_bytes=vmem * MIB),
        cost_estimate=pl.CostEstimate(flops=work, bytes_accessed=0, transcendentals=0),
        name=name,
    )(spot, *ins, *later, *through)


def shape(dims, dtype=BF):
    return jax.ShapeDtypeStruct(tuple(dims), dtype)


def pack_kernel(spot, tokens, keys, values, own, side, core, both, kv):
    h, c = spot[H], spot[C]
    width = tokens.shape[1]
    kv_w = keys.shape[0]
    for index in range(kv.shape[0]):
        kv[index, :kv_w, :] = keys[...]
        kv[index, kv_w:, :] = values[...]
    for to, to_c, to_h in ((own, c, h), (side, c, 1 - h), (core, 1 - c, h), (both, 1 - c, 1 - h)):
        for part in range(NX):
            for half in range(2):
                start = part * (width // NX) + half * 4 * DH + to_c * 2 * DH + to_h * DH
                start = pl.multiple_of(start, DH)
                to[part, :, half * DH : (half + 1) * DH] = tokens[:, pl.ds(start, DH)]


def pack(spot, tokens, keys, values):
    part = shape((NX, tokens.shape[0], 2 * DH))
    kv = shape((4, 2 * keys.shape[0], keys.shape[1]))
    return call(
        pack_kernel,
        "pack",
        spot,
        (tokens, keys, values),
        [VMEM] * 3,
        [part] * 4 + [kv],
        [VMEM] * 5,
        vmem=64,
    )


def block_kernel(quarter, spot, own, side, core, both, out, start):
    start[0] = ((1 - spot[H]) * 2 + spot[C]) * quarter + lax.rem(spot[X], 2) * (quarter // 2)
    h = spot[H]
    rows = own.shape[1]
    near = pl.ds(pl.multiple_of(h * rows, rows), rows)
    far = pl.ds(pl.multiple_of((1 - h) * rows, rows), rows)
    out[:, 0, near, :] = own[...]
    out[:, 0, far, :] = side[...]
    out[:, 1, near, :] = core[...]
    out[:, 1, far, :] = both[...]


def token_block(spot, parts, quarter, later):
    part, rows, wide = parts[0].shape
    return call(
        functools.partial(block_kernel, quarter),
        "token_block",
        spot,
        parts,
        [VMEM] * 4,
        [shape((part, 2, 2 * rows, wide)), shape((1,), jnp.int32)],
        [VMEM, SMEM],
        later=later,
    )


def again_kernel(spot, value, out):
    out[...] = value[...]


def again(spot, value, later):
    return call(
        again_kernel, "again", spot, (value,), [VMEM], [shape(value.shape)], [VMEM], later=later
    )[0]


def halves_kernel(spot, up, down, out_up, out_down):
    out_up[...] = up[...]
    out_down[...] = down[...]


def halves(spot, up, down, later):
    part = (up.shape[0] // 2, *up.shape[1:])
    zeros = (0,) * (len(part) - 1)
    first = pl.BlockSpec(part, lambda step: (0, *zeros))
    return call(
        halves_kernel,
        "halves",
        spot,
        (up, down),
        [first, pl.BlockSpec(part, lambda step: (1, *zeros))],
        [shape(part)] * 2,
        [first] * 2,
        grid=(1,),
        later=later,
    )


def weights_kernel(spot, w_query, w_key, w_value, *rest):
    parts, (out, out_kv, sems) = rest[:4], rest[4:]
    h, c, side = spot[H], spot[C], lax.rem(spot[X], 2)
    half, q2 = out.shape
    q_w, kv_w = q2 // 2, w_key.shape[0]
    piece = parts[0].shape[0] - 2 * kv_w
    start = pl.multiple_of(h * half, half)
    near = [pl.ds(pl.multiple_of(kind * 2 * kv_w + h * kv_w, kv_w), kv_w) for kind in (0, 1)]
    far = [pl.ds(pl.multiple_of(kind * 2 * kv_w + (1 - h) * kv_w, kv_w), kv_w) for kind in (0, 1)]
    pairs = [
        (w_query.at[pl.ds(start, half), :], out.at[:, pl.ds(0, q_w)]),
        (w_key.at[:, pl.ds(start, half)], out_kv.at[near[0], :]),
        (w_value.at[:, pl.ds(start, half)], out_kv.at[near[1], :]),
    ]
    places = ((c, side), (c, 1 - side), (1 - c, side), (1 - c, 1 - side))
    for ref, (core, part) in zip(parts, places):
        row = pl.multiple_of(core * (half // 2) + part * piece, piece)
        pairs.append((ref.at[pl.ds(0, piece), :], out.at[pl.ds(row, piece), pl.ds(q_w, q_w)]))
        for kind in (0, 1):
            pairs.append(
                (
                    ref.at[pl.ds(piece + kind * kv_w, kv_w), :],
                    out_kv.at[far[kind], pl.ds(row, piece)],
                )
            )
    run_copies(
        [
            pltpu.make_async_copy(source, target, sems.at[index])
            for index, (source, target) in enumerate(pairs)
        ]
    )


def gather_weights(spot, w_query, w_key, w_value, parts, later):
    width, q_w = w_query.shape
    return call(
        weights_kernel,
        "gather_weights",
        spot,
        (w_query, w_key, w_value, *parts),
        [ANY] * 7,
        [shape((width // 2, 2 * q_w)), shape((4 * w_key.shape[0], width // 2))],
        [ANY] * 2,
        [pltpu.SemaphoreType.DMA((15,))],
        later=later,
    )


def attend_kernel(
    spot, kv, query, grad, output, norms, out_a, out_b, send, keep, keys, values, total, turned, grads
):
    head = pl.program_id(0)
    heads = pl.num_programs(0)
    scaling = DH ** (-0.5)
    seq = query.shape[0]
    part = kv.shape[1] // 2

    @pl.when(head == 0)
    def _():
        for index in range(kv.shape[0]):
            keys[index * part : (index + 1) * part, :] = kv[index, :part, :]
            values[index * part : (index + 1) * part, :] = kv[index, part:, :]
        total[...] = jnp.zeros_like(total)
        filler = jnp.zeros((DH - norms.shape[0], seq), F32)
        turned[...] = jnp.concatenate([norms[...], filler]).T

    which = lax.broadcasted_iota(jnp.int32, turned.shape, 1) == head
    norm = jnp.sum(jnp.where(which, turned[...], 0.0), axis=1, keepdims=True)
    for tile in range(seq // TILE):
        rows = slice(tile * TILE, (tile + 1) * TILE)
        width = (tile + 1) * TILE
        query_t, grad_t = query[rows, :], grad[rows, :]
        scores = dot(query_t, keys[:, :width], 1, 0)
        probs = jnp.exp(scores * scaling - norm[rows])
        row_ids = lax.broadcasted_iota(jnp.int32, probs.shape, 0) + tile * TILE
        col_ids = lax.broadcasted_iota(jnp.int32, probs.shape, 1)
        probs = jnp.where(col_ids <= row_ids, probs, 0.0)
        delta = jnp.sum(grad_t.astype(F32) * output[rows, :].astype(F32), axis=1, keepdims=True)
        dprobs = dot(grad_t, values[:, :width], 1, 0)
        dscores = (probs * (dprobs - delta)).astype(BF)
        grads[rows, :] = (dot(dscores, keys[:, :width], 1, 1) * scaling).astype(BF)
        total[0, :, :width] += dot(query_t, dscores, 0, 0)
        total[1, :, :width] += dot(grad_t, probs.astype(BF), 0, 0)

    @pl.when(head < heads // 2)
    def _():
        out_a[...] = grads[...]

    @pl.when(head >= heads // 2)
    def _():
        out_b[...] = grads[...]

    @pl.when(head == heads - 1)
    def _():
        half = DH // 2
        mine = spot[ZB]
        near = pl.ds(pl.multiple_of(mine * half, half), half)
        far = pl.ds(pl.multiple_of((1 - mine) * half, half), half)
        for index, factor in enumerate((scaling, 1.0)):
            keep[index] = total[index, near, :] * factor
            send[index] = (total[index, far, :] * factor).astype(BF)


def attend(spot, kv, queries, out_grads, outputs, norms, later):
    seq = queries.shape[0]
    heads = queries.shape[1] // DH
    cols = pl.BlockSpec((seq, DH), lambda head: (0, head))
    full = lambda a: pl.BlockSpec(a.shape, lambda head: (0,) * len(a.shape))
    outs = [
        shape((seq, heads // 2 * DH)),
        shape((seq, heads // 2 * DH)),
        shape((2, DH // 2, seq)),
        shape((2, DH // 2, seq), F32),
    ]
    return call(
        attend_kernel,
        "attend",
        spot,
        (kv, queries, out_grads, outputs, norms),
        [full(kv), cols, cols, cols, full(norms)],
        outs,
        [
            pl.BlockSpec((seq, DH), lambda head: (0, jnp.minimum(head, heads // 2 - 1))),
            pl.BlockSpec((seq, DH), lambda head: (0, jnp.maximum(head - heads // 2, 0))),
            *[full(out) for out in outs[2:]],
        ],
        [
            pltpu.VMEM((DH, seq), BF),
            pltpu.VMEM((DH, seq), BF),
            pltpu.VMEM((2, DH, seq), F32),
            pltpu.VMEM((seq, DH), F32),
            pltpu.VMEM((seq, DH), BF),
        ],
        grid=(heads,),
        work=10**9,
        later=later,
    )


def middle_kernel(spot, keep, arrived, out, send):
    total = keep[...] + arrived[...].astype(F32)
    out[...] = total
    send[...] = total.astype(BF)


def middle(spot, keep, arrived, later, through):
    return call(
        middle_kernel,
        "kv_middle",
        spot,
        (keep, arrived),
        [VMEM] * 2,
        [shape(keep.shape, F32), shape(keep.shape)],
        [VMEM] * 2,
        later=later,
        through=through,
    )


def final_kv_kernel(spot, keep, arrived, early, far, out):
    total = keep[...] + arrived[...].astype(F32)
    start = early.shape[1]
    deep = start + far.shape[1]
    out[:, :start] = early[...]
    out[:, start:deep] = far[...]
    out[:, deep:] = total.reshape(out.shape[1] - deep, out.shape[0]).T.astype(BF)


def final_kv(spot, keep, arrived, early, far, later):
    return call(
        final_kv_kernel,
        "kv_final",
        spot,
        (keep, arrived, early, far),
        [VMEM] * 4,
        [shape((keep.shape[2], early.shape[1] + far.shape[1] + keep.shape[0] * keep.shape[1]))],
        [VMEM],
        later=later,
    )[0]


def offsets(pieces):
    starts, at = [], 0
    for piece in pieces:
        starts.append(at)
        at += piece.shape[1]
    return starts, at


AWAYS = (4, 3, -3, 2, -2, 1, -1, 0)


def load_rows(aways, z, pieces, held, sems):
    starts, total = offsets(pieces)
    skip = total - held.shape[1]
    rows = pieces[0].shape[0] // NZ
    copies = []
    for slot, away in enumerate(aways):
        row = pl.multiple_of(lax.rem(z + away + NZ, NZ) * rows, rows)
        for index, piece in enumerate(pieces):
            copies.append(
                pltpu.make_async_copy(
                    piece.at[pl.ds(row, rows), pl.ds(skip, piece.shape[1] - skip)],
                    held.at[
                        pl.ds(slot * rows, rows), pl.ds(starts[index], piece.shape[1] - skip)
                    ],
                    sems.at[slot, index],
                )
            )
    return copies


def early_kernel(spot, weights, *rest):
    pieces, (out, packed, held, sems) = rest[:3], rest[3:]
    rows = out.shape[1]

    @pl.when(pl.program_id(0) == 0)
    def _():
        run_copies(load_rows(AWAYS, spot[Z], pieces, held, sems))
        for slot, away in enumerate(AWAYS):
            row = pl.multiple_of(lax.rem(spot[Z] + away + NZ, NZ) * rows, rows)
            packed[pl.ds(row, rows), :] = held[slot * rows : (slot + 1) * rows, :]

    total = dot(held[...], weights[:, : held.shape[1]], 1, 1)
    out[...] = total.reshape(out.shape)


def early_parts(spot, weights, pieces, later):
    seq = pieces[0].shape[0]
    width, deep = weights.shape
    _, depth = offsets(pieces)
    wide = 512
    return call(
        early_kernel,
        "early_parts",
        spot,
        (weights, *pieces),
        [pl.BlockSpec((wide, deep), lambda step: (step, 0)), *[ANY] * 3],
        [shape((NZ, seq // NZ, width), F32), shape((seq, depth))],
        [
            pl.BlockSpec((NZ, seq // NZ, wide), lambda step: (0, 0, step)),
            pl.BlockSpec((seq, depth), lambda step: (0, 0)),
        ],
        [pltpu.VMEM((seq, depth), BF), pltpu.SemaphoreType.DMA((NZ, 3))],
        grid=(width // wide,),
        work=10**9,
        later=later,
    )


def first_kernel(spot, weights, weights_kv, base, late, up, down, held, sems):
    run_copies(load_rows(AWAYS[:1], spot[Z], (late,), held, sems))
    wide = up.shape[1]
    deep = weights.shape[1]
    for index, out in enumerate((up, down)):
        part = slice(index * wide, (index + 1) * wide)
        total = dot(held[:, :deep], weights[part, :], 1, 1)
        total += dot(held[:, deep:], weights_kv[:, part], 1, 0)
        out[...] = (base[0, :, part] + total).astype(BF)


def first_parts(spot, weights, weights_kv, base, late, deep):
    _, rows, width = base.shape
    depth = deep + weights_kv.shape[0]
    last = weights.shape[1] // deep - 1
    out = pl.BlockSpec((rows, width // 2), lambda step: (0, 0))
    return call(
        first_kernel,
        "first_parts",
        spot,
        (weights, weights_kv, base, late),
        [
            pl.BlockSpec((width, deep), lambda step: (0, last)),
            pl.BlockSpec(weights_kv.shape, lambda step: (0, 0)),
            pl.BlockSpec((1, rows, width), lambda step: (0, 0, 0)),
            ANY,
        ],
        [shape((rows, width // 2))] * 2,
        [out] * 2,
        [pltpu.VMEM((rows, depth), BF), pltpu.SemaphoreType.DMA((1, 1))],
        grid=(1,),
    )


def rest_kernel(spot, weights, weights_kv, base, late, out, held, sems):
    @pl.when(pl.program_id(0) == 0)
    def _():
        run_copies(load_rows(AWAYS[1:], spot[Z], (late,), held, sems))

    deep = weights.shape[1]
    total = dot(held[:, :deep], weights[...], 1, 1) + dot(held[:, deep:], weights_kv[...], 1, 0)
    out[...] = (base[1:] + total.reshape(out.shape)).astype(BF)


def rest_parts(spot, weights, weights_kv, base, late, deep, later):
    count, rows, width = base.shape
    depth = deep + weights_kv.shape[0]
    last = weights.shape[1] // deep - 1
    wide = 512
    return call(
        rest_kernel,
        "rest_parts",
        spot,
        (weights, weights_kv, base, late),
        [
            pl.BlockSpec((wide, deep), lambda step: (step, last)),
            pl.BlockSpec((depth - deep, wide), lambda step: (0, step)),
            pl.BlockSpec((count, rows, wide), lambda step: (0, 0, step)),
            ANY,
        ],
        [shape((count - 1, rows, width))],
        [pl.BlockSpec((count - 1, rows, wide), lambda step: (0, 0, step))],
        [pltpu.VMEM(((count - 1) * rows, depth), BF), pltpu.SemaphoreType.DMA((count - 1, 1))],
        grid=(width // wide,),
        work=10**9,
        later=later,
    )[0]


def ring_kernel(kind, spot, up, down, ups, downs, *outs):
    wide = up.shape[1]
    if kind == "first":
        for arrived, part, out, start in ((up, ups, outs[0], 0), (down, downs, outs[1], wide)):
            out[...] = part[0]
            cols = slice(start, start + wide)
            out[:, cols] = (part[0, :, cols].astype(F32) + arrived[...].astype(F32)).astype(BF)
    elif kind == "next":
        for arrived, part, out in ((up, ups, outs[0]), (down, downs, outs[1])):
            out[...] = (part[0].astype(F32) + arrived[...].astype(F32)).astype(BF)
    else:
        own, send = outs
        h = spot[H]
        rows = own.shape[0]
        for out, side in ((own, h), (send, 1 - h)):
            here = pl.ds(pl.multiple_of(side * rows, rows), rows)
            total = ups[0, here, :].astype(F32) + up[here, :].astype(F32) + down[here, :].astype(F32)
            out[...] = total.astype(BF)


def ring_step(kind, spot, up, down, parts, slots, later):
    _, rows, width = parts.shape
    whole = lambda a: pl.BlockSpec(a.shape, lambda step: (0,) * len(a.shape))
    term = [pl.BlockSpec((1, rows, width), lambda step, slot=slot: (slot, 0, 0)) for slot in slots]
    out = shape((rows // 2 if kind == "last" else rows, width))
    return call(
        functools.partial(ring_kernel, kind),
        "ring_step",
        spot,
        (up, down, parts, parts),
        [whole(up), whole(down), *term],
        [out] * 2,
        [whole(out)] * 2,
        grid=(1,),
        later=later,
    )


def wgrad_kernel(spot, *rest):
    blocks, (up, down), rest = rest[: NZ - 1], rest[NZ - 1 : NZ + 1], rest[NZ + 1 :]
    pieces, (out, done, held, lefts, sems, left_sems, last_sems) = rest[:2], rest[2:]
    z = spot[Z]
    rows = blocks[0].shape[2]
    places = (0, -1, 1, -2, 2, -3, 3)

    @pl.when(pl.program_id(0) == 0)
    def _():
        def place(away):
            return pl.ds(pl.multiple_of(lax.rem(z + away + NZ, NZ) * rows, rows), rows)

        copies = [
            pltpu.make_async_copy(piece, held.at[index], sems.at[index])
            for index, piece in enumerate(pieces)
        ]
        for index, (block, away) in enumerate(zip(blocks, places)):
            copies.append(
                pltpu.make_async_copy(
                    block, lefts.at[:, :, place(away), :], left_sems.at[index]
                )
            )
        for index, last in enumerate((up, down)):
            half = NX // 2
            copies.append(
                pltpu.make_async_copy(
                    last,
                    lefts.at[pl.ds(index * half, half), :, place(NZ // 2), :],
                    last_sems.at[index],
                )
            )
        run_copies(copies)

    done[...] = jnp.zeros_like(done)
    left = lefts[pl.program_id(0)]
    left = left.reshape(left.shape[0] * left.shape[1], left.shape[2])
    right = held[...].reshape(left.shape[0], held.shape[2])
    out[0] = dot(left, right, 0, 0).astype(out.dtype)


def wgrad_parts(spot, blocks, up, down, here, there, later):
    seq, depth = here.shape
    wide = blocks[0].shape[3]
    return call(
        wgrad_kernel,
        "wgrad_parts",
        spot,
        (*blocks, up, down, here, there),
        [ANY] * (NZ + 3),
        [shape((NX, wide, depth)), shape((8, DH), F32)],
        [
            pl.BlockSpec((1, wide, depth), lambda step: (step, 0, 0)),
            pl.BlockSpec((8, DH), lambda step: (0, 0)),
        ],
        [
            pltpu.VMEM((2, seq, depth), BF),
            pltpu.VMEM((NX, 2, seq, wide), BF),
            pltpu.SemaphoreType.DMA((2,)),
            pltpu.SemaphoreType.DMA((NZ - 1,)),
            pltpu.SemaphoreType.DMA((2,)),
        ],
        grid=(NX,),
        work=10**10,
        later=later,
    )


def wgrad_sum_kernel(spot, terms, own, own_kv, send):
    total = terms[0].astype(F32)
    for index in range(1, terms.shape[0]):
        total += terms[index].astype(F32)
    q_w = own.shape[1]
    own[...] = total[:, :q_w]
    own_kv[...] = total[:, 2 * q_w :]
    send[...] = total[:, q_w:].astype(BF)


def wgrad_sum(spot, terms, q_w, later):
    _, rows, depth = terms.shape
    return call(
        wgrad_sum_kernel,
        "wgrad_sum",
        spot,
        (terms,),
        [VMEM],
        [shape((rows, q_w), F32), shape((rows, depth - 2 * q_w), F32), shape((rows, depth - q_w))],
        [VMEM] * 3,
        later=later,
    )


def final_kernel(
    spot, mine, other, own, own_kv, arrived, out_tokens, out, out_k, out_v, turned
):
    h = spot[H]
    wide = mine.shape[1]
    out_tokens[:, pl.ds(pl.multiple_of(h * wide, wide), wide)] = mine[...]
    out_tokens[:, pl.ds(pl.multiple_of((1 - h) * wide, wide), wide)] = other[...]
    rows, q_w = own.shape
    kv_w = out_k.shape[0]
    near = pl.ds(pl.multiple_of(h * rows, rows), rows)
    far = pl.ds(pl.multiple_of((1 - h) * rows, rows), rows)
    out[near, :] = own[...]
    out[far, :] = arrived[:, :q_w].astype(F32)
    for cols, value in ((near, own_kv[...]), (far, arrived[:, q_w:].astype(F32))):
        turned[...] = value.T
        for index, to in enumerate((out_k, out_v)):
            start = pl.multiple_of((2 * index + h) * kv_w, kv_w)
            to[:, cols] = turned[pl.ds(start, kv_w), :]


def final(spot, mine, other, own, own_kv, arrived, kv_w):
    n_own, wide = mine.shape
    rows, q_w = own.shape
    return call(
        final_kernel,
        "final",
        spot,
        (mine, other, own, own_kv, arrived),
        [VMEM] * 5,
        [
            shape((n_own, 2 * wide)),
            shape((2 * rows, q_w), F32),
            *[shape((kv_w, 2 * rows), F32)] * 2,
        ],
        [VMEM] * 4,
        [pltpu.VMEM((own_kv.shape[1], rows), F32)],
    )


def body(
    tokens,
    queries,
    saved_keys,
    saved_values,
    outputs,
    out_grads,
    log_norms,
    w_query,
    w_key,
    w_value,
):
    t = lax.axis_index("tensor")
    d = lax.axis_index("dp")
    h = t % 2
    spot = jnp.stack([t // 2, h, d % 2, d // 4, t // 2 % 2]).astype(jnp.int32)
    kv_w = saved_keys.shape[1]
    q_w = queries.shape[1]
    n_own = tokens.shape[0]
    heads4 = [[4 * k + j for j in range(4)] for k in range(4)]
    ring_x = [[r + 4 * k for k in range(NX)] for r in range(4)]
    plane = [[r + 2 * k for k in range(8)] for r in range(2)]

    w_key, w_value = w_key.T, w_value.T
    own, side, core, both, kv = pack(spot, tokens, saved_keys.T, saved_values.T)
    side = swap_quad(side, 0, 1)
    core = swap_quad(core, 1, 0)
    both = swap_quad(both, 1, 1)
    kv = lax.all_to_all(kv, "tensor", 0, 0, axis_index_groups=heads4, tiled=True)
    quarter = tokens.shape[1] // 4
    block, start = token_block(spot, (own, side, core, both), quarter, [])
    up1, down1 = shift(block, "tensor", 2), shift(block, "tensor", -2)
    piece = quarter // 2
    row = start[0]
    w_send = jnp.concatenate(
        [
            lax.dynamic_slice_in_dim(w_query, row, piece, 0),
            *[lax.dynamic_slice_in_dim(w, row, piece, 1) for w in (w_key, w_value)],
        ]
    )
    w_side = swap(w_send, "tensor", 1)

    own_a, own_b, kv_send, kv_keep = attend(
        spot, kv, queries, out_grads, outputs, log_norms, [block]
    )
    w_side = again(spot, w_side, [up1, down1, own_a])
    far_a = swap(own_a, "tensor", 1)
    kv_z = swap(kv_send, "tensor", 2)
    up2, down2 = shift(up1, "tensor", 2), shift(down1, "tensor", -2)
    w_x = swap(w_side, "dp", 4)
    kv_keep, kv_send = middle(spot, kv_keep, kv_z, [up2, down2, far_a, w_x], [])
    kv_y = swap(kv_send, "tensor", 1)
    far_b = swap(own_b, "tensor", 1)
    up3, down3 = shift(up2, "tensor", 2), shift(down2, "tensor", -2)
    w_parts = [w_side, w_x] + [swap(value, "dp", 1) for value in (w_side, w_x)]
    weights, weights_kv = gather_weights(spot, w_query, w_key, w_value, w_parts, [kv_send])
    base, early = early_parts(spot, weights, [own_a, own_b, far_a], [])
    up4, down4 = halves(spot, up3, down3, [base])
    up4, down4 = shift(up4, "tensor", 2), shift(down4, "tensor", -2)
    here = final_kv(spot, kv_keep, kv_y, early, far_b, [base, up3, down3])
    there = swap(here, "dp", 1)

    up, down = first_parts(spot, weights, weights_kv, base, here, 2 * DH)
    up_next, down_next = shift(up, "tensor", 2), shift(down, "tensor", -2)
    parts = rest_parts(spot, weights, weights_kv, base, here, 2 * DH, [up])
    blocks = [block, up1, down1, up2, down2, up3, down3]
    terms, done = wgrad_parts(
        spot, blocks, up4, down4, here, there, [parts, up_next, down_next]
    )
    for kind, slots in (("first", (0, 1)), ("next", (2, 3)), ("next", (4, 5))):
        up, down = ring_step(kind, spot, up_next, down_next, parts, slots, [done])
        up_next, down_next = shift(up, "tensor", 2), shift(down, "tensor", -2)

    terms = terms.reshape(8, DH, terms.shape[2])
    terms = lax.all_to_all(terms, "dp", 0, 0, axis_index_groups=plane, tiled=True)
    w_own, w_own_kv, w_send = wgrad_sum(spot, terms, q_w, [up])
    w_other = swap(w_send, "tensor", 1)

    mine, other = ring_step("last", spot, up_next, down_next, parts, (6, 6), [w_send])
    other = swap(other, "tensor", 1)
    token_grads, query_wgrad, key_wgrad, value_wgrad = final(
        spot, mine, other, w_own, w_own_kv, w_other, kv_w
    )
    return token_grads, query_wgrad, key_wgrad.T, value_wgrad.T


def solution(mesh):
    in_specs = (
        P(("dp", "tensor"), None),
        P("dp", "tensor"),
        P("dp", "tensor"),
        P("dp", "tensor"),
        P("dp", "tensor"),
        P("dp", "tensor"),
        P("tensor", "dp"),
        P(None, "tensor"),
        P(None, "tensor"),
        P(None, "tensor"),
    )
    out_specs = (P(("dp", "tensor"), None), P("dp", "tensor"), P("dp", "tensor"), P("dp", "tensor"))
    return jax.shard_map(body, mesh=mesh, in_specs=in_specs, out_specs=out_specs, check_vma=False)
```

```python
import functools

import jax
import jax.numpy as jnp
from jax import lax
from jax.experimental import pallas as pl
from jax.experimental.pallas import tpu as pltpu
from jax.sharding import PartitionSpec as P

DH = 128
NZ = 8
NX = 4
TILE = 256
MIB = 2**20
BF = jnp.bfloat16
F32 = jnp.float32
ANY = pl.BlockSpec(memory_space=pl.ANY)
SMEM = pl.BlockSpec(memory_space=pltpu.SMEM)
VMEM = pl.BlockSpec(memory_space=pltpu.VMEM)
Z, H, C, X, ZB = range(5)


def shift(value, axis, step):
    size = lax.axis_size(axis)
    pairs = [(source, (source + step) % size) for source in range(size)]
    return lax.ppermute(value, axis, pairs)


def swap(value, axis, mask):
    pairs = [(source, source ^ mask) for source in range(lax.axis_size(axis))]
    return lax.ppermute(value, axis, pairs)


def swap_quad(value, core, side):
    tensor = lax.axis_size("tensor")
    size = lax.axis_size("dp") * tensor
    mask = core * tensor + side
    pairs = [(source, source ^ mask) for source in range(size)]
    return lax.ppermute(value, ("dp", "tensor"), pairs)


def dot(left, right, left_dim, right_dim):
    return lax.dot_general(
        left, right, (((left_dim,), (right_dim,)), ((), ())), preferred_element_type=F32
    )


def run_copies(copies):
    for copy in copies:
        copy.start()
    for copy in copies:
        copy.wait()


def call(
    kernel, name, spot, ins, specs, outs, out_specs, scratch=(), grid=(), work=0, later=(), through=(), vmem=20
):
    n_ins, n_later, n_through = 1 + len(ins), len(later), len(through)
    n_outs = len(outs)

    def whole(*refs):
        ins_end = n_ins + n_later + n_through
        kernel(*refs[:n_ins], *refs[ins_end : ins_end + n_outs], *refs[ins_end + n_outs + n_through :])

    return pl.pallas_call(
        whole,
        grid=grid,
        in_specs=[SMEM, *specs, *[ANY] * (n_later + n_through)],
        out_specs=[*out_specs, *[ANY] * n_through],
        out_shape=[*outs, *[shape(value.shape, value.dtype) for value in through]],
        input_output_aliases={
            n_ins + n_later + index: n_outs + index for index in range(n_through)
        },
        scratch_shapes=scratch,
        compiler_params=pltpu.CompilerParams(vmem_limit_bytes=vmem * MIB),
        cost_estimate=pl.CostEstimate(flops=work, bytes_accessed=0, transcendentals=0),
        name=name,
    )(spot, *ins, *later, *through)


def shape(dims, dtype=BF):
    return jax.ShapeDtypeStruct(tuple(dims), dtype)


def pack_kernel(spot, tokens, keys, values, own, side, core, both, kv):
    h, c = spot[H], spot[C]
    width = tokens.shape[1]
    kv_w = keys.shape[0]
    for index in range(kv.shape[0]):
        kv[index, :kv_w, :] = keys[...]
        kv[index, kv_w:, :] = values[...]
    for to, to_c, to_h in ((own, c, h), (side, c, 1 - h), (core, 1 - c, h), (both, 1 - c, 1 - h)):
        for part in range(NX):
            for half in range(2):
                start = part * (width // NX) + half * 4 * DH + to_c * 2 * DH + to_h * DH
                start = pl.multiple_of(start, DH)
                to[part, :, half * DH : (half + 1) * DH] = tokens[:, pl.ds(start, DH)]


def pack(spot, tokens, keys, values):
    part = shape((NX, tokens.shape[0], 2 * DH))
    kv = shape((4, 2 * keys.shape[0], keys.shape[1]))
    return call(
        pack_kernel,
        "pack",
        spot,
        (tokens, keys, values),
        [VMEM] * 3,
        [part] * 4 + [kv],
        [VMEM] * 5,
        vmem=64,
    )


def block_kernel(spot, own, side, core, both, w_query, w_key, w_value, out, w_send, sems):
    h = spot[H]
    rows = own.shape[1]
    kv_w = w_key.shape[0]
    piece = w_send.shape[0] - 2 * kv_w
    row = ((1 - h) * 2 + spot[C]) * (2 * piece) + lax.rem(spot[X], 2) * piece
    part = pl.ds(pl.multiple_of(row, piece), piece)
    copies = [
        pltpu.make_async_copy(source, w_send.at[pl.ds(start, size), :], sems.at[index])
        for index, (source, start, size) in enumerate(
            (
                (w_query.at[part, :], 0, piece),
                (w_key.at[:, part], piece, kv_w),
                (w_value.at[:, part], piece + kv_w, kv_w),
            )
        )
    ]
    for copy in copies:
        copy.start()
    near = pl.ds(pl.multiple_of(h * rows, rows), rows)
    far = pl.ds(pl.multiple_of((1 - h) * rows, rows), rows)
    out[:, 0, near, :] = own[...]
    out[:, 0, far, :] = side[...]
    out[:, 1, near, :] = core[...]
    out[:, 1, far, :] = both[...]
    for copy in copies:
        copy.wait()


def token_block(spot, parts, w_query, w_key, w_value):
    part, rows, wide = parts[0].shape
    w_rows = w_query.shape[0] // 8 + 2 * w_key.shape[0]
    return call(
        block_kernel,
        "token_block",
        spot,
        (*parts, w_query, w_key, w_value),
        [VMEM] * 4 + [ANY] * 3,
        [shape((part, 2, 2 * rows, wide)), shape((w_rows, w_query.shape[1]))],
        [VMEM, VMEM],
        [pltpu.SemaphoreType.DMA((3,))],
        vmem=64,
    )


def again_kernel(spot, value, out):
    out[...] = value[...]


def again(spot, value, later):
    return call(
        again_kernel, "again", spot, (value,), [VMEM], [shape(value.shape)], [VMEM], later=later
    )[0]


def halves_kernel(spot, up, down, out_up, out_down):
    out_up[...] = up[...]
    out_down[...] = down[...]


def halves(spot, up, down, later):
    part = (up.shape[0] // 2, *up.shape[1:])
    zeros = (0,) * (len(part) - 1)
    first = pl.BlockSpec(part, lambda step: (0, *zeros))
    return call(
        halves_kernel,
        "halves",
        spot,
        (up, down),
        [first, pl.BlockSpec(part, lambda step: (1, *zeros))],
        [shape(part)] * 2,
        [first] * 2,
        grid=(1,),
        later=later,
    )


def weights_kernel(spot, w_query, w_key, w_value, *rest):
    parts, (out, out_kv, sems) = rest[:4], rest[4:]
    h, c, side = spot[H], spot[C], lax.rem(spot[X], 2)
    half, q2 = out.shape
    q_w, kv_w = q2 // 2, w_key.shape[0]
    piece = parts[0].shape[0] - 2 * kv_w
    start = pl.multiple_of(h * half, half)
    near = [pl.ds(pl.multiple_of(kind * 2 * kv_w + h * kv_w, kv_w), kv_w) for kind in (0, 1)]
    far = [pl.ds(pl.multiple_of(kind * 2 * kv_w + (1 - h) * kv_w, kv_w), kv_w) for kind in (0, 1)]
    pairs = [
        (w_query.at[pl.ds(start, half), :], out.at[:, pl.ds(0, q_w)]),
        (w_key.at[:, pl.ds(start, half)], out_kv.at[near[0], :]),
        (w_value.at[:, pl.ds(start, half)], out_kv.at[near[1], :]),
    ]
    places = ((c, side), (c, 1 - side), (1 - c, side), (1 - c, 1 - side))
    for ref, (core, part) in zip(parts, places):
        row = pl.multiple_of(core * (half // 2) + part * piece, piece)
        pairs.append((ref.at[pl.ds(0, piece), :], out.at[pl.ds(row, piece), pl.ds(q_w, q_w)]))
        for kind in (0, 1):
            pairs.append(
                (
                    ref.at[pl.ds(piece + kind * kv_w, kv_w), :],
                    out_kv.at[far[kind], pl.ds(row, piece)],
                )
            )
    run_copies(
        [
            pltpu.make_async_copy(source, target, sems.at[index])
            for index, (source, target) in enumerate(pairs)
        ]
    )


def gather_weights(spot, w_query, w_key, w_value, parts, later):
    width, q_w = w_query.shape
    return call(
        weights_kernel,
        "gather_weights",
        spot,
        (w_query, w_key, w_value, *parts),
        [ANY] * 7,
        [shape((width // 2, 2 * q_w)), shape((4 * w_key.shape[0], width // 2))],
        [ANY] * 2,
        [pltpu.SemaphoreType.DMA((15,))],
        later=later,
    )


def attend_kernel(
    spot, kv, query, grad, output, norms, out_a, out_b, send, keep, keys, values, total, turned, grads
):
    head = pl.program_id(0)
    heads = pl.num_programs(0)
    scaling = DH ** (-0.5)
    seq = query.shape[0]
    part = kv.shape[1] // 2

    @pl.when(head == 0)
    def _():
        for index in range(kv.shape[0]):
            keys[index * part : (index + 1) * part, :] = kv[index, :part, :]
            values[index * part : (index + 1) * part, :] = kv[index, part:, :]
        total[...] = jnp.zeros_like(total)
        filler = jnp.zeros((DH - norms.shape[0], seq), F32)
        turned[...] = jnp.concatenate([norms[...], filler]).T

    which = lax.broadcasted_iota(jnp.int32, turned.shape, 1) == head
    norm = jnp.sum(jnp.where(which, turned[...], 0.0), axis=1, keepdims=True)
    for tile in range(seq // TILE):
        rows = slice(tile * TILE, (tile + 1) * TILE)
        width = (tile + 1) * TILE
        query_t, grad_t = query[rows, :], grad[rows, :]
        scores = dot(query_t, keys[:, :width], 1, 0)
        probs = jnp.exp(scores * scaling - norm[rows])
        row_ids = lax.broadcasted_iota(jnp.int32, probs.shape, 0) + tile * TILE
        col_ids = lax.broadcasted_iota(jnp.int32, probs.shape, 1)
        probs = jnp.where(col_ids <= row_ids, probs, 0.0)
        delta = jnp.sum(grad_t.astype(F32) * output[rows, :].astype(F32), axis=1, keepdims=True)
        dprobs = dot(grad_t, values[:, :width], 1, 0)
        dscores = (probs * (dprobs - delta)).astype(BF)
        grads[rows, :] = (dot(dscores, keys[:, :width], 1, 1) * scaling).astype(BF)
        total[0, :, :width] += dot(query_t, dscores, 0, 0)
        total[1, :, :width] += dot(grad_t, probs.astype(BF), 0, 0)

    @pl.when(head < heads // 2)
    def _():
        out_a[...] = grads[...]

    @pl.when(head >= heads // 2)
    def _():
        out_b[...] = grads[...]

    @pl.when(head == heads - 1)
    def _():
        half = DH // 2
        mine = spot[ZB]
        near = pl.ds(pl.multiple_of(mine * half, half), half)
        far = pl.ds(pl.multiple_of((1 - mine) * half, half), half)
        for index, factor in enumerate((scaling, 1.0)):
            keep[index] = total[index, near, :] * factor
            send[index] = (total[index, far, :] * factor).astype(BF)


def attend(spot, kv, queries, out_grads, outputs, norms, later):
    seq = queries.shape[0]
    heads = queries.shape[1] // DH
    cols = pl.BlockSpec((seq, DH), lambda head: (0, head))
    full = lambda a: pl.BlockSpec(a.shape, lambda head: (0,) * len(a.shape))
    outs = [
        shape((seq, heads // 2 * DH)),
        shape((seq, heads // 2 * DH)),
        shape((2, DH // 2, seq)),
        shape((2, DH // 2, seq), F32),
    ]
    return call(
        attend_kernel,
        "attend",
        spot,
        (kv, queries, out_grads, outputs, norms),
        [full(kv), cols, cols, cols, full(norms)],
        outs,
        [
            pl.BlockSpec((seq, DH), lambda head: (0, jnp.minimum(head, heads // 2 - 1))),
            pl.BlockSpec((seq, DH), lambda head: (0, jnp.maximum(head - heads // 2, 0))),
            *[full(out) for out in outs[2:]],
        ],
        [
            pltpu.VMEM((DH, seq), BF),
            pltpu.VMEM((DH, seq), BF),
            pltpu.VMEM((2, DH, seq), F32),
            pltpu.VMEM((seq, DH), F32),
            pltpu.VMEM((seq, DH), BF),
        ],
        grid=(heads,),
        work=10**9,
        later=later,
    )


def middle_kernel(spot, keep, arrived, out, send):
    total = keep[...] + arrived[...].astype(F32)
    out[...] = total
    send[...] = total.astype(BF)


def middle(spot, keep, arrived, later, through):
    return call(
        middle_kernel,
        "kv_middle",
        spot,
        (keep, arrived),
        [VMEM] * 2,
        [shape(keep.shape, F32), shape(keep.shape)],
        [VMEM] * 2,
        later=later,
        through=through,
    )


def final_kv_kernel(spot, keep, arrived, early, far, out):
    total = keep[...] + arrived[...].astype(F32)
    start = early.shape[1]
    deep = start + far.shape[1]
    out[:, :start] = early[...]
    out[:, start:deep] = far[...]
    out[:, deep:] = total.reshape(out.shape[1] - deep, out.shape[0]).T.astype(BF)


def final_kv(spot, keep, arrived, early, far, later):
    return call(
        final_kv_kernel,
        "kv_final",
        spot,
        (keep, arrived, early, far),
        [VMEM] * 4,
        [shape((keep.shape[2], early.shape[1] + far.shape[1] + keep.shape[0] * keep.shape[1]))],
        [VMEM],
        later=later,
    )[0]


def offsets(pieces):
    starts, at = [], 0
    for piece in pieces:
        starts.append(at)
        at += piece.shape[1]
    return starts, at


AWAYS = (4, 3, -3, 2, -2, 1, -1, 0)


def load_rows(aways, z, pieces, held, sems):
    starts, total = offsets(pieces)
    skip = total - held.shape[1]
    rows = pieces[0].shape[0] // NZ
    copies = []
    for slot, away in enumerate(aways):
        row = pl.multiple_of(lax.rem(z + away + NZ, NZ) * rows, rows)
        for index, piece in enumerate(pieces):
            copies.append(
                pltpu.make_async_copy(
                    piece.at[pl.ds(row, rows), pl.ds(skip, piece.shape[1] - skip)],
                    held.at[
                        pl.ds(slot * rows, rows), pl.ds(starts[index], piece.shape[1] - skip)
                    ],
                    sems.at[slot, index],
                )
            )
    return copies


def early_kernel(spot, weights, *rest):
    pieces, (out, packed, held, sems) = rest[:3], rest[3:]
    rows = out.shape[1]

    @pl.when(pl.program_id(0) == 0)
    def _():
        run_copies(load_rows(AWAYS, spot[Z], pieces, held, sems))
        for slot, away in enumerate(AWAYS):
            row = pl.multiple_of(lax.rem(spot[Z] + away + NZ, NZ) * rows, rows)
            packed[pl.ds(row, rows), :] = held[slot * rows : (slot + 1) * rows, :]

    total = dot(held[...], weights[:, : held.shape[1]], 1, 1)
    out[...] = total.reshape(out.shape)


def early_parts(spot, weights, pieces, later):
    seq = pieces[0].shape[0]
    width, deep = weights.shape
    _, depth = offsets(pieces)
    wide = 512
    return call(
        early_kernel,
        "early_parts",
        spot,
        (weights, *pieces),
        [pl.BlockSpec((wide, deep), lambda step: (step, 0)), *[ANY] * 3],
        [shape((NZ, seq // NZ, width), F32), shape((seq, depth))],
        [
            pl.BlockSpec((NZ, seq // NZ, wide), lambda step: (0, 0, step)),
            pl.BlockSpec((seq, depth), lambda step: (0, 0)),
        ],
        [pltpu.VMEM((seq, depth), BF), pltpu.SemaphoreType.DMA((NZ, 3))],
        grid=(width // wide,),
        work=10**9,
        later=later,
    )


def first_kernel(spot, weights, weights_kv, base, late, up, down, held, sems):
    run_copies(load_rows(AWAYS[:1], spot[Z], (late,), held, sems))
    wide = up.shape[1]
    deep = weights.shape[1]
    for index, out in enumerate((up, down)):
        part = slice(index * wide, (index + 1) * wide)
        total = dot(held[:, :deep], weights[part, :], 1, 1)
        total += dot(held[:, deep:], weights_kv[:, part], 1, 0)
        out[...] = (base[0, :, part] + total).astype(BF)


def first_parts(spot, weights, weights_kv, base, late, deep):
    _, rows, width = base.shape
    depth = deep + weights_kv.shape[0]
    last = weights.shape[1] // deep - 1
    out = pl.BlockSpec((rows, width // 2), lambda step: (0, 0))
    return call(
        first_kernel,
        "first_parts",
        spot,
        (weights, weights_kv, base, late),
        [
            pl.BlockSpec((width, deep), lambda step: (0, last)),
            pl.BlockSpec(weights_kv.shape, lambda step: (0, 0)),
            pl.BlockSpec((1, rows, width), lambda step: (0, 0, 0)),
            ANY,
        ],
        [shape((rows, width // 2))] * 2,
        [out] * 2,
        [pltpu.VMEM((rows, depth), BF), pltpu.SemaphoreType.DMA((1, 1))],
        grid=(1,),
    )


def rest_kernel(spot, weights, weights_kv, base, late, out, held, sems):
    @pl.when(pl.program_id(0) == 0)
    def _():
        run_copies(load_rows(AWAYS[1:], spot[Z], (late,), held, sems))

    deep = weights.shape[1]
    total = dot(held[:, :deep], weights[...], 1, 1) + dot(held[:, deep:], weights_kv[...], 1, 0)
    out[...] = (base[1:] + total.reshape(out.shape)).astype(BF)


def rest_parts(spot, weights, weights_kv, base, late, deep, later):
    count, rows, width = base.shape
    depth = deep + weights_kv.shape[0]
    last = weights.shape[1] // deep - 1
    wide = 512
    return call(
        rest_kernel,
        "rest_parts",
        spot,
        (weights, weights_kv, base, late),
        [
            pl.BlockSpec((wide, deep), lambda step: (step, last)),
            pl.BlockSpec((depth - deep, wide), lambda step: (0, step)),
            pl.BlockSpec((count, rows, wide), lambda step: (0, 0, step)),
            ANY,
        ],
        [shape((count - 1, rows, width))],
        [pl.BlockSpec((count - 1, rows, wide), lambda step: (0, 0, step))],
        [pltpu.VMEM(((count - 1) * rows, depth), BF), pltpu.SemaphoreType.DMA((count - 1, 1))],
        grid=(width // wide,),
        work=10**9,
        later=later,
    )[0]


def ring_kernel(kind, spot, up, down, ups, downs, *outs):
    wide = up.shape[1]
    if kind == "first":
        for arrived, part, out, start in ((up, ups, outs[0], 0), (down, downs, outs[1], wide)):
            out[...] = part[0]
            cols = slice(start, start + wide)
            out[:, cols] = (part[0, :, cols].astype(F32) + arrived[...].astype(F32)).astype(BF)
    elif kind == "next":
        for arrived, part, out in ((up, ups, outs[0]), (down, downs, outs[1])):
            out[...] = (part[0].astype(F32) + arrived[...].astype(F32)).astype(BF)
    else:
        own, send = outs
        h = spot[H]
        rows = own.shape[0]
        for out, side in ((own, h), (send, 1 - h)):
            here = pl.ds(pl.multiple_of(side * rows, rows), rows)
            total = ups[0, here, :].astype(F32) + up[here, :].astype(F32) + down[here, :].astype(F32)
            out[...] = total.astype(BF)


def ring_step(kind, spot, up, down, parts, slots, later):
    _, rows, width = parts.shape
    whole = lambda a: pl.BlockSpec(a.shape, lambda step: (0,) * len(a.shape))
    term = [pl.BlockSpec((1, rows, width), lambda step, slot=slot: (slot, 0, 0)) for slot in slots]
    out = shape((rows // 2 if kind == "last" else rows, width))
    return call(
        functools.partial(ring_kernel, kind),
        "ring_step",
        spot,
        (up, down, parts, parts),
        [whole(up), whole(down), *term],
        [out] * 2,
        [whole(out)] * 2,
        grid=(1,),
        later=later,
    )


def wgrad_kernel(spot, *rest):
    blocks, (up, down), rest = rest[: NZ - 1], rest[NZ - 1 : NZ + 1], rest[NZ + 1 :]
    pieces, (out, done, held, lefts, sems, left_sems, last_sems) = rest[:2], rest[2:]
    z = spot[Z]
    rows = blocks[0].shape[2]
    places = (0, -1, 1, -2, 2, -3, 3)

    @pl.when(pl.program_id(0) == 0)
    def _():
        def place(away):
            return pl.ds(pl.multiple_of(lax.rem(z + away + NZ, NZ) * rows, rows), rows)

        copies = [
            pltpu.make_async_copy(piece, held.at[index], sems.at[index])
            for index, piece in enumerate(pieces)
        ]
        for index, (block, away) in enumerate(zip(blocks, places)):
            copies.append(
                pltpu.make_async_copy(
                    block, lefts.at[:, :, place(away), :], left_sems.at[index]
                )
            )
        for index, last in enumerate((up, down)):
            half = NX // 2
            copies.append(
                pltpu.make_async_copy(
                    last,
                    lefts.at[pl.ds(index * half, half), :, place(NZ // 2), :],
                    last_sems.at[index],
                )
            )
        run_copies(copies)

    done[...] = jnp.zeros_like(done)
    left = lefts[pl.program_id(0)]
    left = left.reshape(left.shape[0] * left.shape[1], left.shape[2])
    right = held[...].reshape(left.shape[0], held.shape[2])
    out[0] = dot(left, right, 0, 0).astype(out.dtype)


def wgrad_parts(spot, blocks, up, down, here, there, later):
    seq, depth = here.shape
    wide = blocks[0].shape[3]
    return call(
        wgrad_kernel,
        "wgrad_parts",
        spot,
        (*blocks, up, down, here, there),
        [ANY] * (NZ + 3),
        [shape((NX, wide, depth)), shape((8, DH), F32)],
        [
            pl.BlockSpec((1, wide, depth), lambda step: (step, 0, 0)),
            pl.BlockSpec((8, DH), lambda step: (0, 0)),
        ],
        [
            pltpu.VMEM((2, seq, depth), BF),
            pltpu.VMEM((NX, 2, seq, wide), BF),
            pltpu.SemaphoreType.DMA((2,)),
            pltpu.SemaphoreType.DMA((NZ - 1,)),
            pltpu.SemaphoreType.DMA((2,)),
        ],
        grid=(NX,),
        work=10**10,
        later=later,
    )


def wgrad_sum_kernel(spot, terms, own, own_kv, send):
    total = terms[0].astype(F32)
    for index in range(1, terms.shape[0]):
        total += terms[index].astype(F32)
    q_w = own.shape[1]
    own[...] = total[:, :q_w]
    own_kv[...] = total[:, 2 * q_w :]
    send[...] = total[:, q_w:].astype(BF)


def wgrad_sum(spot, terms, q_w, later):
    _, rows, depth = terms.shape
    return call(
        wgrad_sum_kernel,
        "wgrad_sum",
        spot,
        (terms,),
        [VMEM],
        [shape((rows, q_w), F32), shape((rows, depth - 2 * q_w), F32), shape((rows, depth - q_w))],
        [VMEM] * 3,
        later=later,
    )


def final_kernel(
    spot, mine, other, own, own_kv, arrived, out_tokens, out, out_k, out_v, turned
):
    h = spot[H]
    wide = mine.shape[1]
    out_tokens[:, pl.ds(pl.multiple_of(h * wide, wide), wide)] = mine[...]
    out_tokens[:, pl.ds(pl.multiple_of((1 - h) * wide, wide), wide)] = other[...]
    rows, q_w = own.shape
    kv_w = out_k.shape[0]
    near = pl.ds(pl.multiple_of(h * rows, rows), rows)
    far = pl.ds(pl.multiple_of((1 - h) * rows, rows), rows)
    out[near, :] = own[...]
    out[far, :] = arrived[:, :q_w].astype(F32)
    for cols, value in ((near, own_kv[...]), (far, arrived[:, q_w:].astype(F32))):
        turned[...] = value.T
        for index, to in enumerate((out_k, out_v)):
            start = pl.multiple_of((2 * index + h) * kv_w, kv_w)
            to[:, cols] = turned[pl.ds(start, kv_w), :]


def final(spot, mine, other, own, own_kv, arrived, kv_w):
    n_own, wide = mine.shape
    rows, q_w = own.shape
    return call(
        final_kernel,
        "final",
        spot,
        (mine, other, own, own_kv, arrived),
        [VMEM] * 5,
        [
            shape((n_own, 2 * wide)),
            shape((2 * rows, q_w), F32),
            *[shape((kv_w, 2 * rows), F32)] * 2,
        ],
        [VMEM] * 4,
        [pltpu.VMEM((own_kv.shape[1], rows), F32)],
    )


def body(
    tokens,
    queries,
    saved_keys,
    saved_values,
    outputs,
    out_grads,
    log_norms,
    w_query,
    w_key,
    w_value,
):
    t = lax.axis_index("tensor")
    d = lax.axis_index("dp")
    h = t % 2
    spot = jnp.stack([t // 2, h, d % 2, d // 4, t // 2 % 2]).astype(jnp.int32)
    kv_w = saved_keys.shape[1]
    q_w = queries.shape[1]
    n_own = tokens.shape[0]
    heads4 = [[4 * k + j for j in range(4)] for k in range(4)]
    ring_x = [[r + 4 * k for k in range(NX)] for r in range(4)]
    plane = [[r + 2 * k for k in range(8)] for r in range(2)]

    w_key, w_value = w_key.T, w_value.T
    own, side, core, both, kv = pack(spot, tokens, saved_keys.T, saved_values.T)
    side = swap_quad(side, 0, 1)
    core = swap_quad(core, 1, 0)
    both = swap_quad(both, 1, 1)
    kv = lax.all_to_all(kv, "tensor", 0, 0, axis_index_groups=heads4, tiled=True)
    block, w_send = token_block(spot, (own, side, core, both), w_query, w_key, w_value)
    w_side = swap(w_send, "tensor", 1)
    up1, down1 = shift(block, "tensor", 2), shift(block, "tensor", -2)
    own_a, own_b, kv_send, kv_keep = attend(
        spot, kv, queries, out_grads, outputs, log_norms, [block]
    )
    w_side = again(spot, w_side, [up1, down1, own_a])
    far_a = swap(own_a, "tensor", 1)
    kv_z = swap(kv_send, "tensor", 2)
    up2, down2 = shift(up1, "tensor", 2), shift(down1, "tensor", -2)
    w_x = swap(w_side, "dp", 4)
    kv_keep, kv_send = middle(spot, kv_keep, kv_z, [up2, down2, far_a, w_x], [])
    kv_y = swap(kv_send, "tensor", 1)
    far_b = swap(own_b, "tensor", 1)
    up3, down3 = shift(up2, "tensor", 2), shift(down2, "tensor", -2)
    w_parts = [w_side, w_x] + [swap(value, "dp", 1) for value in (w_side, w_x)]
    weights, weights_kv = gather_weights(spot, w_query, w_key, w_value, w_parts, [kv_send])
    base, early = early_parts(spot, weights, [own_a, own_b, far_a], [])
    up4, down4 = halves(spot, up3, down3, [base])
    up4, down4 = shift(up4, "tensor", 2), shift(down4, "tensor", -2)
    here = final_kv(spot, kv_keep, kv_y, early, far_b, [base, up3, down3])
    there = swap(here, "dp", 1)

    up, down = first_parts(spot, weights, weights_kv, base, here, 2 * DH)
    up_next, down_next = shift(up, "tensor", 2), shift(down, "tensor", -2)
    parts = rest_parts(spot, weights, weights_kv, base, here, 2 * DH, [up])
    blocks = [block, up1, down1, up2, down2, up3, down3]
    terms, done = wgrad_parts(
        spot, blocks, up4, down4, here, there, [parts, up_next, down_next]
    )
    for kind, slots in (("first", (0, 1)), ("next", (2, 3)), ("next", (4, 5))):
        up, down = ring_step(kind, spot, up_next, down_next, parts, slots, [done])
        up_next, down_next = shift(up, "tensor", 2), shift(down, "tensor", -2)

    terms = terms.reshape(8, DH, terms.shape[2])
    terms = lax.all_to_all(terms, "dp", 0, 0, axis_index_groups=plane, tiled=True)
    w_own, w_own_kv, w_send = wgrad_sum(spot, terms, q_w, [up])
    w_other = swap(w_send, "tensor", 1)

    mine, other = ring_step("last", spot, up_next, down_next, parts, (6, 6), [w_send])
    other = swap(other, "tensor", 1)
    token_grads, query_wgrad, key_wgrad, value_wgrad = final(
        spot, mine, other, w_own, w_own_kv, w_other, kv_w
    )
    return token_grads, query_wgrad, key_wgrad.T, value_wgrad.T


def solution(mesh):
    in_specs = (
        P(("dp", "tensor"), None),
        P("dp", "tensor"),
        P("dp", "tensor"),
        P("dp", "tensor"),
        P("dp", "tensor"),
        P("dp", "tensor"),
        P("tensor", "dp"),
        P(None, "tensor"),
        P(None, "tensor"),
        P(None, "tensor"),
    )
    out_specs = (P(("dp", "tensor"), None), P("dp", "tensor"), P("dp", "tensor"), P("dp", "tensor"))
    return jax.shard_map(body, mesh=mesh, in_specs=in_specs, out_specs=out_specs, check_vma=False)
```

```python
import functools

import jax
import jax.numpy as jnp
from jax import lax
from jax.experimental import pallas as pl
from jax.experimental.pallas import tpu as pltpu
from jax.sharding import PartitionSpec as P

DH = 128
NZ = 8
NX = 4
TILE = 256
MIB = 2**20
BF = jnp.bfloat16
F32 = jnp.float32
ANY = pl.BlockSpec(memory_space=pl.ANY)
SMEM = pl.BlockSpec(memory_space=pltpu.SMEM)
VMEM = pl.BlockSpec(memory_space=pltpu.VMEM)
Z, H, C, X, ZB = range(5)


def shift(value, axis, step):
    size = lax.axis_size(axis)
    pairs = [(source, (source + step) % size) for source in range(size)]
    return lax.ppermute(value, axis, pairs)


def swap(value, axis, mask):
    pairs = [(source, source ^ mask) for source in range(lax.axis_size(axis))]
    return lax.ppermute(value, axis, pairs)


def swap_quad(value, core, side):
    tensor = lax.axis_size("tensor")
    size = lax.axis_size("dp") * tensor
    mask = core * tensor + side
    pairs = [(source, source ^ mask) for source in range(size)]
    return lax.ppermute(value, ("dp", "tensor"), pairs)


def dot(left, right, left_dim, right_dim):
    return lax.dot_general(
        left, right, (((left_dim,), (right_dim,)), ((), ())), preferred_element_type=F32
    )


def run_copies(copies):
    for copy in copies:
        copy.start()
    for copy in copies:
        copy.wait()


def call(
    kernel, name, spot, ins, specs, outs, out_specs, scratch=(), grid=(), work=0, later=(), through=(), vmem=20
):
    n_ins, n_later, n_through = 1 + len(ins), len(later), len(through)
    n_outs = len(outs)

    def whole(*refs):
        ins_end = n_ins + n_later + n_through
        kernel(*refs[:n_ins], *refs[ins_end : ins_end + n_outs], *refs[ins_end + n_outs + n_through :])

    return pl.pallas_call(
        whole,
        grid=grid,
        in_specs=[SMEM, *specs, *[ANY] * (n_later + n_through)],
        out_specs=[*out_specs, *[ANY] * n_through],
        out_shape=[*outs, *[shape(value.shape, value.dtype) for value in through]],
        input_output_aliases={
            n_ins + n_later + index: n_outs + index for index in range(n_through)
        },
        scratch_shapes=scratch,
        compiler_params=pltpu.CompilerParams(vmem_limit_bytes=vmem * MIB),
        cost_estimate=pl.CostEstimate(flops=work, bytes_accessed=0, transcendentals=0),
        name=name,
    )(spot, *ins, *later, *through)


def shape(dims, dtype=BF):
    return jax.ShapeDtypeStruct(tuple(dims), dtype)


def pack_kernel(spot, tokens, keys, values, own, side, core, both, kv):
    h, c = spot[H], spot[C]
    width = tokens.shape[1]
    kv_w = keys.shape[0]
    for index in range(kv.shape[0]):
        kv[index, :kv_w, :] = keys[...]
        kv[index, kv_w:, :] = values[...]
    for to, to_c, to_h in ((own, c, h), (side, c, 1 - h), (core, 1 - c, h), (both, 1 - c, 1 - h)):
        for part in range(NX):
            for half in range(2):
                start = part * (width // NX) + half * 4 * DH + to_c * 2 * DH + to_h * DH
                start = pl.multiple_of(start, DH)
                to[part, :, half * DH : (half + 1) * DH] = tokens[:, pl.ds(start, DH)]


def pack(spot, tokens, keys, values):
    part = shape((NX, tokens.shape[0], 2 * DH))
    kv = shape((4, 2 * keys.shape[0], keys.shape[1]))
    return call(
        pack_kernel,
        "pack",
        spot,
        (tokens, keys, values),
        [VMEM] * 3,
        [part] * 4 + [kv],
        [VMEM] * 5,
        vmem=64,
    )


def block_kernel(
    spot, own, side, core, both, w_query, w_key, w_value, out, w_send, done, sems
):
    h = spot[H]
    rows = own.shape[1]
    kv_w = w_key.shape[0]
    piece = w_send.shape[0] - 2 * kv_w
    row = ((1 - h) * 2 + spot[C]) * (2 * piece) + lax.rem(spot[X], 2) * piece
    part = pl.ds(pl.multiple_of(row, piece), piece)
    copies = [
        pltpu.make_async_copy(source, w_send.at[pl.ds(start, size), :], sems.at[index])
        for index, (source, start, size) in enumerate(
            (
                (w_query.at[part, :], 0, piece),
                (w_key.at[:, part], piece, kv_w),
                (w_value.at[:, part], piece + kv_w, kv_w),
            )
        )
    ]
    for copy in copies:
        copy.start()
    near = pl.ds(pl.multiple_of(h * rows, rows), rows)
    far = pl.ds(pl.multiple_of((1 - h) * rows, rows), rows)
    out[:, 0, near, :] = own[...]
    out[:, 0, far, :] = side[...]
    out[:, 1, near, :] = core[...]
    out[:, 1, far, :] = both[...]
    done[...] = jnp.zeros_like(done)
    for copy in copies:
        copy.wait()


def token_block(spot, parts, w_query, w_key, w_value):
    part, rows, wide = parts[0].shape
    w_rows = w_query.shape[0] // 8 + 2 * w_key.shape[0]
    return call(
        block_kernel,
        "token_block",
        spot,
        (*parts, w_query, w_key, w_value),
        [VMEM] * 4 + [ANY] * 3,
        [
            shape((part, 2, 2 * rows, wide)),
            shape((w_rows, w_query.shape[1])),
            shape((8, DH), F32),
        ],
        [VMEM] * 3,
        [pltpu.SemaphoreType.DMA((3,))],
        vmem=64,
    )


def again_kernel(spot, value, out):
    out[...] = value[...]


def again(spot, value, later):
    return call(
        again_kernel, "again", spot, (value,), [VMEM], [shape(value.shape)], [VMEM], later=later
    )[0]


def halves_kernel(spot, up, down, out_up, out_down):
    out_up[...] = up[...]
    out_down[...] = down[...]


def halves(spot, up, down, later):
    part = (up.shape[0] // 2, *up.shape[1:])
    zeros = (0,) * (len(part) - 1)
    first = pl.BlockSpec(part, lambda step: (0, *zeros))
    return call(
        halves_kernel,
        "halves",
        spot,
        (up, down),
        [first, pl.BlockSpec(part, lambda step: (1, *zeros))],
        [shape(part)] * 2,
        [first] * 2,
        grid=(1,),
        later=later,
    )


def weights_kernel(spot, w_query, w_key, w_value, *rest):
    parts, (out, out_kv, sems) = rest[:4], rest[4:]
    h, c, side = spot[H], spot[C], lax.rem(spot[X], 2)
    half, q2 = out.shape
    q_w, kv_w = q2 // 2, w_key.shape[0]
    piece = parts[0].shape[0] - 2 * kv_w
    start = pl.multiple_of(h * half, half)
    near = [pl.ds(pl.multiple_of(kind * 2 * kv_w + h * kv_w, kv_w), kv_w) for kind in (0, 1)]
    far = [pl.ds(pl.multiple_of(kind * 2 * kv_w + (1 - h) * kv_w, kv_w), kv_w) for kind in (0, 1)]
    pairs = [
        (w_query.at[pl.ds(start, half), :], out.at[:, pl.ds(0, q_w)]),
        (w_key.at[:, pl.ds(start, half)], out_kv.at[near[0], :]),
        (w_value.at[:, pl.ds(start, half)], out_kv.at[near[1], :]),
    ]
    places = ((c, side), (c, 1 - side), (1 - c, side), (1 - c, 1 - side))
    for ref, (core, part) in zip(parts, places):
        row = pl.multiple_of(core * (half // 2) + part * piece, piece)
        pairs.append((ref.at[pl.ds(0, piece), :], out.at[pl.ds(row, piece), pl.ds(q_w, q_w)]))
        for kind in (0, 1):
            pairs.append(
                (
                    ref.at[pl.ds(piece + kind * kv_w, kv_w), :],
                    out_kv.at[far[kind], pl.ds(row, piece)],
                )
            )
    run_copies(
        [
            pltpu.make_async_copy(source, target, sems.at[index])
            for index, (source, target) in enumerate(pairs)
        ]
    )


def gather_weights(spot, w_query, w_key, w_value, parts, later):
    width, q_w = w_query.shape
    return call(
        weights_kernel,
        "gather_weights",
        spot,
        (w_query, w_key, w_value, *parts),
        [ANY] * 7,
        [shape((width // 2, 2 * q_w)), shape((4 * w_key.shape[0], width // 2))],
        [ANY] * 2,
        [pltpu.SemaphoreType.DMA((15,))],
        later=later,
    )


def attend_kernel(
    spot, kv, query, grad, output, norms, out_a, out_b, send, keep, keys, values, total, turned, grads
):
    head = pl.program_id(0)
    heads = pl.num_programs(0)
    scaling = DH ** (-0.5)
    seq = query.shape[0]
    part = kv.shape[1] // 2

    @pl.when(head == 0)
    def _():
        for index in range(kv.shape[0]):
            keys[index * part : (index + 1) * part, :] = kv[index, :part, :]
            values[index * part : (index + 1) * part, :] = kv[index, part:, :]
        total[...] = jnp.zeros_like(total)
        filler = jnp.zeros((DH - norms.shape[0], seq), F32)
        turned[...] = jnp.concatenate([norms[...], filler]).T

    which = lax.broadcasted_iota(jnp.int32, turned.shape, 1) == head
    norm = jnp.sum(jnp.where(which, turned[...], 0.0), axis=1, keepdims=True)
    for tile in range(seq // TILE):
        rows = slice(tile * TILE, (tile + 1) * TILE)
        width = (tile + 1) * TILE
        query_t, grad_t = query[rows, :], grad[rows, :]
        scores = dot(query_t, keys[:, :width], 1, 0)
        probs = jnp.exp(scores * scaling - norm[rows])
        row_ids = lax.broadcasted_iota(jnp.int32, probs.shape, 0) + tile * TILE
        col_ids = lax.broadcasted_iota(jnp.int32, probs.shape, 1)
        probs = jnp.where(col_ids <= row_ids, probs, 0.0)
        delta = jnp.sum(grad_t.astype(F32) * output[rows, :].astype(F32), axis=1, keepdims=True)
        dprobs = dot(grad_t, values[:, :width], 1, 0)
        dscores = (probs * (dprobs - delta)).astype(BF)
        grads[rows, :] = (dot(dscores, keys[:, :width], 1, 1) * scaling).astype(BF)
        total[0, :, :width] += dot(query_t, dscores, 0, 0)
        total[1, :, :width] += dot(grad_t, probs.astype(BF), 0, 0)

    @pl.when(head < heads // 2)
    def _():
        out_a[...] = grads[...]

    @pl.when(head >= heads // 2)
    def _():
        out_b[...] = grads[...]

    @pl.when(head == heads - 1)
    def _():
        half = DH // 2
        mine = spot[ZB]
        near = pl.ds(pl.multiple_of(mine * half, half), half)
        far = pl.ds(pl.multiple_of((1 - mine) * half, half), half)
        for index, factor in enumerate((scaling, 1.0)):
            keep[index] = total[index, near, :] * factor
            send[index] = (total[index, far, :] * factor).astype(BF)


def attend(spot, kv, queries, out_grads, outputs, norms, later):
    seq = queries.shape[0]
    heads = queries.shape[1] // DH
    cols = pl.BlockSpec((seq, DH), lambda head: (0, head))
    full = lambda a: pl.BlockSpec(a.shape, lambda head: (0,) * len(a.shape))
    outs = [
        shape((seq, heads // 2 * DH)),
        shape((seq, heads // 2 * DH)),
        shape((2, DH // 2, seq)),
        shape((2, DH // 2, seq), F32),
    ]
    return call(
        attend_kernel,
        "attend",
        spot,
        (kv, queries, out_grads, outputs, norms),
        [full(kv), cols, cols, cols, full(norms)],
        outs,
        [
            pl.BlockSpec((seq, DH), lambda head: (0, jnp.minimum(head, heads // 2 - 1))),
            pl.BlockSpec((seq, DH), lambda head: (0, jnp.maximum(head - heads // 2, 0))),
            *[full(out) for out in outs[2:]],
        ],
        [
            pltpu.VMEM((DH, seq), BF),
            pltpu.VMEM((DH, seq), BF),
            pltpu.VMEM((2, DH, seq), F32),
            pltpu.VMEM((seq, DH), F32),
            pltpu.VMEM((seq, DH), BF),
        ],
        grid=(heads,),
        work=10**9,
        later=later,
    )


def middle_kernel(spot, keep, arrived, out, send):
    total = keep[...] + arrived[...].astype(F32)
    out[...] = total
    send[...] = total.astype(BF)


def middle(spot, keep, arrived, later, through):
    return call(
        middle_kernel,
        "kv_middle",
        spot,
        (keep, arrived),
        [VMEM] * 2,
        [shape(keep.shape, F32), shape(keep.shape)],
        [VMEM] * 2,
        later=later,
        through=through,
    )


def final_kv_kernel(spot, keep, arrived, early, far, out):
    total = keep[...] + arrived[...].astype(F32)
    start = early.shape[1]
    deep = start + far.shape[1]
    out[:, :start] = early[...]
    out[:, start:deep] = far[...]
    out[:, deep:] = total.reshape(out.shape[1] - deep, out.shape[0]).T.astype(BF)


def final_kv(spot, keep, arrived, early, far, later):
    return call(
        final_kv_kernel,
        "kv_final",
        spot,
        (keep, arrived, early, far),
        [VMEM] * 4,
        [shape((keep.shape[2], early.shape[1] + far.shape[1] + keep.shape[0] * keep.shape[1]))],
        [VMEM],
        later=later,
    )[0]


def offsets(pieces):
    starts, at = [], 0
    for piece in pieces:
        starts.append(at)
        at += piece.shape[1]
    return starts, at


AWAYS = (4, 3, -3, 2, -2, 1, -1, 0)


def load_rows(aways, z, pieces, held, sems):
    starts, total = offsets(pieces)
    skip = total - held.shape[1]
    rows = pieces[0].shape[0] // NZ
    copies = []
    for slot, away in enumerate(aways):
        row = pl.multiple_of(lax.rem(z + away + NZ, NZ) * rows, rows)
        for index, piece in enumerate(pieces):
            copies.append(
                pltpu.make_async_copy(
                    piece.at[pl.ds(row, rows), pl.ds(skip, piece.shape[1] - skip)],
                    held.at[
                        pl.ds(slot * rows, rows), pl.ds(starts[index], piece.shape[1] - skip)
                    ],
                    sems.at[slot, index],
                )
            )
    return copies


def early_kernel(spot, weights, *rest):
    pieces, (out, packed, held, sems) = rest[:3], rest[3:]
    rows = out.shape[1]

    @pl.when(pl.program_id(0) == 0)
    def _():
        run_copies(load_rows(AWAYS, spot[Z], pieces, held, sems))
        for slot, away in enumerate(AWAYS):
            row = pl.multiple_of(lax.rem(spot[Z] + away + NZ, NZ) * rows, rows)
            packed[pl.ds(row, rows), :] = held[slot * rows : (slot + 1) * rows, :]

    total = dot(held[...], weights[:, : held.shape[1]], 1, 1)
    out[...] = total.reshape(out.shape)


def early_parts(spot, weights, pieces, later):
    seq = pieces[0].shape[0]
    width, deep = weights.shape
    _, depth = offsets(pieces)
    wide = 512
    return call(
        early_kernel,
        "early_parts",
        spot,
        (weights, *pieces),
        [pl.BlockSpec((wide, deep), lambda step: (step, 0)), *[ANY] * 3],
        [shape((NZ, seq // NZ, width), F32), shape((seq, depth))],
        [
            pl.BlockSpec((NZ, seq // NZ, wide), lambda step: (0, 0, step)),
            pl.BlockSpec((seq, depth), lambda step: (0, 0)),
        ],
        [pltpu.VMEM((seq, depth), BF), pltpu.SemaphoreType.DMA((NZ, 3))],
        grid=(width // wide,),
        work=10**9,
        later=later,
    )


def first_kernel(spot, weights, weights_kv, base, late, up, down, held, sems):
    run_copies(load_rows(AWAYS[:1], spot[Z], (late,), held, sems))
    wide = up.shape[1]
    deep = weights.shape[1]
    for index, out in enumerate((up, down)):
        part = slice(index * wide, (index + 1) * wide)
        total = dot(held[:, :deep], weights[part, :], 1, 1)
        total += dot(held[:, deep:], weights_kv[:, part], 1, 0)
        out[...] = (base[0, :, part] + total).astype(BF)


def first_parts(spot, weights, weights_kv, base, late, deep):
    _, rows, width = base.shape
    depth = deep + weights_kv.shape[0]
    last = weights.shape[1] // deep - 1
    out = pl.BlockSpec((rows, width // 2), lambda step: (0, 0))
    return call(
        first_kernel,
        "first_parts",
        spot,
        (weights, weights_kv, base, late),
        [
            pl.BlockSpec((width, deep), lambda step: (0, last)),
            pl.BlockSpec(weights_kv.shape, lambda step: (0, 0)),
            pl.BlockSpec((1, rows, width), lambda step: (0, 0, 0)),
            ANY,
        ],
        [shape((rows, width // 2))] * 2,
        [out] * 2,
        [pltpu.VMEM((rows, depth), BF), pltpu.SemaphoreType.DMA((1, 1))],
        grid=(1,),
    )


def rest_kernel(spot, weights, weights_kv, base, late, out, held, sems):
    @pl.when(pl.program_id(0) == 0)
    def _():
        run_copies(load_rows(AWAYS[1:], spot[Z], (late,), held, sems))

    deep = weights.shape[1]
    total = dot(held[:, :deep], weights[...], 1, 1) + dot(held[:, deep:], weights_kv[...], 1, 0)
    out[...] = (base[1:] + total.reshape(out.shape)).astype(BF)


def rest_parts(spot, weights, weights_kv, base, late, deep, later):
    count, rows, width = base.shape
    depth = deep + weights_kv.shape[0]
    last = weights.shape[1] // deep - 1
    wide = 512
    return call(
        rest_kernel,
        "rest_parts",
        spot,
        (weights, weights_kv, base, late),
        [
            pl.BlockSpec((wide, deep), lambda step: (step, last)),
            pl.BlockSpec((depth - deep, wide), lambda step: (0, step)),
            pl.BlockSpec((count, rows, wide), lambda step: (0, 0, step)),
            ANY,
        ],
        [shape((count - 1, rows, width))],
        [pl.BlockSpec((count - 1, rows, wide), lambda step: (0, 0, step))],
        [pltpu.VMEM(((count - 1) * rows, depth), BF), pltpu.SemaphoreType.DMA((count - 1, 1))],
        grid=(width // wide,),
        work=10**9,
        later=later,
    )[0]


def ring_kernel(kind, spot, up, down, ups, downs, *outs):
    wide = up.shape[1]
    if kind == "first":
        for arrived, part, out, start in ((up, ups, outs[0], 0), (down, downs, outs[1], wide)):
            out[...] = part[0]
            cols = slice(start, start + wide)
            out[:, cols] = (part[0, :, cols].astype(F32) + arrived[...].astype(F32)).astype(BF)
    elif kind == "next":
        for arrived, part, out in ((up, ups, outs[0]), (down, downs, outs[1])):
            out[...] = (part[0].astype(F32) + arrived[...].astype(F32)).astype(BF)
    else:
        own, send = outs
        h = spot[H]
        rows = own.shape[0]
        for out, side in ((own, h), (send, 1 - h)):
            here = pl.ds(pl.multiple_of(side * rows, rows), rows)
            total = ups[0, here, :].astype(F32) + up[here, :].astype(F32) + down[here, :].astype(F32)
            out[...] = total.astype(BF)


def ring_step(kind, spot, up, down, parts, slots, later):
    _, rows, width = parts.shape
    whole = lambda a: pl.BlockSpec(a.shape, lambda step: (0,) * len(a.shape))
    term = [pl.BlockSpec((1, rows, width), lambda step, slot=slot: (slot, 0, 0)) for slot in slots]
    out = shape((rows // 2 if kind == "last" else rows, width))
    return call(
        functools.partial(ring_kernel, kind),
        "ring_step",
        spot,
        (up, down, parts, parts),
        [whole(up), whole(down), *term],
        [out] * 2,
        [whole(out)] * 2,
        grid=(1,),
        later=later,
    )


def wgrad_kernel(spot, *rest):
    blocks, (up, down), rest = rest[: NZ - 1], rest[NZ - 1 : NZ + 1], rest[NZ + 1 :]
    pieces, (out, done, held, lefts, sems, left_sems, last_sems) = rest[:2], rest[2:]
    z = spot[Z]
    rows = blocks[0].shape[2]
    places = (0, -1, 1, -2, 2, -3, 3)

    @pl.when(pl.program_id(0) == 0)
    def _():
        def place(away):
            return pl.ds(pl.multiple_of(lax.rem(z + away + NZ, NZ) * rows, rows), rows)

        copies = [
            pltpu.make_async_copy(piece, held.at[index], sems.at[index])
            for index, piece in enumerate(pieces)
        ]
        for index, (block, away) in enumerate(zip(blocks, places)):
            copies.append(
                pltpu.make_async_copy(
                    block, lefts.at[:, :, place(away), :], left_sems.at[index]
                )
            )
        for index, last in enumerate((up, down)):
            half = NX // 2
            copies.append(
                pltpu.make_async_copy(
                    last,
                    lefts.at[pl.ds(index * half, half), :, place(NZ // 2), :],
                    last_sems.at[index],
                )
            )
        run_copies(copies)

    done[...] = jnp.zeros_like(done)
    left = lefts[pl.program_id(0)]
    left = left.reshape(left.shape[0] * left.shape[1], left.shape[2])
    right = held[...].reshape(left.shape[0], held.shape[2])
    out[0] = dot(left, right, 0, 0).astype(out.dtype)


def wgrad_parts(spot, blocks, up, down, here, there, later):
    seq, depth = here.shape
    wide = blocks[0].shape[3]
    return call(
        wgrad_kernel,
        "wgrad_parts",
        spot,
        (*blocks, up, down, here, there),
        [ANY] * (NZ + 3),
        [shape((NX, wide, depth)), shape((8, DH), F32)],
        [
            pl.BlockSpec((1, wide, depth), lambda step: (step, 0, 0)),
            pl.BlockSpec((8, DH), lambda step: (0, 0)),
        ],
        [
            pltpu.VMEM((2, seq, depth), BF),
            pltpu.VMEM((NX, 2, seq, wide), BF),
            pltpu.SemaphoreType.DMA((2,)),
            pltpu.SemaphoreType.DMA((NZ - 1,)),
            pltpu.SemaphoreType.DMA((2,)),
        ],
        grid=(NX,),
        work=10**10,
        later=later,
    )


def wgrad_sum_kernel(spot, terms, own, own_kv, send):
    total = terms[0].astype(F32)
    for index in range(1, terms.shape[0]):
        total += terms[index].astype(F32)
    q_w = own.shape[1]
    own[...] = total[:, :q_w]
    own_kv[...] = total[:, 2 * q_w :]
    send[...] = total[:, q_w:].astype(BF)


def wgrad_sum(spot, terms, q_w, later):
    _, rows, depth = terms.shape
    return call(
        wgrad_sum_kernel,
        "wgrad_sum",
        spot,
        (terms,),
        [VMEM],
        [shape((rows, q_w), F32), shape((rows, depth - 2 * q_w), F32), shape((rows, depth - q_w))],
        [VMEM] * 3,
        later=later,
    )


def final_kernel(
    spot, mine, other, own, own_kv, arrived, out_tokens, out, out_k, out_v, turned
):
    h = spot[H]
    wide = mine.shape[1]
    out_tokens[:, pl.ds(pl.multiple_of(h * wide, wide), wide)] = mine[...]
    out_tokens[:, pl.ds(pl.multiple_of((1 - h) * wide, wide), wide)] = other[...]
    rows, q_w = own.shape
    kv_w = out_k.shape[0]
    near = pl.ds(pl.multiple_of(h * rows, rows), rows)
    far = pl.ds(pl.multiple_of((1 - h) * rows, rows), rows)
    out[near, :] = own[...]
    out[far, :] = arrived[:, :q_w].astype(F32)
    for cols, value in ((near, own_kv[...]), (far, arrived[:, q_w:].astype(F32))):
        turned[...] = value.T
        for index, to in enumerate((out_k, out_v)):
            start = pl.multiple_of((2 * index + h) * kv_w, kv_w)
            to[:, cols] = turned[pl.ds(start, kv_w), :]


def final(spot, mine, other, own, own_kv, arrived, kv_w):
    n_own, wide = mine.shape
    rows, q_w = own.shape
    return call(
        final_kernel,
        "final",
        spot,
        (mine, other, own, own_kv, arrived),
        [VMEM] * 5,
        [
            shape((n_own, 2 * wide)),
            shape((2 * rows, q_w), F32),
            *[shape((kv_w, 2 * rows), F32)] * 2,
        ],
        [VMEM] * 4,
        [pltpu.VMEM((own_kv.shape[1], rows), F32)],
    )


def body(
    tokens,
    queries,
    saved_keys,
    saved_values,
    outputs,
    out_grads,
    log_norms,
    w_query,
    w_key,
    w_value,
):
    t = lax.axis_index("tensor")
    d = lax.axis_index("dp")
    h = t % 2
    spot = jnp.stack([t // 2, h, d % 2, d // 4, t // 2 % 2]).astype(jnp.int32)
    kv_w = saved_keys.shape[1]
    q_w = queries.shape[1]
    n_own = tokens.shape[0]
    heads4 = [[4 * k + j for j in range(4)] for k in range(4)]
    ring_x = [[r + 4 * k for k in range(NX)] for r in range(4)]
    plane = [[r + 2 * k for k in range(8)] for r in range(2)]

    w_key, w_value = w_key.T, w_value.T
    own, side, core, both, kv = pack(spot, tokens, saved_keys.T, saved_values.T)
    side = swap_quad(side, 0, 1)
    core = swap_quad(core, 1, 0)
    both = swap_quad(both, 1, 1)
    kv = lax.all_to_all(kv, "tensor", 0, 0, axis_index_groups=heads4, tiled=True)
    block, w_send, formed = token_block(
        spot, (own, side, core, both), w_query, w_key, w_value
    )
    w_side = swap(w_send, "tensor", 1)
    up1, down1 = shift(block, "tensor", 2), shift(block, "tensor", -2)
    own_a, own_b, kv_send, kv_keep = attend(
        spot, kv, queries, out_grads, outputs, log_norms, [formed]
    )
    w_side = again(spot, w_side, [up1, down1, own_a])
    far_a = swap(own_a, "tensor", 1)
    kv_z = swap(kv_send, "tensor", 2)
    up2, down2 = shift(up1, "tensor", 2), shift(down1, "tensor", -2)
    w_x = swap(w_side, "dp", 4)
    kv_keep, kv_send = middle(spot, kv_keep, kv_z, [up2, down2, far_a, w_x], [])
    kv_y = swap(kv_send, "tensor", 1)
    far_b = swap(own_b, "tensor", 1)
    up3, down3 = shift(up2, "tensor", 2), shift(down2, "tensor", -2)
    w_parts = [w_side, w_x] + [swap(value, "dp", 1) for value in (w_side, w_x)]
    weights, weights_kv = gather_weights(spot, w_query, w_key, w_value, w_parts, [kv_send])
    base, early = early_parts(spot, weights, [own_a, own_b, far_a], [])
    up4, down4 = halves(spot, up3, down3, [base])
    up4, down4 = shift(up4, "tensor", 2), shift(down4, "tensor", -2)
    here = final_kv(spot, kv_keep, kv_y, early, far_b, [base, up3, down3])
    there = swap(here, "dp", 1)

    up, down = first_parts(spot, weights, weights_kv, base, here, 2 * DH)
    up_next, down_next = shift(up, "tensor", 2), shift(down, "tensor", -2)
    parts = rest_parts(spot, weights, weights_kv, base, here, 2 * DH, [up])
    blocks = [block, up1, down1, up2, down2, up3, down3]
    terms, done = wgrad_parts(
        spot, blocks, up4, down4, here, there, [parts, up_next, down_next]
    )
    for kind, slots in (("first", (0, 1)), ("next", (2, 3)), ("next", (4, 5))):
        up, down = ring_step(kind, spot, up_next, down_next, parts, slots, [done])
        up_next, down_next = shift(up, "tensor", 2), shift(down, "tensor", -2)

    terms = terms.reshape(8, DH, terms.shape[2])
    terms = lax.all_to_all(terms, "dp", 0, 0, axis_index_groups=plane, tiled=True)
    w_own, w_own_kv, w_send = wgrad_sum(spot, terms, q_w, [up])
    w_other = swap(w_send, "tensor", 1)

    mine, other = ring_step("last", spot, up_next, down_next, parts, (6, 6), [w_send])
    other = swap(other, "tensor", 1)
    token_grads, query_wgrad, key_wgrad, value_wgrad = final(
        spot, mine, other, w_own, w_own_kv, w_other, kv_w
    )
    return token_grads, query_wgrad, key_wgrad.T, value_wgrad.T


def solution(mesh):
    in_specs = (
        P(("dp", "tensor"), None),
        P("dp", "tensor"),
        P("dp", "tensor"),
        P("dp", "tensor"),
        P("dp", "tensor"),
        P("dp", "tensor"),
        P("tensor", "dp"),
        P(None, "tensor"),
        P(None, "tensor"),
        P(None, "tensor"),
    )
    out_specs = (P(("dp", "tensor"), None), P("dp", "tensor"), P("dp", "tensor"), P("dp", "tensor"))
    return jax.shard_map(body, mesh=mesh, in_specs=in_specs, out_specs=out_specs, check_vma=False)
```
